32 devices in a mesh: seq: 8 (over z, y), ch: 4 (over x, core).
Axes of the slice: x: 2, y: 2, z: 4, core: 2. Of those that a mesh axis runs over, the one named last changes fastest.
Arguments:
- tokens: int32 [4096], P('seq'), may hold values from 0 to 3
- hidden: bfloat16 [4096, 1024], P('seq', 'ch'), may hold values from -6 to 6
- embedding: bfloat16 [4, 1024], P(None, 'ch'), may hold values from -6 to 6
- w_in: bfloat16 [1024, 1024], P(None, 'ch'), may hold values from -0.1875 to 0.1875
- w_gate: bfloat16 [1024, 1024], P(None, 'ch'), may hold values from -0.1875 to 0.1875
- conv_w: float32 [3, 4, 1024], P(None, None, 'ch'), may hold values from -3 to 3
- channel_order: int32 [1024], replicated, may hold values from 0 to 1023, each once
- gain: float32 [1024], replicated, may hold values from 0.5 to 1.5
- w_out: bfloat16 [1024, 1024], P(None, 'ch'), may hold values from -0.1875 to 0.1875
- cotangent: bfloat16 [4096, 1024], P('seq', 'ch'), may hold values from -6 to 6
Outputs:
- output: bfloat16 [4096, 1024], P('seq', 'ch')
- grad_in: bfloat16 [1024, 1024], P(None, 'ch')
- grad_gate: bfloat16 [1024, 1024], P(None, 'ch')
- grad_out: bfloat16 [1024, 1024], P(None, 'ch')
- grad_conv: float32 [3, 4, 1024], P(None, None, 'ch')
The draws below stay inside these ranges and needn't reach their ends.
Inputs may be any that keep to these rules, and one draw needn't show every extreme that they name: `channel_order`: each channel index once.
All inputs are finite; a program needn't handle non-finite values.
Results may differ from the reference program's by a relative error of at most 0.025.
Values may be sent and summed in bfloat16 or wider, within the bound.
No kernel may reach another device: no remote copies, remote signals or barrier semaphores. Data moves between devices by JAX's collectives and lax.ppermute only.
A program may use at most 64 MiB of HBM per device.

```python
import jax
import jax.numpy as jnp
from jax import lax

D = 1024
LENGTH = 4096
N_CH = 4


def place_ends(result, key, smallest, largest):
    place = [jax.random.randint(jax.random.fold_in(key, axis), (), 0, length) for axis, length in enumerate(result.shape)]
    widest = result.shape.index(max(result.shape))
    neighbour = place[:widest] + [(place[widest] + 1) % result.shape[widest]] + place[widest + 1:]
    return result.at[tuple(place)].set(smallest).at[tuple(neighbour)].set(largest)


def shard_levels(own_key, extent, split, smallest, top_value):
    level, own = 1.0, jax.random.fold_in(own_key, 6)
    for dim, blocks in split:
        draws = jnp.exp(jax.random.uniform(jax.random.fold_in(own, dim), (blocks,), jnp.float32, smallest / len(split), top_value / len(split)))
        level = level * jnp.repeat(draws, extent[dim] // blocks).reshape([-1 if axis == dim else 1 for axis in range(len(extent))])
    return level


def centred(stream_key, dims, deviation, limit, shards=(), held_as=jnp.bfloat16):
    entries = deviation * jax.random.normal(stream_key, dims, jnp.float32)
    if shards:
        entries = entries * shard_levels(stream_key, dims, shards, -0.22, 0.18)
    return jnp.clip(entries, -limit, limit).astype(held_as)


def setup_inputs(seed: int = 0) -> dict:
    arg_keys = jax.random.split(jax.random.key(seed), 11)
    tokens = place_ends(jax.random.randint(arg_keys[0], (LENGTH,), 0, 4), jax.random.fold_in(arg_keys[0], 1), 0, 3).astype(jnp.int32)
    hidden = centred(arg_keys[1], (LENGTH, D), 1.0, 6.0, ((0, 8), (1, 4)))
    embedding = centred(arg_keys[2], (4, D), 1.0, 6.0, ((1, 4),))
    w_in = centred(arg_keys[3], (D, D), D ** -0.5, 0.1875, ((1, 4),))
    w_gate = centred(arg_keys[4], (D, D), D ** -0.5, 0.1875, ((1, 4),))
    conv_w = centred(arg_keys[5], (3, 4, D), 0.5, 3.0, ((2, 4),), jnp.float32)
    channel_order = jax.random.permutation(arg_keys[6], D).astype(jnp.int32)
    gain = jnp.clip(1.0 + 0.1 * jax.random.normal(arg_keys[7], (D,), jnp.float32), 0.5, 1.5)
    w_out = centred(arg_keys[8], (D, D), D ** -0.5, 0.1875, ((1, 4),))
    cotangent = centred(arg_keys[9], (LENGTH, D), 1.0, 6.0, ((0, 8), (1, 4)))
    return {"tokens": tokens, "hidden": hidden, "embedding": embedding, "w_in": w_in, "w_gate": w_gate, "conv_w": conv_w, "channel_order": channel_order, "gain": gain, "w_out": w_out, "cotangent": cotangent}


DILATIONS = (1, 8, 64)
EPSILON = 1e-06

def conv_forward(source, weights, dilation):
    length = source.shape[0]
    padded = jnp.pad(source, ((2 * dilation, 2 * dilation), (0, 0)))
    total = jnp.zeros(source.shape, jnp.float32)
    for position in range(4):
        begin = 2 * dilation + (position - 2) * dilation
        total = total + weights[position][None, :] * padded[begin:begin + length].astype(jnp.float32)
    return (total, padded)

def conv_backward(upstream, weights, padded_source, dilation):
    length = upstream.shape[0]
    padded_grad = jnp.pad(upstream, ((2 * dilation, 2 * dilation), (0, 0)))
    upstream_wide = upstream.astype(jnp.float32)
    total = jnp.zeros(upstream.shape, jnp.float32)
    weight_rows = []
    for position in range(4):
        begin = 2 * dilation - (position - 2) * dilation
        total = total + weights[position][None, :] * padded_grad[begin:begin + length].astype(jnp.float32)
        start = 2 * dilation + (position - 2) * dilation
        weight_rows.append(lax.optimization_barrier(jnp.sum(upstream_wide * padded_source[start:start + length].astype(jnp.float32), axis=0)))
    return (total, jnp.stack(weight_rows))

def reference(tokens, hidden, embedding, w_in, w_gate, conv_w, channel_order, gain, w_out, cotangent):
    width_full = hidden.shape[1]
    width_group = width_full // N_CH
    block_in = (hidden.astype(jnp.float32) + embedding[tokens].astype(jnp.float32)).astype(jnp.bfloat16)
    projected = jnp.dot(block_in, w_in, preferred_element_type=jnp.float32).astype(jnp.bfloat16)
    gate_pre = jnp.dot(block_in, w_gate, preferred_element_type=jnp.float32)
    saved = []
    current = projected
    for level in range(3):
        total, padded = conv_forward(current, conv_w[level], DILATIONS[level])
        saved.append(padded)
        current = total.astype(jnp.bfloat16)
    gate_act = jax.nn.silu(gate_pre)
    gated = (current.astype(jnp.float32) * gate_act).astype(jnp.bfloat16)
    combined = gated.astype(jnp.float32) + gated[::-1][:, channel_order].astype(jnp.float32)
    inv_scale = lax.rsqrt(lax.optimization_barrier(jnp.mean(combined * combined, axis=1, keepdims=True)) + EPSILON)
    normalized = (combined * inv_scale * gain[None, :]).astype(jnp.bfloat16)
    output = (block_in.astype(jnp.float32) + jnp.dot(normalized, w_out, preferred_element_type=jnp.float32)).astype(jnp.bfloat16)
    grad_norm = jnp.zeros(combined.shape, jnp.float32)
    for group in range(N_CH):
        low = group * width_group
        part = jnp.dot(cotangent[:, low:low + width_group], w_out[:, low:low + width_group].T, preferred_element_type=jnp.float32)
        grad_norm = grad_norm + part.astype(jnp.bfloat16).astype(jnp.float32)
    hat = combined * inv_scale
    scaled = grad_norm * gain[None, :]
    row_total = lax.optimization_barrier(jnp.sum(scaled * hat, axis=1, keepdims=True))
    grad_comb = (inv_scale * (scaled - hat * row_total / width_full)).astype(jnp.bfloat16)
    inverse = jnp.zeros_like(channel_order).at[channel_order].set(jnp.arange(width_full, dtype=jnp.int32))
    grad_gated = grad_comb.astype(jnp.float32) + grad_comb[:, inverse][::-1].astype(jnp.float32)
    grad_level = (grad_gated * gate_act).astype(jnp.bfloat16)
    sigmoid_gate = jax.nn.sigmoid(gate_pre)
    grad_gate_pre = (grad_gated * current.astype(jnp.float32) * sigmoid_gate * (1.0 + gate_pre * (1.0 - sigmoid_gate))).astype(jnp.bfloat16)
    tap_grads = [None, None, None]
    for level in (2, 1, 0):
        total, tap_grads[level] = conv_backward(grad_level, conv_w[level], saved[level], DILATIONS[level])
        grad_level = total.astype(jnp.bfloat16)
    contract_rows = (((0,), (0,)), ((), ()))
    grad_in = lax.dot_general(block_in, grad_level, contract_rows, preferred_element_type=jnp.float32)
    grad_gate = lax.dot_general(block_in, grad_gate_pre, contract_rows, preferred_element_type=jnp.float32)
    grad_out = lax.dot_general(normalized, cotangent, contract_rows, preferred_element_type=jnp.float32)
    return (output, grad_in.astype(jnp.bfloat16), grad_gate.astype(jnp.bfloat16), grad_out.astype(jnp.bfloat16), jnp.stack(tap_grads))
```

```python
import jax
import jax.numpy as jnp
from jax import lax
from jax.sharding import PartitionSpec as P

DILATIONS = (1, 8, 64)
EPSILON = 1e-06
REACH_BACK = 2 * sum(DILATIONS)
REACH_AHEAD = sum(DILATIONS)
BACK = -(-REACH_BACK // 16) * 16
AHEAD = -(-REACH_AHEAD // 16) * 16


def swap(block, distance):
    count = lax.axis_size("ch")
    return lax.ppermute(block, "ch", [(i, i ^ distance) for i in range(count)])


def gather_relative(block):
    blocks = {0: block}
    distance = lax.axis_size("ch") // 2
    while distance:
        for j in list(blocks):
            blocks[j ^ distance] = swap(blocks[j], distance)
        distance //= 2
    return [blocks[j] for j in range(len(blocks))]


def reorder(array, width, axis=0):
    me = lax.axis_index("ch")
    count = lax.axis_size("ch")
    return jnp.concatenate(
        [lax.dynamic_slice_in_dim(array, (me ^ j) * width, width, axis) for j in range(count)], axis=axis
    )


def mirror(block):
    count = lax.axis_size("seq")
    return lax.ppermute(block, "seq", [(i, count - 1 - i) for i in range(count)])


def with_halo(block, before, after):
    count = lax.axis_size("seq")
    left = lax.ppermute(block[block.shape[0] - before :], "seq", [(i, i + 1) for i in range(count - 1)])
    right = lax.ppermute(block[:after], "seq", [(i + 1, i) for i in range(count - 1)])
    return jnp.concatenate([left, block, right], axis=0)


def flip(block):
    rows = block.shape[0]
    index = jnp.arange(rows, dtype=jnp.int32)
    anti = (index[:, None] + index[None, :] == rows - 1).astype(block.dtype)
    return jnp.dot(anti, block, preferred_element_type=jnp.float32).astype(block.dtype)


def inside(before, rows, after):
    place = lax.axis_index("seq") * rows + jnp.arange(-before, rows + after, dtype=jnp.int32)
    return ((place >= 0) & (place < lax.axis_size("seq") * rows))[:, None]


def local(tokens, hidden, embedding, w_in, w_gate, conv_w, channel_order, gain, w_out, cotangent):
    rows, width = hidden.shape
    full = gain.shape[0]
    bf16, f32 = jnp.bfloat16, jnp.float32
    shift = jnp.zeros((rows, width), f32)
    for base in range(embedding.shape[0]):
        shift = jnp.where((tokens == base)[:, None], embedding[base].astype(f32)[None, :], shift)
    local_input = (hidden.astype(f32) + shift).astype(bf16)
    full_input = jnp.concatenate(gather_relative(local_input), axis=1)

    w_in_r = reorder(w_in, width)
    w_gate_r = reorder(w_gate, width)
    w_out_r = reorder(w_out, width)
    gain_r = reorder(gain, width)
    order_r = reorder(channel_order, width)
    index_r = reorder(jnp.arange(full, dtype=jnp.int32), width)
    choose = (index_r[:, None] == order_r[None, :]).astype(bf16)
    choose_inverse = (order_r[:, None] == index_r[None, :width]).astype(bf16)

    grad_terms = lax.dot_general(cotangent, w_out, (((1,), (1,)), ((), ())), preferred_element_type=f32)
    grad_own = lax.psum_scatter(grad_terms.astype(bf16), "ch", scatter_dimension=1, tiled=True)
    grad_norm = reorder(lax.all_gather(grad_own, "ch", axis=1, tiled=True), width, 1).astype(f32)

    projected = jnp.dot(full_input, w_in_r, preferred_element_type=f32).astype(bf16)
    level = with_halo(projected, BACK, AHEAD)
    gate_pre = jnp.dot(full_input, w_gate_r, preferred_element_type=f32)
    before, after = BACK, AHEAD
    saved = []
    for number, dilation in enumerate(DILATIONS):
        saved.append((level, before))
        last = number == len(DILATIONS) - 1
        next_before = 0 if last else before - 2 * dilation
        next_after = 0 if last else after - dilation
        total = 0.0
        for tap in range(4):
            begin = before - next_before + (tap - 2) * dilation
            total = total + conv_w[number, tap][None, :] * level[
                begin : begin + next_before + rows + next_after
            ].astype(f32)
        if not last:
            total = jnp.where(inside(next_before, rows, next_after), total, 0.0)
        level = total.astype(bf16)
        before, after = next_before, next_after
    level_3 = level
    sigmoid = jax.nn.sigmoid(gate_pre)
    gate_act = gate_pre * sigmoid
    gated = (level_3.astype(f32) * gate_act).astype(bf16)
    mirrored = mirror(flip(gated))
    gated_full = jnp.concatenate(gather_relative(gated), axis=1)
    mirrored_full = jnp.concatenate(gather_relative(mirrored), axis=1)
    combined = gated_full.astype(f32) + jnp.dot(mirrored_full, choose, preferred_element_type=f32)
    inv_scale = lax.rsqrt(jnp.mean(combined * combined, axis=1, keepdims=True) + EPSILON)
    hat = combined * inv_scale
    scaled = grad_norm * gain_r[None, :]
    row_total = jnp.sum(scaled * hat, axis=1, keepdims=True)
    grad_comb = (inv_scale * (scaled - hat * row_total / full)).astype(bf16)
    chosen = jnp.dot(grad_comb, choose_inverse, preferred_element_type=f32).astype(bf16)
    grad_mirror = mirror(flip(chosen))

    normalized = (hat * gain_r[None, :]).astype(bf16)
    output = (
        local_input.astype(f32) + jnp.dot(normalized, w_out_r, preferred_element_type=f32)
    ).astype(bf16)

    contract_rows = (((0,), (0,)), ((), ()))

    def weight_grad(left, right):
        product = lax.dot_general(left, right, contract_rows, preferred_element_type=f32)
        return reorder(product.astype(bf16), width)

    def sum_early(part):
        own = lax.psum_scatter(part, "seq", scatter_dimension=0, tiled=True)
        return lax.all_gather(own, "seq", axis=0, tiled=True)

    grad_out = sum_early(weight_grad(normalized, cotangent))

    grad_gated = grad_comb[:, :width].astype(f32) + grad_mirror.astype(f32)
    upstream = (grad_gated * gate_act).astype(bf16)
    grad_gate_pre = (
        grad_gated * level_3.astype(f32) * sigmoid * (1.0 + gate_pre * (1.0 - sigmoid))
    ).astype(bf16)
    before, after = AHEAD, BACK
    extended = with_halo(upstream, before, after)
    grad_gate = sum_early(weight_grad(full_input, grad_gate_pre))
    tap_grads = []
    for number in reversed(range(len(DILATIONS))):
        dilation = DILATIONS[number]
        source, source_before = saved[number]
        own = extended[before : before + rows].astype(f32)
        for tap in range(4):
            begin = source_before + (tap - 2) * dilation
            tap_grads.append(jnp.sum(own * source[begin : begin + rows].astype(f32), axis=0))
        last = number == 0
        next_before = 0 if last else before - dilation
        next_after = 0 if last else after - 2 * dilation
        total = 0.0
        for tap in range(4):
            begin = before - next_before - (tap - 2) * dilation
            total = total + conv_w[number, tap][None, :] * extended[
                begin : begin + next_before + rows + next_after
            ].astype(f32)
        if not last:
            total = jnp.where(inside(next_before, rows, next_after), total, 0.0)
        extended = total.astype(bf16)
        before, after = next_before, next_after
    taps = jnp.stack([jnp.stack(tap_grads[4 * (2 - number) : 4 * (3 - number)]) for number in range(3)])
    grad_conv = lax.psum(taps, "seq")
    grad_in = lax.psum(weight_grad(full_input, extended), "seq")
    return output, grad_in, grad_gate, grad_out, grad_conv


def solution(mesh):
    placed = (
        P("seq"),
        P("seq", "ch"),
        P(None, "ch"),
        P(None, "ch"),
        P(None, "ch"),
        P(None, None, "ch"),
        P(),
        P(),
        P(None, "ch"),
        P("seq", "ch"),
    )
    return jax.shard_map(
        local,
        mesh=mesh,
        in_specs=placed,
        out_specs=(
            P("seq", "ch"),
            P(None, "ch"),
            P(None, "ch"),
            P(None, "ch"),
            P(None, None, "ch"),
        ),
        check_vma=False,
    )
```

```python
import jax
import jax.numpy as jnp
from jax import lax
from jax.sharding import PartitionSpec as P

DILATIONS = (1, 8, 64)
EPSILON = 1e-06
REACH_BACK = 2 * sum(DILATIONS)
REACH_AHEAD = sum(DILATIONS)
BACK = -(-REACH_BACK // 16) * 16
AHEAD = -(-REACH_AHEAD // 16) * 16
CHUNKS = 2


def exchange(block, axis, distance):
    count = lax.axis_size(axis)
    return lax.ppermute(block, axis, [(i, i ^ distance) for i in range(count)])


def distances(axis):
    return [1 << bit for bit in range(lax.axis_size(axis).bit_length() - 1)]


def gather_relative(block):
    blocks = {0: block}
    for distance in reversed(distances("ch")):
        for j in list(blocks):
            blocks[j ^ distance] = exchange(blocks[j], "ch", distance)
    return [blocks[j] for j in range(len(blocks))]


def sum_relative(blocks):
    blocks = dict(enumerate(blocks))
    width = blocks[0].shape[1]
    for distance in distances("ch"):
        sent = [j for j in blocks if j & distance]
        other = exchange(
            jnp.concatenate([blocks[j].astype(jnp.bfloat16) for j in sent], axis=1), "ch", distance
        )
        for place, j in enumerate(sent):
            part = other[:, place * width : (place + 1) * width]
            blocks[j ^ distance] = blocks[j ^ distance] + part.astype(jnp.float32)
            del blocks[j]
    return blocks[0].astype(jnp.bfloat16)


def sum_over_seq(part, order):
    me = lax.axis_index("seq")
    for distance in order:
        half = part.shape[0] // 2
        bit = (me & distance) // distance
        sent = lax.dynamic_slice_in_dim(part, (1 - bit) * half, half, 0).astype(jnp.bfloat16)
        kept = lax.dynamic_slice_in_dim(part, bit * half, half, 0)
        part = kept.astype(jnp.float32) + exchange(sent, "seq", distance).astype(jnp.float32)
    part = part.astype(jnp.bfloat16)
    for distance in reversed(order):
        bit = (me & distance) // distance
        other = exchange(part, "seq", distance)
        part = jnp.where(
            bit == 0, jnp.concatenate([part, other], axis=0), jnp.concatenate([other, part], axis=0)
        )
    return part


def sum_gradient(part):
    order = distances("seq")
    half = part.shape[0] // 2
    return jnp.concatenate(
        [sum_over_seq(part[:half], order), sum_over_seq(part[half:], order[1:] + order[:1])], axis=0
    )


def sum_small(part):
    for distance in distances("seq"):
        part = part + exchange(part, "seq", distance)
    return part


def reorder(array, width, axis=0):
    me = lax.axis_index("ch")
    count = lax.axis_size("ch")
    return jnp.concatenate(
        [lax.dynamic_slice_in_dim(array, (me ^ j) * width, width, axis) for j in range(count)], axis=axis
    )


def mirror(block):
    count = lax.axis_size("seq")
    return lax.ppermute(block, "seq", [(i, count - 1 - i) for i in range(count)])


def pair_routes(turn):
    count = lax.axis_size("seq")
    return [(low, low + 1) for low in range(turn, count - 1, 2)]


def halo(block, before, after, far=0):
    reach = max(before, after)
    odd = lax.axis_index("seq") % 2 == 1
    head, tail = block[:reach], block[block.shape[0] - reach :]
    received = []
    for turn in range(2):
        channels = lax.axis_size("ch")
        route = []
        for low, high in pair_routes(turn):
            for c in range(channels):
                route.append((low * channels + c, high * channels + (c ^ far)))
                route.append((high * channels + c, low * channels + (c ^ far)))
        sent = jnp.where(odd, head, tail) if turn == 0 else jnp.where(odd, tail, head)
        received.append(lax.ppermute(sent, ("seq", "ch"), route))
    left = jnp.where(odd, received[0], received[1])
    right = jnp.where(odd, received[1], received[0])
    return left[reach - before :], right[:after]


def flip(block):
    rows = block.shape[0]
    index = jnp.arange(rows, dtype=jnp.int32)
    anti = (index[:, None] + index[None, :] == rows - 1).astype(block.dtype)
    return jnp.dot(anti, block, preferred_element_type=jnp.float32).astype(block.dtype)


def inside(before, rows, after):
    place = lax.axis_index("seq") * rows + jnp.arange(-before, rows + after, dtype=jnp.int32)
    return ((place >= 0) & (place < lax.axis_size("seq") * rows))[:, None]


def local(tokens, hidden, embedding, w_in, w_gate, conv_w, channel_order, gain, w_out, cotangent):
    rows, width = hidden.shape
    full = gain.shape[0]
    channels = full // width
    bf16, f32 = jnp.bfloat16, jnp.float32
    bases = jnp.arange(embedding.shape[0], dtype=jnp.int32)
    one_hot = (bases[:, None] == tokens[None, :]).astype(bf16)
    shift = lax.dot_general(one_hot, embedding, (((0,), (0,)), ((), ())), preferred_element_type=f32)
    local_input = (hidden.astype(f32) + shift).astype(bf16)

    edges = [jnp.concatenate(halo(local_input, BACK, AHEAD, far), axis=0) for far in range(0, channels, 2)]
    mains = gather_relative(local_input)
    edge_blocks = {}
    packed = exchange(jnp.concatenate(edges, axis=0), "ch", 1)
    for place, far in enumerate(range(0, channels, 2)):
        edge_blocks[far] = edges[place]
        edge_blocks[far ^ 1] = packed[place * (BACK + AHEAD) : (place + 1) * (BACK + AHEAD)]
    full_input = jnp.concatenate(mains, axis=1)
    edge_input = jnp.concatenate([edge_blocks[j] for j in range(channels)], axis=1)

    w_in_r = reorder(w_in, width)
    w_gate_r = reorder(w_gate, width)
    w_out_r = reorder(w_out, width)
    gain_r = reorder(gain, width)
    order_r = reorder(channel_order, width)
    index_r = reorder(jnp.arange(full, dtype=jnp.int32), width)
    choose = (index_r[:, None] == order_r[None, :]).astype(bf16)
    choose_inverse = (order_r[:, None] == index_r[None, :width]).astype(bf16)

    grad_terms = lax.dot_general(
        cotangent, w_out_r, (((1,), (1,)), ((), ())), preferred_element_type=f32
    ).astype(bf16)
    grad_own = sum_relative(
        [grad_terms[:, j * width : (j + 1) * width].astype(f32) for j in range(channels)]
    )
    grad_norm = jnp.concatenate(gather_relative(grad_own), axis=1)

    projected = jnp.dot(full_input, w_in_r, preferred_element_type=f32).astype(bf16)
    projected_edge = jnp.dot(edge_input, w_in_r, preferred_element_type=f32).astype(bf16)
    level = jnp.concatenate([projected_edge[:BACK], projected, projected_edge[BACK:]], axis=0)
    gate_pre = jnp.dot(full_input, w_gate_r, preferred_element_type=f32)
    before, after = BACK, AHEAD
    saved = []
    for number, dilation in enumerate(DILATIONS):
        saved.append((level, before))
        last = number == len(DILATIONS) - 1
        next_before = 0 if last else before - 2 * dilation
        next_after = 0 if last else after - dilation
        total = 0.0
        for tap in range(4):
            begin = before - next_before + (tap - 2) * dilation
            total = total + conv_w[number, tap][None, :] * level[
                begin : begin + next_before + rows + next_after
            ].astype(f32)
        if not last:
            total = jnp.where(inside(next_before, rows, next_after), total, 0.0)
        level = total.astype(bf16)
        before, after = next_before, next_after
    level_3 = level
    sigmoid = jax.nn.sigmoid(gate_pre)
    gate_act = gate_pre * sigmoid
    gated = (level_3.astype(f32) * gate_act).astype(bf16)

    flipped = flip(gated)
    size = rows // CHUNKS
    chunks = [slice(k * size, (k + 1) * size) for k in range(CHUNKS)]
    mirrored = [mirror(flipped[chunk]) for chunk in chunks]
    gated_full = jnp.concatenate(gather_relative(gated), axis=1)
    grad_comb, grad_mirror, normalized = [], [], []
    for chunk, part in zip(chunks, mirrored):
        mirrored_full = jnp.concatenate(gather_relative(part), axis=1)
        combined = gated_full[chunk].astype(f32) + jnp.dot(
            mirrored_full, choose, preferred_element_type=f32
        )
        inv_scale = lax.rsqrt(jnp.mean(combined * combined, axis=1, keepdims=True) + EPSILON)
        hat = combined * inv_scale
        scaled = grad_norm[chunk].astype(f32) * gain_r[None, :]
        row_total = jnp.sum(scaled * hat, axis=1, keepdims=True)
        grad_here = (inv_scale * (scaled - hat * row_total / full)).astype(bf16)
        chosen = jnp.dot(grad_here, choose_inverse, preferred_element_type=f32).astype(bf16)
        grad_mirror.append(mirror(flip(chosen)))
        grad_comb.append(grad_here[:, :width])
        normalized.append((hat * gain_r[None, :]).astype(bf16))
    normalized = jnp.concatenate(normalized, axis=0)
    grad_comb = jnp.concatenate(grad_comb, axis=0)
    grad_mirror = jnp.concatenate(grad_mirror[::-1], axis=0)

    output = (
        local_input.astype(f32) + jnp.dot(normalized, w_out_r, preferred_element_type=f32)
    ).astype(bf16)

    contract_rows = (((0,), (0,)), ((), ()))

    def weight_grad(left, right):
        product = lax.dot_general(left, right, contract_rows, preferred_element_type=f32)
        return reorder(product.astype(bf16), width)

    grad_out = sum_gradient(weight_grad(normalized, cotangent))

    grad_gated = grad_comb.astype(f32) + grad_mirror.astype(f32)
    upstream = (grad_gated * gate_act).astype(bf16)
    grad_gate_pre = (
        grad_gated * level_3.astype(f32) * sigmoid * (1.0 + gate_pre * (1.0 - sigmoid))
    ).astype(bf16)
    before, after = AHEAD, BACK
    left, right = halo(upstream, before, after)
    extended = jnp.concatenate([left, upstream, right], axis=0)
    grad_gate = sum_gradient(weight_grad(full_input, grad_gate_pre))
    tap_grads = []
    for number in reversed(range(len(DILATIONS))):
        dilation = DILATIONS[number]
        source, source_before = saved[number]
        own = extended[before : before + rows].astype(f32)
        for tap in range(4):
            begin = source_before + (tap - 2) * dilation
            tap_grads.append(jnp.sum(own * source[begin : begin + rows].astype(f32), axis=0))
        last = number == 0
        next_before = 0 if last else before - dilation
        next_after = 0 if last else after - 2 * dilation
        total = 0.0
        for tap in range(4):
            begin = before - next_before - (tap - 2) * dilation
            total = total + conv_w[number, tap][None, :] * extended[
                begin : begin + next_before + rows + next_after
            ].astype(f32)
        if not last:
            total = jnp.where(inside(next_before, rows, next_after), total, 0.0)
        extended = total.astype(bf16)
        before, after = next_before, next_after
    taps = jnp.stack([jnp.stack(tap_grads[4 * (2 - number) : 4 * (3 - number)]) for number in range(3)])
    grad_conv = sum_small(taps)
    grad_in = sum_gradient(weight_grad(full_input, extended))
    return output, grad_in, grad_gate, grad_out, grad_conv


def solution(mesh):
    placed = (
        P("seq"),
        P("seq", "ch"),
        P(None, "ch"),
        P(None, "ch"),
        P(None, "ch"),
        P(None, None, "ch"),
        P(),
        P(),
        P(None, "ch"),
        P("seq", "ch"),
    )
    return jax.shard_map(
        local,
        mesh=mesh,
        in_specs=placed,
        out_specs=(
            P("seq", "ch"),
            P(None, "ch"),
            P(None, "ch"),
            P(None, "ch"),
            P(None, None, "ch"),
        ),
        check_vma=False,
    )
```

```python
import jax
import jax.numpy as jnp
from jax import lax
from jax.sharding import PartitionSpec as P

DILATIONS = (1, 8, 64)
EPSILON = 1e-06
REACH_BACK = 2 * sum(DILATIONS)
REACH_AHEAD = sum(DILATIONS)
BACK = -(-REACH_BACK // 16) * 16
AHEAD = -(-REACH_AHEAD // 16) * 16
def exchange(block, axis, distance):
    count = lax.axis_size(axis)
    return lax.ppermute(block, axis, [(i, i ^ distance) for i in range(count)])


def distances(axis):
    return [1 << bit for bit in range(lax.axis_size(axis).bit_length() - 1)]


def gather_relative(block):
    blocks = {0: block}
    for distance in reversed(distances("ch")):
        for j in list(blocks):
            blocks[j ^ distance] = exchange(blocks[j], "ch", distance)
    return [blocks[j] for j in range(len(blocks))]


def sum_relative(blocks):
    blocks = dict(enumerate(blocks))
    width = blocks[0].shape[1]
    for distance in distances("ch"):
        sent = [j for j in blocks if j & distance]
        packed = jnp.concatenate([blocks[j].astype(jnp.bfloat16) for j in sent], axis=1)
        other = exchange(packed, "ch", distance)
        for place, j in enumerate(sent):
            part = other[:, place * width : (place + 1) * width]
            blocks[j ^ distance] = blocks[j ^ distance] + part.astype(jnp.float32)
            del blocks[j]
    return blocks[0].astype(jnp.bfloat16)


def halve(part, distance):
    half = part.shape[0] // 2
    bit = (lax.axis_index("seq") & distance) // distance
    sent = lax.dynamic_slice_in_dim(part, (1 - bit) * half, half, 0).astype(jnp.bfloat16)
    kept = lax.dynamic_slice_in_dim(part, bit * half, half, 0)
    return kept.astype(jnp.float32) + exchange(sent, "seq", distance).astype(jnp.float32)


def double(part, distance):
    part = part.astype(jnp.bfloat16)
    bit = (lax.axis_index("seq") & distance) // distance
    other = exchange(part, "seq", distance)
    return jnp.where(
        bit == 0, jnp.concatenate([part, other], axis=0), jnp.concatenate([other, part], axis=0)
    )


def reorder(array, width, axis=0):
    me = lax.axis_index("ch")
    count = lax.axis_size("ch")
    return jnp.concatenate(
        [lax.dynamic_slice_in_dim(array, (me ^ j) * width, width, axis) for j in range(count)], axis=axis
    )


def mirror(block):
    count = lax.axis_size("seq")
    return lax.ppermute(block, "seq", [(i, count - 1 - i) for i in range(count)])


def pair_routes(turn):
    count = lax.axis_size("seq")
    return [(low, low + 1) for low in range(turn, count - 1, 2)]


def halo(block, before, after, far=0):
    reach = max(before, after)
    odd = lax.axis_index("seq") % 2 == 1
    head, tail = block[:reach], block[block.shape[0] - reach :]
    received = []
    for turn in range(2):
        channels = lax.axis_size("ch")
        route = []
        for low, high in pair_routes(turn):
            for c in range(channels):
                route.append((low * channels + c, high * channels + (c ^ far)))
                route.append((high * channels + c, low * channels + (c ^ far)))
        sent = jnp.where(odd, head, tail) if turn == 0 else jnp.where(odd, tail, head)
        received.append(lax.ppermute(sent, ("seq", "ch"), route))
    left = jnp.where(odd, received[0], received[1])
    right = jnp.where(odd, received[1], received[0])
    return left[reach - before :], right[:after]


def flip(block):
    rows = block.shape[0]
    index = jnp.arange(rows, dtype=jnp.int32)
    anti = (index[:, None] + index[None, :] == rows - 1).astype(block.dtype)
    return jnp.dot(anti, block, preferred_element_type=jnp.float32).astype(block.dtype)


def inside(before, rows, after):
    place = lax.axis_index("seq") * rows + jnp.arange(-before, rows + after, dtype=jnp.int32)
    return ((place >= 0) & (place < lax.axis_size("seq") * rows))[:, None]


def local(tokens, hidden, embedding, w_in, w_gate, conv_w, channel_order, gain, w_out, cotangent):
    rows, width = hidden.shape
    full = gain.shape[0]
    channels = full // width
    bf16, f32 = jnp.bfloat16, jnp.float32
    bases = jnp.arange(embedding.shape[0], dtype=jnp.int32)
    one_hot = (bases[:, None] == tokens[None, :]).astype(bf16)
    shift = lax.dot_general(one_hot, embedding, (((0,), (0,)), ((), ())), preferred_element_type=f32)
    local_input = (hidden.astype(f32) + shift).astype(bf16)

    mains = gather_relative(local_input)
    edge_source, mains[1] = lax.optimization_barrier((local_input, mains[1]))
    edges = [jnp.concatenate(halo(edge_source, BACK, AHEAD, far), axis=0) for far in range(0, channels, 2)]
    full_input = jnp.concatenate(mains, axis=1)

    w_in_r = reorder(w_in, width)
    w_gate_r = reorder(w_gate, width)
    w_out_r = reorder(w_out, width)
    gain_r = reorder(gain, width)
    order_r = reorder(channel_order, width)
    index_r = reorder(jnp.arange(full, dtype=jnp.int32), width)
    choose = (index_r[:, None] == order_r[None, :]).astype(bf16)
    choose_inverse = (order_r[:, None] == index_r[None, :width]).astype(bf16)

    early_cotangent, edges[0] = lax.optimization_barrier((cotangent, edges[0]))
    grad_terms = lax.dot_general(
        early_cotangent, w_out_r, (((1,), (1,)), ((), ())), preferred_element_type=f32
    ).astype(bf16)
    grad_own = sum_relative(
        [grad_terms[:, j * width : (j + 1) * width].astype(f32) for j in range(channels)]
    )

    edge_blocks = {}
    packed = exchange(jnp.concatenate(edges, axis=0), "ch", 1)
    for place, far in enumerate(range(0, channels, 2)):
        edge_blocks[far] = edges[place]
        edge_blocks[far ^ 1] = packed[place * (BACK + AHEAD) : (place + 1) * (BACK + AHEAD)]
    edge_input = jnp.concatenate([edge_blocks[j] for j in range(channels)], axis=1)
    projected = jnp.dot(full_input, w_in_r, preferred_element_type=f32).astype(bf16)
    projected_edge = jnp.dot(edge_input, w_in_r, preferred_element_type=f32).astype(bf16)
    level = jnp.concatenate([projected_edge[:BACK], projected, projected_edge[BACK:]], axis=0)
    gate_pre = jnp.dot(full_input, w_gate_r, preferred_element_type=f32)
    before, after = BACK, AHEAD
    saved = []
    for number, dilation in enumerate(DILATIONS):
        saved.append((level, before))
        last = number == len(DILATIONS) - 1
        next_before = 0 if last else before - 2 * dilation
        next_after = 0 if last else after - dilation
        total = 0.0
        for tap in range(4):
            begin = before - next_before + (tap - 2) * dilation
            total = total + conv_w[number, tap][None, :] * level[
                begin : begin + next_before + rows + next_after
            ].astype(f32)
        if not last:
            total = jnp.where(inside(next_before, rows, next_after), total, 0.0)
        level = total.astype(bf16)
        before, after = next_before, next_after
    level_3 = level
    sigmoid = jax.nn.sigmoid(gate_pre)
    gate_act = gate_pre * sigmoid
    gated = (level_3.astype(f32) * gate_act).astype(bf16)

    mirrored = mirror(flip(gated))
    gated_full = jnp.concatenate(gather_relative(gated), axis=1)
    grad_blocks = gather_relative(grad_own)
    mirrored, grad_blocks[channels // 2] = lax.optimization_barrier((mirrored, grad_blocks[channels // 2]))
    grad_norm = jnp.concatenate(grad_blocks, axis=1).astype(f32)
    mirrored_full = jnp.concatenate(gather_relative(mirrored), axis=1)
    combined = gated_full.astype(f32) + jnp.dot(mirrored_full, choose, preferred_element_type=f32)
    inv_scale = lax.rsqrt(jnp.mean(combined * combined, axis=1, keepdims=True) + EPSILON)
    hat = combined * inv_scale
    scaled = grad_norm * gain_r[None, :]
    row_total = jnp.sum(scaled * hat, axis=1, keepdims=True)
    grad_full = (inv_scale * (scaled - hat * row_total / full)).astype(bf16)
    grad_comb = grad_full[:, :width]
    chosen = jnp.dot(grad_full, choose_inverse, preferred_element_type=f32).astype(bf16)
    flipped = flip(chosen)
    normalized = (hat * gain_r[None, :]).astype(bf16)
    normalized, flipped = lax.optimization_barrier((normalized, flipped))
    grad_mirror = mirror(flipped)

    output = (
        local_input.astype(f32) + jnp.dot(normalized, w_out_r, preferred_element_type=f32)
    ).astype(bf16)

    contract_rows = (((0,), (0,)), ((), ()))

    def weight_grad(left, right):
        product = lax.dot_general(left, right, contract_rows, preferred_element_type=f32)
        return reorder(product.astype(bf16), width)

    steps = distances("seq")
    turned = steps[1:] + steps[:1]
    sum_out = weight_grad(normalized, cotangent)
    sum_out = halve(sum_out, steps[0])
    grad_comb, sum_out = lax.optimization_barrier((grad_comb, sum_out))

    grad_gated = grad_comb.astype(f32) + grad_mirror.astype(f32)
    upstream = (grad_gated * gate_act).astype(bf16)
    grad_gate_pre = (
        grad_gated * level_3.astype(f32) * sigmoid * (1.0 + gate_pre * (1.0 - sigmoid))
    ).astype(bf16)
    before, after = AHEAD, BACK
    left, right = halo(upstream, before, after)
    sum_out = halve(sum_out, steps[1])
    extended = jnp.concatenate([left, upstream, right], axis=0)
    extended, sum_out = lax.optimization_barrier((extended, sum_out))
    rest = [(halve, distance) for distance in steps[2:]] + [(double, distance) for distance in steps[::-1]]
    tap_grads = []
    for number in reversed(range(len(DILATIONS))):
        dilation = DILATIONS[number]
        source, source_before = saved[number]
        own = extended[before : before + rows].astype(f32)
        for tap in range(4):
            begin = source_before + (tap - 2) * dilation
            tap_grads.append(jnp.sum(own * source[begin : begin + rows].astype(f32), axis=0))
        last = number == 0
        next_before = 0 if last else before - dilation
        next_after = 0 if last else after - 2 * dilation
        total = 0.0
        for tap in range(4):
            begin = before - next_before - (tap - 2) * dilation
            total = total + conv_w[number, tap][None, :] * extended[
                begin : begin + next_before + rows + next_after
            ].astype(f32)
        if not last:
            total = jnp.where(inside(next_before, rows, next_after), total, 0.0)
        extended = total.astype(bf16)
        before, after = next_before, next_after
    taps = jnp.stack([tap_grads[4 * (2 - number) + tap] for number in range(3) for tap in range(4)])
    spare = -taps.shape[0] % 128
    product = jnp.concatenate(
        [
            weight_grad(full_input, extended),
            jnp.pad(taps, ((0, spare), (0, 0))).astype(bf16),
        ],
        axis=0,
    )
    sum_in, sum_gate = product, weight_grad(full_input, grad_gate_pre)
    for place in range(len(steps)):
        sum_in, sum_gate, sum_out = lax.optimization_barrier((sum_in, sum_gate, sum_out))
        sum_in = halve(sum_in, steps[place])
        sum_gate = halve(sum_gate, turned[place])
        move, distance = rest.pop(0)
        sum_out = move(sum_out, distance)
    for place in reversed(range(len(steps))):
        sum_in, sum_gate, sum_out = lax.optimization_barrier((sum_in, sum_gate, sum_out))
        sum_in = double(sum_in, steps[place])
        sum_gate = double(sum_gate, turned[place])
        if rest:
            move, distance = rest.pop(0)
            sum_out = move(sum_out, distance)
    for move, distance in rest:
        sum_out = move(sum_out, distance)
    grad_in = sum_in[:full]
    grad_conv = sum_in[full : full + taps.shape[0]].astype(f32).reshape(conv_w.shape)
    return output, grad_in, sum_gate, sum_out, grad_conv


def solution(mesh):
    placed = (
        P("seq"),
        P("seq", "ch"),
        P(None, "ch"),
        P(None, "ch"),
        P(None, "ch"),
        P(None, None, "ch"),
        P(),
        P(),
        P(None, "ch"),
        P("seq", "ch"),
    )
    return jax.shard_map(
        local,
        mesh=mesh,
        in_specs=placed,
        out_specs=(
            P("seq", "ch"),
            P(None, "ch"),
            P(None, "ch"),
            P(None, "ch"),
            P(None, None, "ch"),
        ),
        check_vma=False,
    )
```

```python
import jax
import jax.numpy as jnp
from jax import lax
from jax.sharding import PartitionSpec as P

DILATIONS = (1, 8, 64)
EPSILON = 1e-06
REACH_BACK = 2 * sum(DILATIONS)
REACH_AHEAD = sum(DILATIONS)
BACK = -(-REACH_BACK // 16) * 16
AHEAD = -(-REACH_AHEAD // 16) * 16
def exchange(block, axis, distance):
    count = lax.axis_size(axis)
    return lax.ppermute(block, axis, [(i, i ^ distance) for i in range(count)])


def distances(axis):
    return [1 << bit for bit in range(lax.axis_size(axis).bit_length() - 1)]


def gather_relative(block):
    blocks = {0: block}
    for distance in reversed(distances("ch")):
        for j in list(blocks):
            blocks[j ^ distance] = exchange(blocks[j], "ch", distance)
    return [blocks[j] for j in range(len(blocks))]


def halve(part, distance):
    half = part.shape[0] // 2
    bit = (lax.axis_index("seq") & distance) // distance
    sent = lax.dynamic_slice_in_dim(part, (1 - bit) * half, half, 0).astype(jnp.bfloat16)
    kept = lax.dynamic_slice_in_dim(part, bit * half, half, 0)
    return kept.astype(jnp.float32) + exchange(sent, "seq", distance).astype(jnp.float32)


def double(part, distance):
    part = part.astype(jnp.bfloat16)
    bit = (lax.axis_index("seq") & distance) // distance
    other = exchange(part, "seq", distance)
    return jnp.where(
        bit == 0, jnp.concatenate([part, other], axis=0), jnp.concatenate([other, part], axis=0)
    )


def reorder(array, width, axis=0):
    me = lax.axis_index("ch")
    count = lax.axis_size("ch")
    return jnp.concatenate(
        [lax.dynamic_slice_in_dim(array, (me ^ j) * width, width, axis) for j in range(count)], axis=axis
    )


def mirror(block):
    count = lax.axis_size("seq")
    return lax.ppermute(block, "seq", [(i, count - 1 - i) for i in range(count)])


def pair_routes(turn):
    count = lax.axis_size("seq")
    return [(low, low + 1) for low in range(turn, count - 1, 2)]


def halo(block, before, after, far=0):
    reach = max(before, after)
    odd = lax.axis_index("seq") % 2 == 1
    head, tail = block[:reach], block[block.shape[0] - reach :]
    received = []
    for turn in range(2):
        channels = lax.axis_size("ch")
        route = []
        for low, high in pair_routes(turn):
            for c in range(channels):
                route.append((low * channels + c, high * channels + (c ^ far)))
                route.append((high * channels + c, low * channels + (c ^ far)))
        sent = jnp.where(odd, head, tail) if turn == 0 else jnp.where(odd, tail, head)
        received.append(lax.ppermute(sent, ("seq", "ch"), route))
    left = jnp.where(odd, received[0], received[1])
    right = jnp.where(odd, received[1], received[0])
    return left[reach - before :], right[:after]


def flip(block):
    rows = block.shape[0]
    index = jnp.arange(rows, dtype=jnp.int32)
    anti = (index[:, None] + index[None, :] == rows - 1).astype(block.dtype)
    return jnp.dot(anti, block, preferred_element_type=jnp.float32).astype(block.dtype)


def inside(before, rows, after):
    place = lax.axis_index("seq") * rows + jnp.arange(-before, rows + after, dtype=jnp.int32)
    return ((place >= 0) & (place < lax.axis_size("seq") * rows))[:, None]


def local(tokens, hidden, embedding, w_in, w_gate, conv_w, channel_order, gain, w_out, cotangent):
    rows, width = hidden.shape
    full = gain.shape[0]
    channels = full // width
    bf16, f32 = jnp.bfloat16, jnp.float32
    bases = jnp.arange(embedding.shape[0], dtype=jnp.int32)
    one_hot = (bases[:, None] == tokens[None, :]).astype(bf16)
    shift = lax.dot_general(one_hot, embedding, (((0,), (0,)), ((), ())), preferred_element_type=f32)
    local_input = (hidden.astype(f32) + shift).astype(bf16)

    mains = gather_relative(local_input)
    edge_source, mains[1] = lax.optimization_barrier((local_input, mains[1]))
    edges = [jnp.concatenate(halo(edge_source, BACK, AHEAD, far), axis=0) for far in range(0, channels, 2)]
    full_input = jnp.concatenate(mains, axis=1)

    w_in_r = reorder(w_in, width)
    w_gate_r = reorder(w_gate, width)
    w_out_r = reorder(w_out, width)
    gain_r = reorder(gain, width)
    order_r = reorder(channel_order, width)
    index_r = reorder(jnp.arange(full, dtype=jnp.int32), width)
    choose = (index_r[:, None] == order_r[None, :]).astype(bf16)
    choose_inverse = (order_r[:, None] == index_r[None, :width]).astype(bf16)

    mirrored_cotangent = mirror(flip(cotangent))
    w_out_r, mains[channels // 2] = lax.optimization_barrier((w_out_r, mains[channels // 2]))
    w_out_blocks = gather_relative(w_out_r)
    both_cotangent = jnp.concatenate([cotangent, mirrored_cotangent], axis=0)
    send_cotangent, w_out_blocks[channels // 2] = lax.optimization_barrier(
        (both_cotangent, w_out_blocks[channels // 2])
    )
    all_cotangent = jnp.concatenate(gather_relative(send_cotangent), axis=1)
    all_w_out = jnp.concatenate(
        [
            jnp.concatenate(
                [w_out_blocks[j][(i ^ j) * width : ((i ^ j) + 1) * width] for i in range(channels)], axis=0
            )
            for j in range(channels)
        ],
        axis=1,
    )
    grad_norm = lax.dot_general(
        all_cotangent, all_w_out, (((1,), (1,)), ((), ())), preferred_element_type=f32
    ).astype(bf16)

    edge_blocks = {}
    packed = exchange(jnp.concatenate(edges, axis=0), "ch", 1)
    for place, far in enumerate(range(0, channels, 2)):
        edge_blocks[far] = edges[place]
        edge_blocks[far ^ 1] = packed[place * (BACK + AHEAD) : (place + 1) * (BACK + AHEAD)]
    edge_input = jnp.concatenate([edge_blocks[j] for j in range(channels)], axis=1)
    projected = jnp.dot(full_input, w_in_r, preferred_element_type=f32).astype(bf16)
    projected_edge = jnp.dot(edge_input, w_in_r, preferred_element_type=f32).astype(bf16)
    level = jnp.concatenate([projected_edge[:BACK], projected, projected_edge[BACK:]], axis=0)
    gate_pre = jnp.dot(full_input, w_gate_r, preferred_element_type=f32)
    before, after = BACK, AHEAD
    saved = []
    for number, dilation in enumerate(DILATIONS):
        saved.append((level, before))
        last = number == len(DILATIONS) - 1
        next_before = 0 if last else before - 2 * dilation
        next_after = 0 if last else after - dilation
        total = 0.0
        for tap in range(4):
            begin = before - next_before + (tap - 2) * dilation
            total = total + conv_w[number, tap][None, :] * level[
                begin : begin + next_before + rows + next_after
            ].astype(f32)
        if not last:
            total = jnp.where(inside(next_before, rows, next_after), total, 0.0)
        level = total.astype(bf16)
        before, after = next_before, next_after
    level_3 = level
    sigmoid = jax.nn.sigmoid(gate_pre)
    gate_act = gate_pre * sigmoid
    gated = (level_3.astype(f32) * gate_act).astype(bf16)

    mirrored = mirror(flip(gated))
    gated_full = jnp.concatenate(gather_relative(gated), axis=1)
    mirrored_full = jnp.concatenate(gather_relative(mirrored), axis=1)
    combined = jnp.concatenate([gated_full, mirrored_full], axis=0).astype(f32) + jnp.dot(
        jnp.concatenate([mirrored_full, gated_full], axis=0), choose, preferred_element_type=f32
    )
    inv_scale = lax.rsqrt(jnp.mean(combined * combined, axis=1, keepdims=True) + EPSILON)
    hat = combined * inv_scale
    scaled = grad_norm.astype(f32) * gain_r[None, :]
    row_total = jnp.sum(scaled * hat, axis=1, keepdims=True)
    grad_comb = (inv_scale * (scaled - hat * row_total / full)).astype(bf16)
    grad_gated = grad_comb[:rows, :width].astype(f32) + jnp.dot(
        grad_comb[rows:], choose_inverse, preferred_element_type=f32
    )
    both_normalized = (hat * gain_r[None, :]).astype(bf16)
    normalized = both_normalized[:rows]

    output = (
        local_input.astype(f32) + jnp.dot(normalized, w_out_r, preferred_element_type=f32)
    ).astype(bf16)

    contract_rows = (((0,), (0,)), ((), ()))

    def weight_grad(left, right):
        product = lax.dot_general(left, right, contract_rows, preferred_element_type=f32)
        return reorder(product.astype(bf16), width)

    steps = distances("seq")
    turned = steps[1:] + steps[:1]
    side = lax.axis_index("seq") % 2
    picked = jnp.concatenate(
        [
            lax.dynamic_slice_in_dim(
                both_normalized, ((side * (channels // 2) + j) ^ lax.axis_index("ch")) * width, width, 1
            )
            for j in range(channels // 2)
        ],
        axis=1,
    )
    sum_out = lax.dot_general(picked, both_cotangent, contract_rows, preferred_element_type=f32)

    upstream = (grad_gated * gate_act).astype(bf16)
    grad_gate_pre = (
        grad_gated * level_3.astype(f32) * sigmoid * (1.0 + gate_pre * (1.0 - sigmoid))
    ).astype(bf16)
    before, after = AHEAD, BACK
    left, right = halo(upstream, before, after)
    sum_gate = halve(weight_grad(full_input, grad_gate_pre), turned[0])
    sum_out = halve(sum_out, turned[0])
    extended = jnp.concatenate([left, upstream, right], axis=0)
    extended, sum_gate, sum_out = lax.optimization_barrier((extended, sum_gate, sum_out))
    rest_gate = [(halve, distance) for distance in turned[1:]] + [(double, distance) for distance in turned[::-1]]
    rest_out = [(halve, distance) for distance in turned[1:-1]] + [
        (double, distance) for distance in steps[::-1]
    ]
    tap_grads = []
    for number in reversed(range(len(DILATIONS))):
        dilation = DILATIONS[number]
        source, source_before = saved[number]
        own = extended[before : before + rows].astype(f32)
        for tap in range(4):
            begin = source_before + (tap - 2) * dilation
            tap_grads.append(jnp.sum(own * source[begin : begin + rows].astype(f32), axis=0))
        last = number == 0
        next_before = 0 if last else before - dilation
        next_after = 0 if last else after - 2 * dilation
        total = 0.0
        for tap in range(4):
            begin = before - next_before - (tap - 2) * dilation
            total = total + conv_w[number, tap][None, :] * extended[
                begin : begin + next_before + rows + next_after
            ].astype(f32)
        if not last:
            total = jnp.where(inside(next_before, rows, next_after), total, 0.0)
        extended = total.astype(bf16)
        before, after = next_before, next_after
    taps = jnp.stack([tap_grads[4 * (2 - number) + tap] for number in range(3) for tap in range(4)])
    spare = -taps.shape[0] % 128
    product = jnp.concatenate(
        [
            weight_grad(full_input, extended),
            jnp.pad(taps, ((0, spare), (0, 0))).astype(bf16),
        ],
        axis=0,
    )
    sum_in = product
    rest_in = [(halve, distance) for distance in steps] + [(double, distance) for distance in steps[::-1]]
    for place, (move, distance) in enumerate(rest_in):
        sum_in, sum_gate, sum_out = lax.optimization_barrier((sum_in, sum_gate, sum_out))
        sum_in = move(sum_in, distance)
        if place < len(rest_gate):
            move, distance = rest_gate[place]
            sum_gate = move(sum_gate, distance)
        if place < len(rest_out):
            move, distance = rest_out[place]
            sum_out = move(sum_out, distance)
    grad_in = sum_in[:full]
    grad_conv = sum_in[full : full + taps.shape[0]].astype(f32).reshape(conv_w.shape)
    return output, grad_in, sum_gate, sum_out, grad_conv


def solution(mesh):
    placed = (
        P("seq"),
        P("seq", "ch"),
        P(None, "ch"),
        P(None, "ch"),
        P(None, "ch"),
        P(None, None, "ch"),
        P(),
        P(),
        P(None, "ch"),
        P("seq", "ch"),
    )
    return jax.shard_map(
        local,
        mesh=mesh,
        in_specs=placed,
        out_specs=(
            P("seq", "ch"),
            P(None, "ch"),
            P(None, "ch"),
            P(None, "ch"),
            P(None, None, "ch"),
        ),
        check_vma=False,
    )
```

```python
import jax
import jax.numpy as jnp
from jax import lax
from jax.sharding import PartitionSpec as P

DILATIONS = (1, 8, 64)
EPSILON = 1e-06
REACH_BACK = 2 * sum(DILATIONS)
REACH_AHEAD = sum(DILATIONS)
BACK = -(-REACH_BACK // 16) * 16
AHEAD = -(-REACH_AHEAD // 16) * 16
def exchange(block, axis, distance):
    count = lax.axis_size(axis)
    return lax.ppermute(block, axis, [(i, i ^ distance) for i in range(count)])


def distances(axis):
    return [1 << bit for bit in range(lax.axis_size(axis).bit_length() - 1)]


def gather_relative(block):
    blocks = {0: block}
    for distance in reversed(distances("ch")):
        for j in list(blocks):
            blocks[j ^ distance] = exchange(blocks[j], "ch", distance)
    return [blocks[j] for j in range(len(blocks))]


def halve(part, distance):
    half = part.shape[0] // 2
    bit = (lax.axis_index("seq") & distance) // distance
    sent = lax.dynamic_slice_in_dim(part, (1 - bit) * half, half, 0).astype(jnp.bfloat16)
    kept = lax.dynamic_slice_in_dim(part, bit * half, half, 0)
    return kept.astype(jnp.float32) + exchange(sent, "seq", distance).astype(jnp.float32)


def double(part, distance):
    part = part.astype(jnp.bfloat16)
    bit = (lax.axis_index("seq") & distance) // distance
    other = exchange(part, "seq", distance)
    return jnp.where(
        bit == 0, jnp.concatenate([part, other], axis=0), jnp.concatenate([other, part], axis=0)
    )


def reorder(array, width, axis=0):
    me = lax.axis_index("ch")
    count = lax.axis_size("ch")
    return jnp.concatenate(
        [lax.dynamic_slice_in_dim(array, (me ^ j) * width, width, axis) for j in range(count)], axis=axis
    )


def mirror(block):
    count = lax.axis_size("seq")
    return lax.ppermute(block, "seq", [(i, count - 1 - i) for i in range(count)])


def pair_routes(turn):
    count = lax.axis_size("seq")
    return [(low, low + 1) for low in range(turn, count - 1, 2)]


def halo(block, before, after, far=0):
    reach = max(before, after)
    odd = lax.axis_index("seq") % 2 == 1
    head, tail = block[:reach], block[block.shape[0] - reach :]
    received = []
    for turn in range(2):
        channels = lax.axis_size("ch")
        route = []
        for low, high in pair_routes(turn):
            for c in range(channels):
                route.append((low * channels + c, high * channels + (c ^ far)))
                route.append((high * channels + c, low * channels + (c ^ far)))
        sent = jnp.where(odd, head, tail) if turn == 0 else jnp.where(odd, tail, head)
        received.append(lax.ppermute(sent, ("seq", "ch"), route))
    left = jnp.where(odd, received[0], received[1])
    right = jnp.where(odd, received[1], received[0])
    return left[reach - before :], right[:after]


def flip(block):
    rows = block.shape[0]
    index = jnp.arange(rows, dtype=jnp.int32)
    anti = (index[:, None] + index[None, :] == rows - 1).astype(block.dtype)
    return jnp.dot(anti, block, preferred_element_type=jnp.float32).astype(block.dtype)


def inside(before, rows, after):
    place = lax.axis_index("seq") * rows + jnp.arange(-before, rows + after, dtype=jnp.int32)
    return ((place >= 0) & (place < lax.axis_size("seq") * rows))[:, None]


def local(tokens, hidden, embedding, w_in, w_gate, conv_w, channel_order, gain, w_out, cotangent):
    rows, width = hidden.shape
    full = gain.shape[0]
    channels = full // width
    bf16, f32 = jnp.bfloat16, jnp.float32
    bases = jnp.arange(embedding.shape[0], dtype=jnp.int32)
    one_hot = (bases[:, None] == tokens[None, :]).astype(bf16)
    shift = lax.dot_general(one_hot, embedding, (((0,), (0,)), ((), ())), preferred_element_type=f32)
    local_input = (hidden.astype(f32) + shift).astype(bf16)

    mains = gather_relative(local_input)
    edge_source, mains[1] = lax.optimization_barrier((local_input, mains[1]))
    edges = [jnp.concatenate(halo(edge_source, BACK, AHEAD, far), axis=0) for far in range(0, channels, 2)]
    full_input = jnp.concatenate(mains, axis=1)

    w_in_r = reorder(w_in, width)
    w_gate_r = reorder(w_gate, width)
    w_out_r = reorder(w_out, width)
    gain_r = reorder(gain, width)
    order_r = reorder(channel_order, width)
    index_r = reorder(jnp.arange(full, dtype=jnp.int32), width)
    choose = (index_r[:, None] == order_r[None, :]).astype(bf16)
    choose_inverse = (order_r[:, None] == index_r[None, :width]).astype(bf16)

    early_cotangent, edges[0] = lax.optimization_barrier((flip(cotangent), edges[0]))
    mirrored_cotangent = mirror(early_cotangent)
    w_out_r, mains[channels // 2] = lax.optimization_barrier((w_out_r, mains[channels // 2]))
    w_out_blocks = gather_relative(w_out_r)
    both_cotangent = jnp.concatenate([cotangent, mirrored_cotangent], axis=0)
    send_cotangent, w_out_blocks[channels // 2] = lax.optimization_barrier(
        (both_cotangent, w_out_blocks[channels // 2])
    )
    cotangent_blocks = gather_relative(send_cotangent)
    all_w_out = jnp.concatenate(
        [
            jnp.concatenate(
                [w_out_blocks[j][(i ^ j) * width : ((i ^ j) + 1) * width] for i in range(channels)], axis=0
            )
            for j in range(channels)
        ],
        axis=1,
    )
    edge_blocks = {}
    packed = exchange(jnp.concatenate(edges, axis=0), "ch", 1)
    for place, far in enumerate(range(0, channels, 2)):
        edge_blocks[far] = edges[place]
        edge_blocks[far ^ 1] = packed[place * (BACK + AHEAD) : (place + 1) * (BACK + AHEAD)]
    edge_input = jnp.concatenate([edge_blocks[j] for j in range(channels)], axis=1)
    projected = jnp.dot(full_input, w_in_r, preferred_element_type=f32).astype(bf16)
    projected_edge = jnp.dot(edge_input, w_in_r, preferred_element_type=f32).astype(bf16)
    level = jnp.concatenate([projected_edge[:BACK], projected, projected_edge[BACK:]], axis=0)
    gate_pre = jnp.dot(full_input, w_gate_r, preferred_element_type=f32)
    before, after = BACK, AHEAD
    saved = []
    for number, dilation in enumerate(DILATIONS):
        saved.append((level, before))
        last = number == len(DILATIONS) - 1
        next_before = 0 if last else before - 2 * dilation
        next_after = 0 if last else after - dilation
        total = 0.0
        for tap in range(4):
            begin = before - next_before + (tap - 2) * dilation
            total = total + conv_w[number, tap][None, :] * level[
                begin : begin + next_before + rows + next_after
            ].astype(f32)
        if not last:
            total = jnp.where(inside(next_before, rows, next_after), total, 0.0)
        level = total.astype(bf16)
        before, after = next_before, next_after
    level_3 = level
    sigmoid = jax.nn.sigmoid(gate_pre)
    gate_act = gate_pre * sigmoid
    gated = (level_3.astype(f32) * gate_act).astype(bf16)

    mirrored = mirror(flip(gated))
    gated_full = jnp.concatenate(gather_relative(gated), axis=1)
    mirrored, cotangent_blocks[channels // 2] = lax.optimization_barrier(
        (mirrored, cotangent_blocks[channels // 2])
    )
    mirrored_full = jnp.concatenate(gather_relative(mirrored), axis=1)
    all_cotangent = jnp.concatenate(cotangent_blocks, axis=1)
    grad_norm = lax.dot_general(
        all_cotangent, all_w_out, (((1,), (1,)), ((), ())), preferred_element_type=f32
    ).astype(bf16)
    combined = jnp.concatenate([gated_full, mirrored_full], axis=0).astype(f32) + jnp.dot(
        jnp.concatenate([mirrored_full, gated_full], axis=0), choose, preferred_element_type=f32
    )
    inv_scale = lax.rsqrt(jnp.mean(combined * combined, axis=1, keepdims=True) + EPSILON)
    hat = combined * inv_scale
    scaled = grad_norm.astype(f32) * gain_r[None, :]
    row_total = jnp.sum(scaled * hat, axis=1, keepdims=True)
    grad_comb = (inv_scale * (scaled - hat * row_total / full)).astype(bf16)
    grad_gated = grad_comb[:rows, :width].astype(f32) + jnp.dot(
        grad_comb[rows:], choose_inverse, preferred_element_type=f32
    )
    both_normalized = (hat * gain_r[None, :]).astype(bf16)
    normalized = both_normalized[:rows]

    output = (
        local_input.astype(f32) + jnp.dot(normalized, w_out_r, preferred_element_type=f32)
    ).astype(bf16)

    contract_rows = (((0,), (0,)), ((), ()))

    def weight_grad(left, right):
        product = lax.dot_general(left, right, contract_rows, preferred_element_type=f32)
        return reorder(product.astype(bf16), width)

    steps = distances("seq")
    turned = steps[1:] + steps[:1]
    side = lax.axis_index("seq") % 2
    picked = jnp.concatenate(
        [
            lax.dynamic_slice_in_dim(
                both_normalized, ((side * (channels // 2) + j) ^ lax.axis_index("ch")) * width, width, 1
            )
            for j in range(channels // 2)
        ],
        axis=1,
    )
    sum_out = lax.dot_general(picked, both_cotangent, contract_rows, preferred_element_type=f32)

    upstream = (grad_gated * gate_act).astype(bf16)
    grad_gate_pre = (
        grad_gated * level_3.astype(f32) * sigmoid * (1.0 + gate_pre * (1.0 - sigmoid))
    ).astype(bf16)
    before, after = AHEAD, BACK
    left, right = halo(upstream, before, after)
    sum_gate = halve(weight_grad(full_input, grad_gate_pre), steps[0])
    sum_out = halve(sum_out, turned[0])
    extended = jnp.concatenate([left, upstream, right], axis=0)
    rest_gate = [(halve, distance) for distance in turned[:-1]] + [(double, distance) for distance in steps[::-1]]
    rest_out = [(halve, distance) for distance in turned[1:-1]] + [
        (double, distance) for distance in steps[::-1]
    ]
    tap_grads = []
    for number in reversed(range(len(DILATIONS))):
        dilation = DILATIONS[number]
        source, source_before = saved[number]
        own = extended[before : before + rows].astype(f32)
        for tap in range(4):
            begin = source_before + (tap - 2) * dilation
            tap_grads.append(jnp.sum(own * source[begin : begin + rows].astype(f32), axis=0))
        last = number == 0
        next_before = 0 if last else before - dilation
        next_after = 0 if last else after - 2 * dilation
        total = 0.0
        for tap in range(4):
            begin = before - next_before - (tap - 2) * dilation
            total = total + conv_w[number, tap][None, :] * extended[
                begin : begin + next_before + rows + next_after
            ].astype(f32)
        if not last:
            total = jnp.where(inside(next_before, rows, next_after), total, 0.0)
        extended = total.astype(bf16)
        before, after = next_before, next_after
    taps = jnp.stack([tap_grads[4 * (2 - number) + tap] for number in range(3) for tap in range(4)])
    spare = -taps.shape[0] % 128
    product = jnp.concatenate(
        [
            weight_grad(full_input, extended),
            jnp.pad(taps, ((0, spare), (0, 0))).astype(bf16),
        ],
        axis=0,
    )
    sum_in = product
    rest_in = [(halve, distance) for distance in steps] + [(double, distance) for distance in steps[::-1]]
    for place, (move, distance) in enumerate(rest_in):
        sum_in, sum_gate, sum_out = lax.optimization_barrier((sum_in, sum_gate, sum_out))
        sum_in = move(sum_in, distance)
        if place < len(rest_gate):
            move, distance = rest_gate[place]
            sum_gate = move(sum_gate, distance)
        if place < len(rest_out):
            move, distance = rest_out[place]
            sum_out = move(sum_out, distance)
    grad_in = sum_in[:full]
    grad_conv = sum_in[full : full + taps.shape[0]].astype(f32).reshape(conv_w.shape)
    return output, grad_in, sum_gate, sum_out, grad_conv


def solution(mesh):
    placed = (
        P("seq"),
        P("seq", "ch"),
        P(None, "ch"),
        P(None, "ch"),
        P(None, "ch"),
        P(None, None, "ch"),
        P(),
        P(),
        P(None, "ch"),
        P("seq", "ch"),
    )
    return jax.shard_map(
        local,
        mesh=mesh,
        in_specs=placed,
        out_specs=(
            P("seq", "ch"),
            P(None, "ch"),
            P(None, "ch"),
            P(None, "ch"),
            P(None, None, "ch"),
        ),
        check_vma=False,
    )
```

```python
import functools

import jax
import jax.numpy as jnp
from jax import lax
from jax.experimental import pallas as pl
from jax.experimental.pallas import tpu as pltpu
from jax.sharding import PartitionSpec as P

DILATIONS = (1, 8, 64)
EPSILON = 1e-06
FORE = (160, 144, 128, 0)
AFT = (80, 72, 64, 0)
BACK_FORE = (0, 8, 16, 80)
BACK_AFT = (0, 8, 24, 160)
EDGE = 160
SPARE = 64

BF16, F32 = jnp.bfloat16, jnp.float32
ROWS_DOT = (((0,), (0,)), ((), ()))
LAST_DOT = (((1,), (1,)), ((), ()))


def dot(left, right, dims=(((1,), (0,)), ((), ()))):
    return lax.dot_general(left, right, dims, preferred_element_type=F32)


def run(body, place, operands, outs, scratch=(), megabytes=16, gflop=0.1):
    moved = sum(x.size * x.dtype.itemsize for x in operands)
    return pl.pallas_call(
        body,
        out_shape=[jax.ShapeDtypeStruct(shape, dtype) for shape, dtype in outs],
        in_specs=[pl.BlockSpec(memory_space=pltpu.SMEM)]
        + [pl.BlockSpec(memory_space=pltpu.VMEM)] * len(operands),
        out_specs=[pl.BlockSpec(memory_space=pltpu.VMEM)] * len(outs),
        scratch_shapes=list(scratch),
        compiler_params=pltpu.CompilerParams(vmem_limit_bytes=megabytes << 20),
        cost_estimate=pl.CostEstimate(flops=int(gflop * 1e9), bytes_accessed=moved, transcendentals=0),
    )(place, *operands)


def part(index, size, multiple=None):
    return pl.ds(pl.multiple_of(index * size, multiple or size), size)


def anti_identity(rows):
    down = lax.broadcasted_iota(jnp.int32, (rows, rows), 0)
    across = lax.broadcasted_iota(jnp.int32, (rows, rows), 1)
    return (down + across == rows - 1).astype(F32).astype(BF16)


def input_kernel(place, tokens, hidden, embedding, block_in, first, second, padded):
    bases, rows = embedding.shape[0], hidden.shape[0]
    padded[...] = jnp.zeros_like(padded)
    padded[:bases] = embedding[...].astype(F32)
    base = lax.broadcasted_iota(jnp.int32, (padded.shape[0], rows), 0)
    one_hot = (base == tokens[...]).astype(F32).astype(BF16)
    shift = dot(one_hot, padded[...].astype(BF16), ROWS_DOT)
    block_in[...] = (hidden[...].astype(F32) + shift).astype(BF16)
    odd = place[0] % 2
    far = rows - EDGE
    first[...] = block_in[pl.ds(pl.multiple_of((1 - odd) * far, 16), EDGE), :]
    second[...] = block_in[pl.ds(pl.multiple_of(odd * far, 16), EDGE), :]


def setup_kernel(place, cotangent, order, flipped, choose):
    flipped[...] = dot(anti_identity(cotangent.shape[0]), cotangent[...]).astype(BF16)
    me, width = place[1], cotangent.shape[1]
    down = lax.broadcasted_iota(jnp.int32, (width, width), 0)
    for j in range(order.shape[1] // width):
        for i in range(order.shape[1] // width):
            wanted = order[:, part(me ^ i, width)]
            choose[j * width : (j + 1) * width, i * width : (i + 1) * width] = (
                (down + (me ^ j) * width == wanted).astype(F32).astype(BF16)
            )


def project_kernel(channels, place, *refs):
    mains, (w_in, w_gate, projected, gate_pre) = refs[:channels], refs[channels:]
    me, width = place[1], mains[0].shape[1]
    for weight, out in ((w_in, projected), (w_gate, gate_pre)):
        total = dot(mains[0][...], weight[part(me, width), :])
        for j in range(1, channels):
            total += dot(mains[j][...], weight[part(me ^ j, width), :])
        out[...] = total


def keep_inside(total, place, before, rows):
    position = lax.broadcasted_iota(jnp.int32, total.shape, 0) + (place[0] * rows - before)
    return jnp.where((position >= 0) & (position < place[2] * rows), total, 0.0)


def forward_kernel(channels, place, edges, edges_core, w_in, projected, gate_pre, conv_w, *outs):
    level_0, level_1, level_2, level_3, gated, flipped = outs
    me, odd = place[1], place[0] % 2
    rows, width = projected.shape
    left = jnp.zeros((EDGE, width), F32)
    right = jnp.zeros((AFT[0], width), F32)
    for j in range(channels):
        source = edges_core if j % 2 else edges
        base = (j // 2) * 2 * EDGE
        weight = w_in[part(me ^ j, width), :]
        left += dot(source[pl.ds(pl.multiple_of(base + (1 - odd) * EDGE, 16), EDGE), :], weight)
        right += dot(source[pl.ds(pl.multiple_of(base + odd * EDGE, 16), AFT[0]), :], weight)
    level_0[:EDGE] = left
    level_0[EDGE : EDGE + rows] = projected[...]
    level_0[EDGE + rows :] = right
    source = level_0
    for number, (dilation, target) in enumerate(zip(DILATIONS, (level_1, level_2, level_3))):
        shift = FORE[number] - FORE[number + 1]
        count = target.shape[0]
        total = jnp.zeros((count, width), F32)
        for tap in range(4):
            begin = shift + (tap - 2) * dilation
            total += conv_w[number, tap : tap + 1, :] * source[begin : begin + count]
        if FORE[number + 1]:
            total = keep_inside(total, place, FORE[number + 1], rows)
        target[...] = total
        source = target
    gate = gate_pre[...]
    gated[...] = (level_3[...] * (gate / (1.0 + jnp.exp(-gate)))).astype(BF16)
    flipped[...] = dot(anti_identity(rows), gated[...]).astype(BF16)


def norm_grad_kernel(channels, place, *refs):
    own, mirrored = refs[:channels], refs[channels : 2 * channels]
    near, near_core, far_mine, far_other, far_core_mine, far_core_other, out, far, far_core = refs[2 * channels :]
    me, side = place[1], place[0] % 2
    half = far_mine.shape[0]
    for whole, mine, other in ((far, far_mine, far_other), (far_core, far_core_mine, far_core_other)):
        whole[part(side, half), :] = mine[...]
        whole[part(1 - side, half), :] = other[...]
    weights = (near, near_core, far, far_core)
    rows, width = own[0].shape
    for block, cotangents in enumerate((own, mirrored)):
        for i in range(channels):
            total = jnp.zeros((rows, width), F32)
            for j in range(channels):
                total += dot(cotangents[j][...], weights[j][part(i ^ me, width), :], LAST_DOT)
            out[block * rows : (block + 1) * rows, i * width : (i + 1) * width] = total.astype(BF16)


def combine_kernel(channels, place, *refs):
    own, mirrored = refs[:channels], refs[channels : 2 * channels]
    grad_norm, choose, gain, gate_pre, level_3 = refs[2 * channels : 2 * channels + 5]
    normalized, upstream, grad_gate_pre, first, second, gains, grad_gated = refs[2 * channels + 5 :]
    me = place[1]
    rows, width = own[0].shape
    full = channels * width
    tile = rows // 4
    for j in range(channels):
        gains[:, j * width : (j + 1) * width] = gain[:, part(me ^ j, width)]
    for block, (here, there) in enumerate(((own, mirrored), (mirrored, own))):

        def step(k, carry, block=block, here=here, there=there):
            at = part(k, tile)
            mine = jnp.concatenate([ref[at, :].astype(F32) for ref in here], axis=1)
            other = jnp.concatenate([ref[at, :] for ref in there], axis=1)
            combined = mine + dot(other, choose[...])
            mean = jnp.sum(combined * combined, axis=1, keepdims=True) * (1.0 / full)
            inv_scale = lax.rsqrt(mean + EPSILON)
            hat = combined * inv_scale
            at_both = pl.ds(pl.multiple_of(block * rows + k * tile, tile), tile)
            normalized[at_both, :] = (hat * gains[...]).astype(BF16)
            scaled = grad_norm[at_both, :].astype(F32) * gains[...]
            row_total = jnp.sum(scaled * hat, axis=1, keepdims=True) * (1.0 / full)
            if block == 0:
                grad_gated[at, :] = inv_scale * (scaled[:, :width] - hat[:, :width] * row_total)
            else:
                grad_comb = (inv_scale * (scaled - hat * row_total)).astype(BF16)
                grad_gated[at, :] += dot(grad_comb, choose[:width, :], LAST_DOT)
            return carry

        lax.fori_loop(0, rows // tile, step, 0)
    gate = gate_pre[...]
    sigmoid = 1.0 / (1.0 + jnp.exp(-gate))
    total = grad_gated[...]
    upstream[...] = (total * (gate * sigmoid)).astype(BF16)
    grad_gate_pre[...] = (total * level_3[...] * sigmoid * (1.0 + gate * (1.0 - sigmoid))).astype(BF16)
    odd, far = place[0] % 2, rows - EDGE
    first[...] = upstream[pl.ds(pl.multiple_of((1 - odd) * far, 16), EDGE), :]
    second[...] = upstream[pl.ds(pl.multiple_of(odd * far, 16), EDGE), :]


def output_kernel(channels, place, normalized, w_out, block_in, output):
    me = place[1]
    rows, width = block_in.shape
    total = block_in[...].astype(F32)
    for j in range(channels):
        total += dot(normalized[:rows, j * width : (j + 1) * width], w_out[part(me ^ j, width), :])
    output[...] = total.astype(BF16)


def products_kernel(channels, place, normalized, cotangent, mirrored_cotangent, grad_gate_pre, *refs):
    mains = refs[:channels]
    out_sent, out_kept, gate_sent, gate_kept, whole_out, whole_gate = refs[channels:]
    me, side = place[1], place[0] % 2
    rows, width = cotangent.shape
    for j in range(channels // 2):
        block = (side * (channels // 2) + j) ^ me
        columns = part(block, width)
        whole_out[j * width : (j + 1) * width, :] = dot(
            normalized[:rows, columns], cotangent[...], ROWS_DOT
        ) + dot(normalized[rows:, columns], mirrored_cotangent[...], ROWS_DOT)
    half = whole_out.shape[0] // 2
    bit = (place[0] // 2) % 2
    out_sent[...] = whole_out[part(1 - bit, half), :].astype(BF16)
    out_kept[...] = whole_out[part(bit, half), :]
    for j in range(channels):
        whole_gate[part(me ^ j, width), :] = dot(mains[j][...], grad_gate_pre[...], ROWS_DOT)
    half = whole_gate.shape[0] // 2
    gate_sent[...] = whole_gate[part(1 - side, half), :].astype(BF16)
    gate_kept[...] = whole_gate[part(side, half), :]


def backward_kernel(channels, place, upstream, first, second, level_0, level_1, level_2, conv_w, *refs):
    mains = refs[:channels]
    sent, kept, whole, grad_3, grad_2, grad_1 = refs[channels:]
    me, odd = place[1], place[0] % 2
    rows, width = upstream.shape
    fore = BACK_FORE[3]
    even = (odd == 0).astype(F32)
    early, late = first[...].astype(F32), second[...].astype(F32)
    grad_3[:fore] = (early * (1.0 - even) + late * even)[EDGE - fore :]
    grad_3[fore : fore + rows] = upstream[...].astype(F32)
    grad_3[fore + rows :] = early * even + late * (1.0 - even)
    half = whole.shape[0] // 2
    for top in (half - SPARE, 2 * half - SPARE):
        whole[top : top + SPARE, :] = jnp.zeros((SPARE, width), F32)
    levels = (level_0, level_1, level_2)
    grads = (None, grad_1, grad_2, grad_3)
    grad_0 = None
    for number in (2, 1, 0):
        dilation, source, level = DILATIONS[number], grads[number + 1], levels[number]
        fore = BACK_FORE[number + 1]
        here = source[fore : fore + rows]
        for tap in range(4):
            begin = FORE[number] + (tap - 2) * dilation
            row = half - SPARE + 4 * number + tap
            whole[row : row + 1, :] = jnp.sum(here * level[begin : begin + rows], axis=0, keepdims=True)
        count = BACK_FORE[number] + rows + BACK_AFT[number]
        total = jnp.zeros((count, width), F32)
        for tap in range(4):
            begin = fore - BACK_FORE[number] - (tap - 2) * dilation
            total += conv_w[number, tap : tap + 1, :] * source[begin : begin + count]
        if number:
            grads[number][...] = keep_inside(total, place, BACK_FORE[number], rows)
        else:
            grad_0 = total.astype(BF16)
    for j in range(channels):
        block = me ^ j
        start = (block // (channels // 2)) * half + (block % (channels // 2)) * width
        whole[pl.ds(pl.multiple_of(start, SPARE), width), :] = dot(mains[j][...], grad_0, ROWS_DOT)
    sent[...] = whole[part(1 - odd, half), :].astype(BF16)
    kept[...] = whole[part(odd, half), :]


def exchange(block, axis, distance):
    count = lax.axis_size(axis)
    return lax.ppermute(block, axis, [(i, i ^ distance) for i in range(count)])


def distances(axis):
    return [1 << bit for bit in range(lax.axis_size(axis).bit_length() - 1)]


def mirror(block):
    count = lax.axis_size("seq")
    return lax.ppermute(block, "seq", [(i, count - 1 - i) for i in range(count)])


def swap_edges(first, second, far=0):
    count, channels = lax.axis_size("seq"), lax.axis_size("ch")
    received = []
    for turn, block in enumerate((first, second)):
        route = []
        for low in range(turn, count - 1, 2):
            for c in range(channels):
                route.append((low * channels + c, (low + 1) * channels + (c ^ far)))
                route.append(((low + 1) * channels + c, low * channels + (c ^ far)))
        received.append(lax.ppermute(block, ("seq", "ch"), route))
    return received


def together(*values):
    return lax.optimization_barrier(values)


def seq_bit(distance):
    return (lax.axis_index("seq") & distance) // distance


def halve(total, distance):
    half = total.shape[0] // 2
    bit = seq_bit(distance)
    sent = lax.dynamic_slice_in_dim(total, (1 - bit) * half, half, 0).astype(BF16)
    kept = lax.dynamic_slice_in_dim(total, bit * half, half, 0)
    return kept.astype(F32) + exchange(sent, "seq", distance).astype(F32)


def double(total, distance):
    return jnp.concatenate(both_halves(total, distance), axis=0)


def both_halves(total, distance):
    total = total.astype(BF16)
    other = exchange(total, "seq", distance)
    first = seq_bit(distance) == 0
    return jnp.where(first, total, other), jnp.where(first, other, total)


def local(tokens, hidden, embedding, w_in, w_gate, conv_w, channel_order, gain, w_out, cotangent):
    rows, width = hidden.shape
    full = gain.shape[0]
    channels = full // width
    cross = channels // 2
    taps = conv_w.shape[0] * conv_w.shape[1]
    steps = distances("seq")
    block = ((rows, width), BF16)
    place = jnp.stack([lax.axis_index("seq"), lax.axis_index("ch"), lax.axis_size("seq")]).astype(jnp.int32)

    local_input, first, second = run(
        input_kernel,
        place,
        (tokens.reshape(1, rows), hidden, embedding),
        [block, ((EDGE, width), BF16), ((EDGE, width), BF16)],
        [pltpu.VMEM((16, width), F32)],
    )
    input_x = exchange(local_input, "ch", cross)
    input_core = exchange(local_input, "ch", 1)
    near = swap_edges(first, second)
    far = swap_edges(first, second, cross)
    flipped_cotangent, choose = run(
        setup_kernel,
        place,
        (cotangent, channel_order.reshape(1, full)),
        [block, ((full, full), BF16)],
    )
    w_half = lax.dynamic_slice_in_dim(w_out, seq_bit(1) * (full // 2), full // 2, 0)
    w_half, input_x = together(w_half, input_x)
    w_x_mine = exchange(w_half, "ch", cross)
    mains = [local_input, input_core, input_x, exchange(input_x, "ch", 1)]
    edges = jnp.concatenate(near + far, axis=0)
    edges_core = exchange(edges, "ch", 1)
    edges, flipped_cotangent = together(edges, flipped_cotangent)
    mirrored_cotangent = mirror(flipped_cotangent)
    early_cotangent, w_x_mine = together(cotangent, w_x_mine)
    cotangent_x = exchange(early_cotangent, "ch", cross)
    w_x_other = exchange(w_x_mine, "seq", 1)
    late_cotangent, cotangent_x = together(mirrored_cotangent, cotangent_x)
    mirrored_cotangent_x = exchange(late_cotangent, "ch", cross)

    projected, gate_pre = run(
        functools.partial(project_kernel, channels),
        place,
        (*mains, w_in, w_gate),
        [((rows, width), F32)] * 2,
        gflop=0.6,
    )
    level_0, level_1, level_2, level_3, gated, flipped = run(
        functools.partial(forward_kernel, channels),
        place,
        (edges, edges_core, w_in, projected, gate_pre, conv_w),
        [((fore + rows + aft, width), F32) for fore, aft in zip(FORE, AFT)] + [block, block],
        megabytes=24,
        gflop=0.4,
    )
    mirrored = mirror(flipped)
    gated_x = exchange(gated, "ch", cross)
    gated_all = [gated, exchange(gated, "ch", 1), gated_x, exchange(gated_x, "ch", 1)]
    mirrored, mirrored_cotangent_x = together(mirrored, mirrored_cotangent_x)
    mirrored_x = exchange(mirrored, "ch", cross)
    cotangent_all = [cotangent, exchange(cotangent, "ch", 1), cotangent_x, exchange(cotangent_x, "ch", 1)]
    mirrored_cotangent_all = [
        mirrored_cotangent,
        exchange(mirrored_cotangent, "ch", 1),
        mirrored_cotangent_x,
        exchange(mirrored_cotangent_x, "ch", 1),
    ]
    grad_norm = run(
        functools.partial(norm_grad_kernel, channels),
        place,
        (
            *cotangent_all,
            *mirrored_cotangent_all,
            w_out,
            exchange(w_out, "ch", 1),
            w_x_mine,
            w_x_other,
            exchange(w_x_mine, "ch", 1),
            exchange(w_x_other, "ch", 1),
        ),
        [((2 * rows, full), BF16)],
        [pltpu.VMEM((full, width), BF16)] * 2,
        megabytes=24,
        gflop=2.1,
    )[0]
    mirrored_all = [mirrored, exchange(mirrored, "ch", 1), mirrored_x, exchange(mirrored_x, "ch", 1)]

    normalized, upstream, grad_gate_pre, first, second = run(
        functools.partial(combine_kernel, channels),
        place,
        (*gated_all, *mirrored_all, grad_norm, choose, gain.reshape(1, full), gate_pre, level_3),
        [((2 * rows, full), BF16), block, block, ((EDGE, width), BF16), ((EDGE, width), BF16)],
        [pltpu.VMEM((1, full), F32), pltpu.VMEM((rows, width), F32)],
        megabytes=32,
        gflop=2.5,
    )
    first, second = swap_edges(first, second)
    out_sent, out_kept, gate_sent, gate_kept = run(
        functools.partial(products_kernel, channels),
        place,
        (normalized, cotangent, mirrored_cotangent, grad_gate_pre, *mains),
        [
            ((full // 4, width), BF16),
            ((full // 4, width), F32),
            ((full // 2, width), BF16),
            ((full // 2, width), F32),
        ],
        [pltpu.VMEM((full // 2, width), F32), pltpu.VMEM((full, width), F32)],
        megabytes=24,
        gflop=0.8,
    )
    out_other = exchange(out_sent, "seq", steps[1])
    gate_other = exchange(gate_sent, "seq", steps[0])
    half = full // 2 + SPARE
    in_sent, in_kept = run(
        functools.partial(backward_kernel, channels),
        place,
        (upstream, first, second, level_0, level_1, level_2, conv_w, *mains),
        [((half, width), BF16), ((half, width), F32)],
        [pltpu.VMEM((2 * half, width), F32)]
        + [pltpu.VMEM((BACK_FORE[k] + rows + BACK_AFT[k], width), F32) for k in (3, 2, 1)],
        megabytes=24,
        gflop=0.5,
    )
    output = run(
        functools.partial(output_kernel, channels),
        place,
        (normalized, w_out, local_input),
        [block],
        gflop=0.3,
    )[0]

    sum_out = out_kept + out_other.astype(F32)
    sum_gate = gate_kept + gate_other.astype(F32)
    in_sent, sum_gate, sum_out = together(in_sent, sum_gate, sum_out)
    sum_in = in_kept + exchange(in_sent, "seq", steps[0]).astype(F32)
    undo = [(double, distance) for distance in steps[::-1]]
    rest_gate = [(halve, distance) for distance in steps[1:]] + undo
    rest_out = [(halve, distance) for distance in steps[2:]] + undo
    rest_in = [(halve, distance) for distance in steps[1:]] + undo[:-1]
    for number in range(len(rest_in) + 1):
        if number:
            sum_in, sum_gate, sum_out = together(sum_in, sum_gate, sum_out)
            move, distance = rest_in[number - 1]
            sum_in = move(sum_in, distance)
        if number < len(rest_gate):
            move, distance = rest_gate[number]
            sum_gate = move(sum_gate, distance)
        if number < len(rest_out):
            move, distance = rest_out[number]
            sum_out = move(sum_out, distance)
    low, high = both_halves(sum_in, steps[0])
    grad_in = jnp.concatenate([low[: full // 2], high[: full // 2]], axis=0)
    grad_conv = low[full // 2 : full // 2 + taps].astype(F32).reshape(conv_w.shape)
    return output, grad_in, sum_gate, sum_out, grad_conv


def solution(mesh):
    placed = (
        P("seq"),
        P("seq", "ch"),
        P(None, "ch"),
        P(None, "ch"),
        P(None, "ch"),
        P(None, None, "ch"),
        P(),
        P(),
        P(None, "ch"),
        P("seq", "ch"),
    )
    return jax.shard_map(
        local,
        mesh=mesh,
        in_specs=placed,
        out_specs=(
            P("seq", "ch"),
            P(None, "ch"),
            P(None, "ch"),
            P(None, "ch"),
            P(None, None, "ch"),
        ),
        check_vma=False,
    )
```

```python
import functools

import jax
import jax.numpy as jnp
from jax import lax
from jax.experimental import pallas as pl
from jax.experimental.pallas import tpu as pltpu
from jax.sharding import PartitionSpec as P

DILATIONS = (1, 8, 64)
EPSILON = 1e-06
FORE = (160, 144, 128, 0)
AFT = (80, 72, 64, 0)
BACK_FORE = (0, 8, 16, 80)
BACK_AFT = (0, 8, 24, 160)
EDGE = 160
SPARE = 64

BF16, F32 = jnp.bfloat16, jnp.float32
ROWS_DOT = (((0,), (0,)), ((), ()))
LAST_DOT = (((1,), (1,)), ((), ()))


def dot(left, right, dims=(((1,), (0,)), ((), ()))):
    return lax.dot_general(left, right, dims, preferred_element_type=F32)


def run(body, place, operands, outs, scratch=(), megabytes=8, gflop=0.1):
    moved = sum(x.size * x.dtype.itemsize for x in operands)
    return pl.pallas_call(
        body,
        out_shape=[jax.ShapeDtypeStruct(shape, dtype) for shape, dtype in outs],
        in_specs=[pl.BlockSpec(memory_space=pltpu.SMEM)]
        + [pl.BlockSpec(memory_space=pltpu.VMEM)] * len(operands),
        out_specs=[pl.BlockSpec(memory_space=pltpu.VMEM)] * len(outs),
        scratch_shapes=list(scratch),
        compiler_params=pltpu.CompilerParams(vmem_limit_bytes=megabytes << 20),
        cost_estimate=pl.CostEstimate(flops=int(gflop * 1e9), bytes_accessed=moved, transcendentals=0),
    )(place, *operands)


def part(index, size, multiple=None):
    return pl.ds(pl.multiple_of(index * size, multiple or size), size)


def anti_identity(rows):
    down = lax.broadcasted_iota(jnp.int32, (rows, rows), 0)
    across = lax.broadcasted_iota(jnp.int32, (rows, rows), 1)
    return (down + across == rows - 1).astype(F32).astype(BF16)


def input_kernel(place, tokens, hidden, embedding, block_in, padded):
    bases, rows = embedding.shape[0], hidden.shape[0]
    padded[...] = jnp.zeros_like(padded)
    padded[:bases] = embedding[...].astype(F32)
    base = lax.broadcasted_iota(jnp.int32, (padded.shape[0], rows), 0)
    one_hot = (base == tokens[...]).astype(F32).astype(BF16)
    shift = dot(one_hot, padded[...].astype(BF16), ROWS_DOT)
    block_in[...] = (hidden[...].astype(F32) + shift).astype(BF16)


def setup_kernel(place, block_in, cotangent, order, first, second, flipped, choose):
    odd = place[0] % 2
    far = block_in.shape[0] - EDGE
    first[...] = block_in[pl.ds(pl.multiple_of((1 - odd) * far, 16), EDGE), :]
    second[...] = block_in[pl.ds(pl.multiple_of(odd * far, 16), EDGE), :]
    flipped[...] = dot(anti_identity(cotangent.shape[0]), cotangent[...]).astype(BF16)
    me, width = place[1], cotangent.shape[1]
    down = lax.broadcasted_iota(jnp.int32, (width, width), 0)
    for j in range(order.shape[1] // width):
        for i in range(order.shape[1] // width):
            wanted = order[:, part(me ^ i, width)]
            choose[j * width : (j + 1) * width, i * width : (i + 1) * width] = (
                (down + (me ^ j) * width == wanted).astype(F32).astype(BF16)
            )


def project_kernel(channels, place, *refs):
    mains, (w_in, w_gate, projected, gate_pre) = refs[:channels], refs[channels:]
    me, width = place[1], mains[0].shape[1]
    for weight, out in ((w_in, projected), (w_gate, gate_pre)):
        total = dot(mains[0][...], weight[part(me, width), :])
        for j in range(1, channels):
            total += dot(mains[j][...], weight[part(me ^ j, width), :])
        out[...] = total


def keep_inside(total, place, before, rows):
    position = lax.broadcasted_iota(jnp.int32, total.shape, 0) + (place[0] * rows - before)
    return jnp.where((position >= 0) & (position < place[2] * rows), total, 0.0)


def forward_kernel(channels, place, edges, edges_core, w_in, projected, gate_pre, conv_w, *outs):
    level_0, level_1, level_2, level_3, gated = outs
    me, odd = place[1], place[0] % 2
    rows, width = projected.shape
    left = jnp.zeros((EDGE, width), F32)
    right = jnp.zeros((AFT[0], width), F32)
    for j in range(channels):
        source = edges_core if j % 2 else edges
        base = (j // 2) * 2 * EDGE
        weight = w_in[part(me ^ j, width), :]
        left += dot(source[pl.ds(pl.multiple_of(base + (1 - odd) * EDGE, 16), EDGE), :], weight)
        right += dot(source[pl.ds(pl.multiple_of(base + odd * EDGE, 16), AFT[0]), :], weight)
    level_0[:EDGE] = left
    level_0[EDGE : EDGE + rows] = projected[...]
    level_0[EDGE + rows :] = right
    source = level_0
    for number, (dilation, target) in enumerate(zip(DILATIONS, (level_1, level_2, level_3))):
        shift = FORE[number] - FORE[number + 1]
        count = target.shape[0]
        total = jnp.zeros((count, width), F32)
        for tap in range(4):
            begin = shift + (tap - 2) * dilation
            total += conv_w[number, tap : tap + 1, :] * source[begin : begin + count]
        if FORE[number + 1]:
            total = keep_inside(total, place, FORE[number + 1], rows)
        target[...] = total
        source = target
    gate = gate_pre[...]
    gated[...] = (level_3[...] * (gate / (1.0 + jnp.exp(-gate)))).astype(BF16)


def flip_kernel(place, block, flipped):
    flipped[...] = dot(anti_identity(block.shape[0]), block[...]).astype(BF16)


def norm_grad_kernel(channels, place, *refs):
    own, mirrored = refs[:channels], refs[channels : 2 * channels]
    near, near_core, far_mine, far_other, far_core_mine, far_core_other, out, far, far_core = refs[2 * channels :]
    me, side = place[1], place[0] % 2
    half = far_mine.shape[0]
    for whole, mine, other in ((far, far_mine, far_other), (far_core, far_core_mine, far_core_other)):
        whole[part(side, half), :] = mine[...]
        whole[part(1 - side, half), :] = other[...]
    weights = (near, near_core, far, far_core)
    rows, width = own[0].shape
    for block, cotangents in enumerate((own, mirrored)):
        for i in range(channels):
            total = jnp.zeros((rows, width), F32)
            for j in range(channels):
                total += dot(cotangents[j][...], weights[j][part(i ^ me, width), :], LAST_DOT)
            out[block * rows : (block + 1) * rows, i * width : (i + 1) * width] = total.astype(BF16)


def combine_kernel(channels, place, *refs):
    own, mirrored = refs[:channels], refs[channels : 2 * channels]
    grad_norm, choose, gain, gate_pre, level_3 = refs[2 * channels : 2 * channels + 5]
    normalized, upstream, grad_gate_pre, first, second, gains, grad_gated = refs[2 * channels + 5 :]
    me = place[1]
    rows, width = own[0].shape
    full = channels * width
    tile = rows // 4
    for j in range(channels):
        gains[:, j * width : (j + 1) * width] = gain[:, part(me ^ j, width)]
    for block, (here, there) in enumerate(((own, mirrored), (mirrored, own))):

        def step(k, carry, block=block, here=here, there=there):
            at = part(k, tile)
            mine = jnp.concatenate([ref[at, :].astype(F32) for ref in here], axis=1)
            other = jnp.concatenate([ref[at, :] for ref in there], axis=1)
            combined = mine + dot(other, choose[...])
            mean = jnp.sum(combined * combined, axis=1, keepdims=True) * (1.0 / full)
            inv_scale = lax.rsqrt(mean + EPSILON)
            hat = combined * inv_scale
            at_both = pl.ds(pl.multiple_of(block * rows + k * tile, tile), tile)
            normalized[at_both, :] = (hat * gains[...]).astype(BF16)
            scaled = grad_norm[at_both, :].astype(F32) * gains[...]
            row_total = jnp.sum(scaled * hat, axis=1, keepdims=True) * (1.0 / full)
            if block == 0:
                grad_gated[at, :] = inv_scale * (scaled[:, :width] - hat[:, :width] * row_total)
            else:
                grad_comb = (inv_scale * (scaled - hat * row_total)).astype(BF16)
                grad_gated[at, :] += dot(grad_comb, choose[:width, :], LAST_DOT)
            return carry

        lax.fori_loop(0, rows // tile, step, 0)
    gate = gate_pre[...]
    sigmoid = 1.0 / (1.0 + jnp.exp(-gate))
    total = grad_gated[...]
    upstream[...] = (total * (gate * sigmoid)).astype(BF16)
    grad_gate_pre[...] = (total * level_3[...] * sigmoid * (1.0 + gate * (1.0 - sigmoid))).astype(BF16)
    odd, far = place[0] % 2, rows - EDGE
    first[...] = upstream[pl.ds(pl.multiple_of((1 - odd) * far, 16), EDGE), :]
    second[...] = upstream[pl.ds(pl.multiple_of(odd * far, 16), EDGE), :]


def output_kernel(channels, place, normalized, w_out, block_in, output):
    me = place[1]
    rows, width = block_in.shape
    total = block_in[...].astype(F32)
    for j in range(channels):
        total += dot(normalized[:rows, j * width : (j + 1) * width], w_out[part(me ^ j, width), :])
    output[...] = total.astype(BF16)


def products_kernel(channels, place, normalized, cotangent, mirrored_cotangent, grad_gate_pre, *refs):
    mains = refs[:channels]
    out_sent, out_kept, gate_sent, gate_kept, whole_out, whole_gate = refs[channels:]
    me, side = place[1], place[0] % 2
    rows, width = cotangent.shape
    for j in range(channels // 2):
        block = (side * (channels // 2) + j) ^ me
        columns = part(block, width)
        whole_out[j * width : (j + 1) * width, :] = dot(
            normalized[:rows, columns], cotangent[...], ROWS_DOT
        ) + dot(normalized[rows:, columns], mirrored_cotangent[...], ROWS_DOT)
    half = whole_out.shape[0] // 2
    bit = (place[0] // 2) % 2
    out_sent[...] = whole_out[part(1 - bit, half), :].astype(BF16)
    out_kept[...] = whole_out[part(bit, half), :]
    for j in range(channels):
        whole_gate[part(me ^ j, width), :] = dot(mains[j][...], grad_gate_pre[...], ROWS_DOT)
    half = whole_gate.shape[0] // 2
    gate_sent[...] = whole_gate[part(1 - side, half), :].astype(BF16)
    gate_kept[...] = whole_gate[part(side, half), :]


def backward_kernel(channels, place, upstream, first, second, level_0, level_1, level_2, conv_w, *refs):
    mains = refs[:channels]
    sent, kept, whole, grad_3, grad_2, grad_1 = refs[channels:]
    me, odd = place[1], place[0] % 2
    rows, width = upstream.shape
    fore = BACK_FORE[3]
    even = (odd == 0).astype(F32)
    early, late = first[...].astype(F32), second[...].astype(F32)
    grad_3[:fore] = (early * (1.0 - even) + late * even)[EDGE - fore :]
    grad_3[fore : fore + rows] = upstream[...].astype(F32)
    grad_3[fore + rows :] = early * even + late * (1.0 - even)
    half = whole.shape[0] // 2
    for top in (half - SPARE, 2 * half - SPARE):
        whole[top : top + SPARE, :] = jnp.zeros((SPARE, width), F32)
    levels = (level_0, level_1, level_2)
    grads = (None, grad_1, grad_2, grad_3)
    grad_0 = None
    for number in (2, 1, 0):
        dilation, source, level = DILATIONS[number], grads[number + 1], levels[number]
        fore = BACK_FORE[number + 1]
        here = source[fore : fore + rows]
        for tap in range(4):
            begin = FORE[number] + (tap - 2) * dilation
            row = half - SPARE + 4 * number + tap
            whole[row : row + 1, :] = jnp.sum(here * level[begin : begin + rows], axis=0, keepdims=True)
        count = BACK_FORE[number] + rows + BACK_AFT[number]
        total = jnp.zeros((count, width), F32)
        for tap in range(4):
            begin = fore - BACK_FORE[number] - (tap - 2) * dilation
            total += conv_w[number, tap : tap + 1, :] * source[begin : begin + count]
        if number:
            grads[number][...] = keep_inside(total, place, BACK_FORE[number], rows)
        else:
            grad_0 = total.astype(BF16)
    for j in range(channels):
        block = me ^ j
        start = (block // (channels // 2)) * half + (block % (channels // 2)) * width
        whole[pl.ds(pl.multiple_of(start, SPARE), width), :] = dot(mains[j][...], grad_0, ROWS_DOT)
    sent[...] = whole[part(1 - odd, half), :].astype(BF16)
    kept[...] = whole[part(odd, half), :]


def exchange(block, axis, distance):
    count = lax.axis_size(axis)
    return lax.ppermute(block, axis, [(i, i ^ distance) for i in range(count)])


def distances(axis):
    return [1 << bit for bit in range(lax.axis_size(axis).bit_length() - 1)]


def mirror(block):
    count = lax.axis_size("seq")
    return lax.ppermute(block, "seq", [(i, count - 1 - i) for i in range(count)])


def swap_edges(first, second, far=0):
    count, channels = lax.axis_size("seq"), lax.axis_size("ch")
    received = []
    for turn, block in enumerate((first, second)):
        route = []
        for low in range(turn, count - 1, 2):
            for c in range(channels):
                route.append((low * channels + c, (low + 1) * channels + (c ^ far)))
                route.append(((low + 1) * channels + c, low * channels + (c ^ far)))
        received.append(lax.ppermute(block, ("seq", "ch"), route))
    return received


def together(*values):
    return lax.optimization_barrier(values)


def seq_bit(distance):
    return (lax.axis_index("seq") & distance) // distance


def halve(total, distance):
    half = total.shape[0] // 2
    bit = seq_bit(distance)
    sent = lax.dynamic_slice_in_dim(total, (1 - bit) * half, half, 0).astype(BF16)
    kept = lax.dynamic_slice_in_dim(total, bit * half, half, 0)
    return kept.astype(F32) + exchange(sent, "seq", distance).astype(F32)


def double(total, distance):
    return jnp.concatenate(both_halves(total, distance), axis=0)


def both_halves(total, distance):
    total = total.astype(BF16)
    other = exchange(total, "seq", distance)
    first = seq_bit(distance) == 0
    return jnp.where(first, total, other), jnp.where(first, other, total)


def local(tokens, hidden, embedding, w_in, w_gate, conv_w, channel_order, gain, w_out, cotangent):
    rows, width = hidden.shape
    full = gain.shape[0]
    channels = full // width
    cross = channels // 2
    taps = conv_w.shape[0] * conv_w.shape[1]
    steps = distances("seq")
    block = ((rows, width), BF16)
    place = jnp.stack([lax.axis_index("seq"), lax.axis_index("ch"), lax.axis_size("seq")]).astype(jnp.int32)

    local_input = run(
        input_kernel,
        place,
        (tokens.reshape(1, rows), hidden, embedding),
        [block],
        [pltpu.VMEM((16, width), F32)],
    )[0]
    input_x = exchange(local_input, "ch", cross)
    input_core = exchange(local_input, "ch", 1)
    first, second, flipped_cotangent, choose = run(
        setup_kernel,
        place,
        (local_input, cotangent, channel_order.reshape(1, full)),
        [((EDGE, width), BF16), ((EDGE, width), BF16), block, ((full, full), BF16)],
    )
    near = swap_edges(first, second)
    far = swap_edges(first, second, cross)
    flipped_cotangent, *near = together(flipped_cotangent, *near)
    mirrored_cotangent = mirror(flipped_cotangent)
    w_half = lax.dynamic_slice_in_dim(w_out, seq_bit(1) * (full // 2), full // 2, 0)
    w_half, early_cotangent, input_x = together(w_half, cotangent, input_x)
    w_x_mine = exchange(w_half, "ch", cross)
    mains = [local_input, input_core, input_x, exchange(input_x, "ch", 1)]
    edges = jnp.concatenate(near + far, axis=0)
    edges_core = exchange(edges, "ch", 1)
    cotangent_x = exchange(early_cotangent, "ch", cross)
    w_x_other = exchange(w_x_mine, "seq", 1)
    late_cotangent, cotangent_x = together(mirrored_cotangent, cotangent_x)
    mirrored_cotangent_x = exchange(late_cotangent, "ch", cross)

    projected, gate_pre = run(
        functools.partial(project_kernel, channels),
        place,
        (*mains, w_in, w_gate),
        [((rows, width), F32)] * 2,
        gflop=6.0,
    )
    level_0, level_1, level_2, level_3, gated = run(
        functools.partial(forward_kernel, channels),
        place,
        (edges, edges_core, w_in, projected, gate_pre, conv_w),
        [((fore + rows + aft, width), F32) for fore, aft in zip(FORE, AFT)] + [block],
        gflop=0.4,
    )
    mirrored, w_x_other = together(mirror(gated), w_x_other)
    mirrored = run(flip_kernel, place, (mirrored,), [block], gflop=12.0)[0]
    late_gated, mirrored_cotangent = together(gated, mirrored_cotangent)
    gated_x = exchange(late_gated, "ch", cross)
    mirrored, mirrored_cotangent_x, gated_x = together(mirrored, mirrored_cotangent_x, gated_x)
    mirrored_x = exchange(mirrored, "ch", cross)
    gated_all = [gated, exchange(gated, "ch", 1), gated_x, exchange(gated_x, "ch", 1)]
    cotangent_all = [cotangent, exchange(cotangent, "ch", 1), cotangent_x, exchange(cotangent_x, "ch", 1)]
    mirrored_cotangent_all = [
        mirrored_cotangent,
        exchange(mirrored_cotangent, "ch", 1),
        mirrored_cotangent_x,
        exchange(mirrored_cotangent_x, "ch", 1),
    ]
    grad_norm = run(
        functools.partial(norm_grad_kernel, channels),
        place,
        (
            *cotangent_all,
            *mirrored_cotangent_all,
            w_out,
            exchange(w_out, "ch", 1),
            w_x_mine,
            w_x_other,
            exchange(w_x_mine, "ch", 1),
            exchange(w_x_other, "ch", 1),
        ),
        [((2 * rows, full), BF16)],
        [pltpu.VMEM((full, width), BF16)] * 2,
        gflop=6.0,
    )[0]
    mirrored_x, grad_norm = together(mirrored_x, grad_norm)
    mirrored_all = [mirrored, exchange(mirrored, "ch", 1), mirrored_x, exchange(mirrored_x, "ch", 1)]

    normalized, upstream, grad_gate_pre, first, second = run(
        functools.partial(combine_kernel, channels),
        place,
        (*gated_all, *mirrored_all, grad_norm, choose, gain.reshape(1, full), gate_pre, level_3),
        [((2 * rows, full), BF16), block, block, ((EDGE, width), BF16), ((EDGE, width), BF16)],
        [pltpu.VMEM((1, full), F32), pltpu.VMEM((rows, width), F32)],
        gflop=2.5,
    )
    first, second = swap_edges(first, second)
    out_sent, out_kept, gate_sent, gate_kept = run(
        functools.partial(products_kernel, channels),
        place,
        (normalized, cotangent, mirrored_cotangent, grad_gate_pre, *mains),
        [
            ((full // 4, width), BF16),
            ((full // 4, width), F32),
            ((full // 2, width), BF16),
            ((full // 2, width), F32),
        ],
        [pltpu.VMEM((full // 2, width), F32), pltpu.VMEM((full, width), F32)],
        gflop=0.8,
    )
    out_sent, gate_sent, first, second = together(out_sent, gate_sent, first, second)
    out_other = exchange(out_sent, "seq", steps[1])
    gate_other = exchange(gate_sent, "seq", steps[0])
    half = full // 2 + SPARE
    in_sent, in_kept = run(
        functools.partial(backward_kernel, channels),
        place,
        (upstream, first, second, level_0, level_1, level_2, conv_w, *mains),
        [((half, width), BF16), ((half, width), F32)],
        [pltpu.VMEM((2 * half, width), F32)]
        + [pltpu.VMEM((BACK_FORE[k] + rows + BACK_AFT[k], width), F32) for k in (3, 2, 1)],
        gflop=0.5,
    )
    output = run(
        functools.partial(output_kernel, channels),
        place,
        (normalized, w_out, local_input),
        [block],
        gflop=0.3,
    )[0]

    sum_out = out_kept + out_other.astype(F32)
    sum_gate = gate_kept + gate_other.astype(F32)
    in_sent, sum_gate, sum_out = together(in_sent, sum_gate, sum_out)
    sum_in = in_kept + exchange(in_sent, "seq", steps[0]).astype(F32)
    undo = [(double, distance) for distance in steps[::-1]]
    rest_gate = [(halve, distance) for distance in steps[1:]] + undo
    rest_out = [(halve, distance) for distance in steps[2:]] + undo
    rest_in = [(halve, distance) for distance in steps[1:]] + undo[:-1]
    for number in range(len(rest_in) + 1):
        if number:
            sum_in, sum_gate, sum_out = together(sum_in, sum_gate, sum_out)
            move, distance = rest_in[number - 1]
            sum_in = move(sum_in, distance)
        if number < len(rest_gate):
            move, distance = rest_gate[number]
            sum_gate = move(sum_gate, distance)
        if number < len(rest_out):
            move, distance = rest_out[number]
            sum_out = move(sum_out, distance)
    low, high = both_halves(sum_in, steps[0])
    grad_in = jnp.concatenate([low[: full // 2], high[: full // 2]], axis=0)
    grad_conv = low[full // 2 : full // 2 + taps].astype(F32).reshape(conv_w.shape)
    return output, grad_in, sum_gate, sum_out, grad_conv


def solution(mesh):
    placed = (
        P("seq"),
        P("seq", "ch"),
        P(None, "ch"),
        P(None, "ch"),
        P(None, "ch"),
        P(None, None, "ch"),
        P(),
        P(),
        P(None, "ch"),
        P("seq", "ch"),
    )
    return jax.shard_map(
        local,
        mesh=mesh,
        in_specs=placed,
        out_specs=(
            P("seq", "ch"),
            P(None, "ch"),
            P(None, "ch"),
            P(None, "ch"),
            P(None, None, "ch"),
        ),
        check_vma=False,
    )
```

```python
import functools

import jax
import jax.numpy as jnp
from jax import lax
from jax.experimental import pallas as pl
from jax.experimental.pallas import tpu as pltpu
from jax.sharding import PartitionSpec as P

DILATIONS = (1, 8, 64)
EPSILON = 1e-06
FORE = (160, 144, 128, 0)
AFT = (80, 72, 64, 0)
BACK_FORE = (0, 8, 16, 80)
BACK_AFT = (0, 8, 24, 160)
EDGE = 160
SPARE = 64

BF16, F32 = jnp.bfloat16, jnp.float32
ROWS_DOT = (((0,), (0,)), ((), ()))
LAST_DOT = (((1,), (1,)), ((), ()))


def dot(left, right, dims=(((1,), (0,)), ((), ()))):
    return lax.dot_general(left, right, dims, preferred_element_type=F32)


def run(body, place, operands, outs, scratch=(), megabytes=8, gflop=0.1, fetched=0):
    moved = sum(x.size * x.dtype.itemsize for x in operands)
    return pl.pallas_call(
        body,
        out_shape=[jax.ShapeDtypeStruct(shape, dtype) for shape, dtype in outs],
        in_specs=[pl.BlockSpec(memory_space=pltpu.SMEM)]
        + [pl.BlockSpec(memory_space=pltpu.VMEM)] * (len(operands) - fetched)
        + [pl.BlockSpec(memory_space=pltpu.HBM)] * fetched,
        out_specs=[pl.BlockSpec(memory_space=pltpu.VMEM)] * len(outs),
        scratch_shapes=list(scratch),
        compiler_params=pltpu.CompilerParams(vmem_limit_bytes=megabytes << 20),
        cost_estimate=pl.CostEstimate(flops=int(gflop * 1e9), bytes_accessed=moved, transcendentals=0),
    )(place, *operands)


def fetch(sources, targets, semaphores):
    copies = [
        pltpu.make_async_copy(source, target, semaphores.at[k])
        for k, (source, target) in enumerate(zip(sources, targets))
    ]
    for copy in copies:
        copy.start()
    return copies


def fetch_scratch(operands):
    return [pltpu.VMEM(x.shape, x.dtype) for x in operands] + [pltpu.SemaphoreType.DMA((len(operands),))]


def part(index, size, multiple=None):
    return pl.ds(pl.multiple_of(index * size, multiple or size), size)


def saved_rows(rows, number):
    return -(-(FORE[number] + rows + AFT[number]) // 16) * 16


def anti_identity(rows):
    down = lax.broadcasted_iota(jnp.int32, (rows, rows), 0)
    across = lax.broadcasted_iota(jnp.int32, (rows, rows), 1)
    return (down + across == rows - 1).astype(F32).astype(BF16)


def input_kernel(place, tokens_hbm, hidden_hbm, embedding_hbm, block_in, padded, tokens, hidden, embedding, semaphores):
    copies = fetch((tokens_hbm, hidden_hbm, embedding_hbm), (tokens, hidden, embedding), semaphores)
    bases, rows = embedding.shape[0], hidden.shape[0]
    padded[...] = jnp.zeros_like(padded)
    for copy in copies:
        copy.wait()
    padded[:bases] = embedding[...].astype(F32)
    base = lax.broadcasted_iota(jnp.int32, (padded.shape[0], rows), 0)
    one_hot = (base == tokens[...]).astype(F32).astype(BF16)
    shift = dot(one_hot, padded[...].astype(BF16), ROWS_DOT)
    block_in[...] = (hidden[...].astype(F32) + shift).astype(BF16)


def setup_kernel(place, block_in, order, first, second, choose):
    odd = place[0] % 2
    far = block_in.shape[0] - EDGE
    first[...] = block_in[pl.ds(pl.multiple_of((1 - odd) * far, 16), EDGE), :]
    second[...] = block_in[pl.ds(pl.multiple_of(odd * far, 16), EDGE), :]
    me, width = place[1], block_in.shape[1]
    down = lax.broadcasted_iota(jnp.int32, (width, width), 0)
    for j in range(order.shape[1] // width):
        for i in range(order.shape[1] // width):
            wanted = order[:, part(me ^ i, width)]
            choose[j * width : (j + 1) * width, i * width : (i + 1) * width] = (
                (down + (me ^ j) * width == wanted).astype(F32).astype(BF16)
            )


def project_kernel(channels, place, *refs):
    mains, (w_in, w_gate, projected, gate_pre, w_in_on) = refs[:channels], refs[channels:]
    me, width = place[1], mains[0].shape[1]
    for weight, out in ((w_in, projected), (w_gate, gate_pre)):
        total = dot(mains[0][...], weight[part(me, width), :])
        for j in range(1, channels):
            total += dot(mains[j][...], weight[part(me ^ j, width), :])
        out[...] = total
    w_in_on[...] = w_in[...]


def keep_inside(total, place, before, rows):
    position = lax.broadcasted_iota(jnp.int32, total.shape, 0) + (place[0] * rows - before)
    return jnp.where((position >= 0) & (position < place[2] * rows), total, 0.0)


def forward_kernel(channels, place, edges, edges_core, w_in, projected, gate_pre, conv_w, *outs):
    levels, level_3, gated, *stages = outs
    me, odd = place[1], place[0] % 2
    rows, width = projected.shape
    left = jnp.zeros((EDGE, width), F32)
    right = jnp.zeros((AFT[0], width), F32)
    for j in range(channels):
        source = edges_core if j % 2 else edges
        base = (j // 2) * 2 * EDGE
        weight = w_in[part(me ^ j, width), :]
        left += dot(source[pl.ds(pl.multiple_of(base + (1 - odd) * EDGE, 16), EDGE), :], weight)
        right += dot(source[pl.ds(pl.multiple_of(base + odd * EDGE, 16), AFT[0]), :], weight)
    source = stages[0]
    source[:EDGE] = left
    source[EDGE : EDGE + rows] = projected[...]
    source[EDGE + rows :] = right
    top = 0
    for number, dilation in enumerate(DILATIONS):
        target = stages[number + 1]
        levels[top : top + source.shape[0], :] = source[...].astype(BF16)
        top += source.shape[0]
        shift = FORE[number] - FORE[number + 1]
        count = FORE[number + 1] + rows + AFT[number + 1]
        total = jnp.zeros((count, width), F32)
        for tap in range(4):
            begin = shift + (tap - 2) * dilation
            total += conv_w[number, tap : tap + 1, :] * source[begin : begin + count]
        if FORE[number + 1]:
            total = keep_inside(total, place, FORE[number + 1], rows)
        target[:count] = total
        if count < target.shape[0]:
            target[count:] = jnp.zeros((target.shape[0] - count, width), F32)
        source = target
    gate = gate_pre[...]
    level_3[...] = source[...].astype(BF16)
    gated[...] = (source[...] * (gate / (1.0 + jnp.exp(-gate)))).astype(BF16)


def flip_kernel(place, block, flipped):
    flipped[...] = dot(anti_identity(block.shape[0]), block[...]).astype(BF16)


def norm_grad_kernel(channels, place, *refs):
    own, mirrored = refs[:channels], refs[channels : 2 * channels]
    *weights, out = refs[2 * channels :]
    me = place[1]
    rows, width = own[0].shape
    for block, cotangents in enumerate((own, mirrored)):
        for i in range(channels):
            total = jnp.zeros((rows, width), F32)
            for j in range(channels):
                total += dot(cotangents[j][...], weights[j][part(i ^ me, width), :], LAST_DOT)
            out[block * rows : (block + 1) * rows, i * width : (i + 1) * width] = total.astype(BF16)


def combine_kernel(channels, place, *refs):
    own, mirrored = refs[:channels], refs[channels : 2 * channels]
    grad_norm, choose, gain, gate_pre, level_3 = refs[2 * channels : 2 * channels + 5]
    normalized, upstream, grad_gate_pre, first, second, gains, grad_gated = refs[2 * channels + 5 :]
    me = place[1]
    rows, width = own[0].shape
    full = channels * width
    tile = rows // 4
    for j in range(channels):
        gains[:, j * width : (j + 1) * width] = gain[:, part(me ^ j, width)]
    for block, (here, there) in enumerate(((own, mirrored), (mirrored, own))):

        def step(k, carry, block=block, here=here, there=there):
            at = part(k, tile)
            mine = jnp.concatenate([ref[at, :].astype(F32) for ref in here], axis=1)
            other = jnp.concatenate([ref[at, :] for ref in there], axis=1)
            combined = mine + dot(other, choose[...])
            mean = jnp.sum(combined * combined, axis=1, keepdims=True) * (1.0 / full)
            inv_scale = lax.rsqrt(mean + EPSILON)
            hat = combined * inv_scale
            at_both = pl.ds(pl.multiple_of(block * rows + k * tile, tile), tile)
            normalized[at_both, :] = (hat * gains[...]).astype(BF16)
            scaled = grad_norm[at_both, :].astype(F32) * gains[...]
            row_total = jnp.sum(scaled * hat, axis=1, keepdims=True) * (1.0 / full)
            if block == 0:
                grad_gated[at, :] = inv_scale * (scaled[:, :width] - hat[:, :width] * row_total)
            else:
                grad_comb = (inv_scale * (scaled - hat * row_total)).astype(BF16)
                grad_gated[at, :] += dot(grad_comb, choose[:width, :], LAST_DOT)
            return carry

        lax.fori_loop(0, rows // tile, step, 0, unroll=True)
    gate = gate_pre[...]
    sigmoid = 1.0 / (1.0 + jnp.exp(-gate))
    total = grad_gated[...]
    upstream[...] = (total * (gate * sigmoid)).astype(BF16)
    grad_gate_pre[...] = (total * level_3[...].astype(F32) * sigmoid * (1.0 + gate * (1.0 - sigmoid))).astype(BF16)
    odd, far = place[0] % 2, rows - EDGE
    first[...] = upstream[pl.ds(pl.multiple_of((1 - odd) * far, 16), EDGE), :]
    second[...] = upstream[pl.ds(pl.multiple_of(odd * far, 16), EDGE), :]


def output_kernel(channels, place, normalized, w_out, block_in, output):
    me = place[1]
    rows, width = block_in.shape
    total = block_in[...].astype(F32)
    for j in range(channels):
        total += dot(normalized[:rows, j * width : (j + 1) * width], w_out[part(me ^ j, width), :])
    output[...] = total.astype(BF16)


def products_kernel(channels, place, normalized, cotangent, mirrored_cotangent, grad_gate_pre, *refs):
    mains = refs[:channels]
    out_sent, out_kept, gate_sent, gate_kept, whole_out, whole_gate = refs[channels:]
    me, side = place[1], place[0] % 2
    rows, width = cotangent.shape
    for j in range(channels // 2):
        block = (side * (channels // 2) + j) ^ me
        columns = part(block, width)
        whole_out[j * width : (j + 1) * width, :] = dot(
            normalized[:rows, columns], cotangent[...], ROWS_DOT
        ) + dot(normalized[rows:, columns], mirrored_cotangent[...], ROWS_DOT)
    half = whole_out.shape[0] // 2
    bit = (place[0] // 2) % 2
    out_sent[...] = whole_out[part(1 - bit, half), :].astype(BF16)
    out_kept[...] = whole_out[part(bit, half), :]
    for j in range(channels):
        whole_gate[part(me ^ j, width), :] = dot(mains[j][...], grad_gate_pre[...], ROWS_DOT)
    half = whole_gate.shape[0] // 2
    gate_sent[...] = whole_gate[part(1 - side, half), :].astype(BF16)
    gate_kept[...] = whole_gate[part(side, half), :]


def backward_kernel(channels, place, upstream, first, second, conv_w, *refs):
    mains, (saved, sent, kept, whole, grad_3, grad_2, grad_1, levels) = refs[:channels], refs[channels:]
    levels[...] = saved[...].astype(F32)
    me, odd = place[1], place[0] % 2
    rows, width = upstream.shape
    fore = BACK_FORE[3]
    even = (odd == 0).astype(F32)
    early, late = first[...].astype(F32), second[...].astype(F32)
    grad_3[:fore] = (early * (1.0 - even) + late * even)[EDGE - fore :]
    grad_3[fore : fore + rows] = upstream[...].astype(F32)
    grad_3[fore + rows :] = early * even + late * (1.0 - even)
    half = whole.shape[0] // 2
    for top in (half - SPARE, 2 * half - SPARE):
        whole[top : top + SPARE, :] = jnp.zeros((SPARE, width), F32)
    grads = (None, grad_1, grad_2, grad_3)
    grad_0 = None
    for number in (2, 1, 0):
        dilation, source = DILATIONS[number], grads[number + 1]
        top = sum(saved_rows(rows, below) for below in range(number))
        fore = BACK_FORE[number + 1]
        here = source[fore : fore + rows]
        for tap in range(4):
            begin = top + FORE[number] + (tap - 2) * dilation
            row = half - SPARE + 4 * number + tap
            whole[row : row + 1, :] = jnp.sum(here * levels[begin : begin + rows], axis=0, keepdims=True)
        count = BACK_FORE[number] + rows + BACK_AFT[number]
        total = jnp.zeros((count, width), F32)
        for tap in range(4):
            begin = fore - BACK_FORE[number] - (tap - 2) * dilation
            total += conv_w[number, tap : tap + 1, :] * source[begin : begin + count]
        if number:
            grads[number][...] = keep_inside(total, place, BACK_FORE[number], rows)
        else:
            grad_0 = total.astype(BF16)
    for j in range(channels):
        block = me ^ j
        start = (block // (channels // 2)) * half + (block % (channels // 2)) * width
        whole[pl.ds(pl.multiple_of(start, SPARE), width), :] = dot(mains[j][...], grad_0, ROWS_DOT)
    sent[...] = whole[part(1 - odd, half), :].astype(BF16)
    kept[...] = whole[part(odd, half), :]


def exchange(block, axis, distance):
    count = lax.axis_size(axis)
    return lax.ppermute(block, axis, [(i, i ^ distance) for i in range(count)])


def distances(axis):
    return [1 << bit for bit in range(lax.axis_size(axis).bit_length() - 1)]


def mirror(block):
    count = lax.axis_size("seq")
    return lax.ppermute(block, "seq", [(i, count - 1 - i) for i in range(count)])


def swap_edges(first, second, far=0):
    count, channels = lax.axis_size("seq"), lax.axis_size("ch")
    received = []
    for turn, block in enumerate((first, second)):
        route = []
        for low in range(turn, count - 1, 2):
            for c in range(channels):
                route.append((low * channels + c, (low + 1) * channels + (c ^ far)))
                route.append(((low + 1) * channels + c, low * channels + (c ^ far)))
        received.append(lax.ppermute(block, ("seq", "ch"), route))
    return received


def together(*values):
    return lax.optimization_barrier(values)


def seq_bit(distance):
    return (lax.axis_index("seq") & distance) // distance


def halve(total, distance):
    half = total.shape[0] // 2
    bit = seq_bit(distance)
    sent = lax.dynamic_slice_in_dim(total, (1 - bit) * half, half, 0).astype(BF16)
    kept = lax.dynamic_slice_in_dim(total, bit * half, half, 0)
    return kept.astype(F32) + exchange(sent, "seq", distance).astype(F32)


def double(total, distance):
    return jnp.concatenate(both_halves(total, distance), axis=0)


def both_halves(total, distance):
    total = total.astype(BF16)
    other = exchange(total, "seq", distance)
    first = seq_bit(distance) == 0
    return jnp.where(first, total, other), jnp.where(first, other, total)


def local(tokens, hidden, embedding, w_in, w_gate, conv_w, channel_order, gain, w_out, cotangent):
    rows, width = hidden.shape
    full = gain.shape[0]
    channels = full // width
    cross = channels // 2
    taps = conv_w.shape[0] * conv_w.shape[1]
    steps = distances("seq")
    block = ((rows, width), BF16)
    place = jnp.stack([lax.axis_index("seq"), lax.axis_index("ch"), lax.axis_size("seq")]).astype(jnp.int32)

    cotangent_x = exchange(cotangent, "ch", cross)
    mirrored_cotangent = mirror(cotangent)
    inputs = (tokens.reshape(1, rows), hidden, embedding)
    local_input = run(
        input_kernel, place, inputs, [block], [pltpu.VMEM((16, width), F32), *fetch_scratch(inputs)], 60, fetched=3
    )[0]
    input_x = exchange(local_input, "ch", cross)
    input_core = exchange(local_input, "ch", 1)
    first, second, choose = run(
        setup_kernel,
        place,
        (local_input, channel_order.reshape(1, full)),
        [((EDGE, width), BF16), ((EDGE, width), BF16), ((full, full), BF16)],
    )
    first, second, mirrored_cotangent, cotangent_x = together(first, second, mirrored_cotangent, cotangent_x)
    edges = jnp.concatenate(swap_edges(first, second) + swap_edges(first, second, cross), axis=0)
    edges_core = exchange(edges, "ch", 1)
    early_w_out, input_x = together(w_out, input_x)
    w_out_x = exchange(early_w_out, "ch", cross)
    mains = [local_input, input_core, input_x, exchange(input_x, "ch", 1)]
    mirrored_cotangent = run(flip_kernel, place, (mirrored_cotangent,), [block], gflop=1.0)[0]
    mirrored_cotangent, mains[3] = together(mirrored_cotangent, mains[3])
    mirrored_cotangent, w_out_x = together(mirrored_cotangent, w_out_x)
    mirrored_cotangent_x = exchange(mirrored_cotangent, "ch", cross)

    projected, gate_pre, w_in_on = run(
        functools.partial(project_kernel, channels),
        place,
        (*mains, w_in, w_gate),
        [((rows, width), F32)] * 2 + [(w_in.shape, BF16)],
        gflop=6.0,
    )
    levels, level_3, gated = run(
        functools.partial(forward_kernel, channels),
        place,
        (edges, edges_core, w_in_on, projected, gate_pre, conv_w),
        [((sum(saved_rows(rows, number) for number in range(3)), width), BF16), block, block],
        [pltpu.VMEM((saved_rows(rows, number), width), F32) for number in range(4)],
        gflop=0.4,
    )
    mirrored = run(flip_kernel, place, (mirror(gated),), [block], gflop=12.0)[0]
    gated_x = exchange(gated, "ch", cross)
    mirrored, mirrored_cotangent_x, gated_x = together(mirrored, mirrored_cotangent_x, gated_x)
    mirrored_x = exchange(mirrored, "ch", cross)
    gated_all = [gated, exchange(gated, "ch", 1), gated_x, exchange(gated_x, "ch", 1)]
    cotangent_all = [cotangent, exchange(cotangent, "ch", 1), cotangent_x, exchange(cotangent_x, "ch", 1)]
    mirrored_cotangent_all = [
        mirrored_cotangent,
        exchange(mirrored_cotangent, "ch", 1),
        mirrored_cotangent_x,
        exchange(mirrored_cotangent_x, "ch", 1),
    ]
    grad_norm = run(
        functools.partial(norm_grad_kernel, channels),
        place,
        (
            *cotangent_all,
            *mirrored_cotangent_all,
            w_out,
            exchange(w_out, "ch", 1),
            w_out_x,
            exchange(w_out_x, "ch", 1),
        ),
        [((2 * rows, full), BF16)],
        gflop=6.0,
    )[0]
    mirrored_x, grad_norm = together(mirrored_x, grad_norm)
    mirrored_all = [mirrored, exchange(mirrored, "ch", 1), mirrored_x, exchange(mirrored_x, "ch", 1)]

    normalized, upstream, grad_gate_pre, first, second = run(
        functools.partial(combine_kernel, channels),
        place,
        (*gated_all, *mirrored_all, grad_norm, choose, gain.reshape(1, full), gate_pre, level_3),
        [((2 * rows, full), BF16), block, block, ((EDGE, width), BF16), ((EDGE, width), BF16)],
        [pltpu.VMEM((1, full), F32), pltpu.VMEM((rows, width), F32)],
        gflop=2.5,
    )
    first, second = swap_edges(first, second)
    out_sent, out_kept, gate_sent, gate_kept = run(
        functools.partial(products_kernel, channels),
        place,
        (normalized, cotangent, mirrored_cotangent, grad_gate_pre, *mains),
        [
            ((full // 4, width), BF16),
            ((full // 4, width), F32),
            ((full // 2, width), BF16),
            ((full // 2, width), F32),
        ],
        [pltpu.VMEM((full // 2, width), F32), pltpu.VMEM((full, width), F32)],
        gflop=0.8,
    )
    out_sent, gate_sent, first, second = together(out_sent, gate_sent, first, second)
    out_other = exchange(out_sent, "seq", steps[1])
    gate_other = exchange(gate_sent, "seq", steps[0])
    half = full // 2 + SPARE
    in_sent, in_kept = run(
        functools.partial(backward_kernel, channels),
        place,
        (upstream, first, second, conv_w, *mains, levels),
        [((half, width), BF16), ((half, width), F32)],
        [pltpu.VMEM((2 * half, width), F32)]
        + [pltpu.VMEM((BACK_FORE[k] + rows + BACK_AFT[k], width), F32) for k in (3, 2, 1)]
        + [pltpu.VMEM(levels.shape, F32)],
        gflop=0.5,
    )
    output = run(
        functools.partial(output_kernel, channels),
        place,
        (normalized, w_out, local_input),
        [block],
        gflop=0.3,
    )[0]

    sum_out = out_kept + out_other.astype(F32)
    sum_gate = gate_kept + gate_other.astype(F32)
    in_sent, sum_gate, sum_out = together(in_sent, sum_gate, sum_out)
    sum_in = in_kept + exchange(in_sent, "seq", steps[0]).astype(F32)
    undo = [(double, distance) for distance in steps[::-1]]
    rest_gate = [(halve, distance) for distance in steps[1:]] + undo
    rest_out = [(halve, distance) for distance in steps[2:]] + undo
    rest_in = [(halve, distance) for distance in steps[1:]] + undo[:-1]
    for number in range(len(rest_in) + 1):
        if number:
            sum_in, sum_gate, sum_out = together(sum_in, sum_gate, sum_out)
            move, distance = rest_in[number - 1]
            sum_in = move(sum_in, distance)
        if number < len(rest_gate):
            move, distance = rest_gate[number]
            sum_gate = move(sum_gate, distance)
        if number < len(rest_out):
            move, distance = rest_out[number]
            sum_out = move(sum_out, distance)
    low, high = both_halves(sum_in, steps[0])
    grad_in = jnp.concatenate([low[: full // 2], high[: full // 2]], axis=0)
    grad_conv = low[full // 2 : full // 2 + taps].astype(F32).reshape(conv_w.shape)
    return output, grad_in, sum_gate, sum_out, grad_conv


def solution(mesh):
    placed = (
        P("seq"),
        P("seq", "ch"),
        P(None, "ch"),
        P(None, "ch"),
        P(None, "ch"),
        P(None, None, "ch"),
        P(),
        P(),
        P(None, "ch"),
        P("seq", "ch"),
    )
    return jax.shard_map(
        local,
        mesh=mesh,
        in_specs=placed,
        out_specs=(
            P("seq", "ch"),
            P(None, "ch"),
            P(None, "ch"),
            P(None, "ch"),
            P(None, None, "ch"),
        ),
        check_vma=False,
    )
```

```python
import functools

import jax
import jax.numpy as jnp
from jax import lax
from jax.experimental import pallas as pl
from jax.experimental.pallas import tpu as pltpu
from jax.sharding import PartitionSpec as P

DILATIONS = (1, 8, 64)
EPSILON = 1e-06
FORE = (160, 144, 128, 0)
AFT = (80, 72, 64, 0)
BACK_FORE = (0, 8, 16, 80)
BACK_AFT = (0, 8, 24, 160)
EDGE = 160
SPARE = 64

BF16, F32 = jnp.bfloat16, jnp.float32
ROWS_DOT = (((0,), (0,)), ((), ()))
LAST_DOT = (((1,), (1,)), ((), ()))


def dot(left, right, dims=(((1,), (0,)), ((), ()))):
    return lax.dot_general(left, right, dims, preferred_element_type=F32)


def run(body, place, operands, outs, scratch=(), megabytes=8, gflop=0.1, fetched=0):
    moved = sum(x.size * x.dtype.itemsize for x in operands)
    return pl.pallas_call(
        body,
        out_shape=[jax.ShapeDtypeStruct(shape, dtype) for shape, dtype in outs],
        in_specs=[pl.BlockSpec(memory_space=pltpu.SMEM)]
        + [pl.BlockSpec(memory_space=pltpu.VMEM)] * (len(operands) - fetched)
        + [pl.BlockSpec(memory_space=pltpu.HBM)] * fetched,
        out_specs=[pl.BlockSpec(memory_space=pltpu.VMEM)] * len(outs),
        scratch_shapes=list(scratch),
        compiler_params=pltpu.CompilerParams(vmem_limit_bytes=megabytes << 20),
        cost_estimate=pl.CostEstimate(flops=int(gflop * 1e9), bytes_accessed=moved, transcendentals=0),
    )(place, *operands)


def fetch(sources, targets, semaphores):
    copies = [
        pltpu.make_async_copy(source, target, semaphores.at[k])
        for k, (source, target) in enumerate(zip(sources, targets))
    ]
    for copy in copies:
        copy.start()
    return copies


def fetch_scratch(operands):
    return [pltpu.VMEM(x.shape, x.dtype) for x in operands] + [pltpu.SemaphoreType.DMA((len(operands),))]


def part(index, size, multiple=None):
    return pl.ds(pl.multiple_of(index * size, multiple or size), size)


def saved_rows(rows, number):
    return -(-(FORE[number] + rows + AFT[number]) // 16) * 16


def anti_identity(rows):
    down = lax.broadcasted_iota(jnp.int32, (rows, rows), 0)
    across = lax.broadcasted_iota(jnp.int32, (rows, rows), 1)
    return (down + across == rows - 1).astype(F32).astype(BF16)


def input_kernel(place, tokens_hbm, hidden_hbm, embedding_hbm, block_in, first, second, *scratch):
    padded, tokens, hidden, embedding, semaphores = scratch
    copies = fetch((tokens_hbm, hidden_hbm, embedding_hbm), (tokens, hidden, embedding), semaphores)
    bases, rows = embedding.shape[0], hidden.shape[0]
    padded[...] = jnp.zeros_like(padded)
    for copy in copies:
        copy.wait()
    padded[:bases] = embedding[...].astype(F32)
    base = lax.broadcasted_iota(jnp.int32, (padded.shape[0], rows), 0)
    one_hot = (base == tokens[...]).astype(F32).astype(BF16)
    shift = dot(one_hot, padded[...].astype(BF16), ROWS_DOT)
    block_in[...] = (hidden[...].astype(F32) + shift).astype(BF16)
    odd, far = place[0] % 2, rows - EDGE
    first[...] = block_in[pl.ds(pl.multiple_of((1 - odd) * far, 16), EDGE), :]
    second[...] = block_in[pl.ds(pl.multiple_of(odd * far, 16), EDGE), :]


def project_kernel(channels, place, *refs):
    mains, (w_in, w_gate, projected, gate_pre, w_in_on) = refs[:channels], refs[channels:]
    me, width = place[1], mains[0].shape[1]
    for weight, out in ((w_in, projected), (w_gate, gate_pre)):
        total = dot(mains[0][...], weight[part(me, width), :])
        for j in range(1, channels):
            total += dot(mains[j][...], weight[part(me ^ j, width), :])
        out[...] = total
    w_in_on[...] = w_in[...]


def keep_inside(total, place, before, rows):
    position = lax.broadcasted_iota(jnp.int32, total.shape, 0) + (place[0] * rows - before)
    return jnp.where((position >= 0) & (position < place[2] * rows), total, 0.0)


def forward_kernel(channels, place, edges, edges_core, w_in, projected, gate_pre, conv_w, *outs):
    levels, level_3, gated, *stages = outs
    me, odd = place[1], place[0] % 2
    rows, width = projected.shape
    left = jnp.zeros((EDGE, width), F32)
    right = jnp.zeros((AFT[0], width), F32)
    for j in range(channels):
        source = edges_core if j % 2 else edges
        base = (j // 2) * 2 * EDGE
        weight = w_in[part(me ^ j, width), :]
        left += dot(source[pl.ds(pl.multiple_of(base + (1 - odd) * EDGE, 16), EDGE), :], weight)
        right += dot(source[pl.ds(pl.multiple_of(base + odd * EDGE, 16), AFT[0]), :], weight)
    source = stages[0]
    source[:EDGE] = left
    source[EDGE : EDGE + rows] = projected[...]
    source[EDGE + rows :] = right
    top = 0
    for number, dilation in enumerate(DILATIONS):
        target = stages[number + 1]
        levels[top : top + source.shape[0], :] = source[...].astype(BF16)
        top += source.shape[0]
        shift = FORE[number] - FORE[number + 1]
        count = FORE[number + 1] + rows + AFT[number + 1]
        total = jnp.zeros((count, width), F32)
        for tap in range(4):
            begin = shift + (tap - 2) * dilation
            total += conv_w[number, tap : tap + 1, :] * source[begin : begin + count]
        if FORE[number + 1]:
            total = keep_inside(total, place, FORE[number + 1], rows)
        target[:count] = total
        if count < target.shape[0]:
            target[count:] = jnp.zeros((target.shape[0] - count, width), F32)
        source = target
    gate = gate_pre[...]
    level_3[...] = source[...].astype(BF16)
    gated[...] = (source[...] * (gate / (1.0 + jnp.exp(-gate)))).astype(BF16)


def flip_kernel(place, block, flipped):
    flipped[...] = dot(anti_identity(block.shape[0]), block[...]).astype(BF16)


def norm_grad_kernel(channels, place, *refs):
    own, mirrored = refs[:channels], refs[channels : 2 * channels]
    *weights, order, out, flipped, choose, scratch = refs[2 * channels :]
    me = place[1]
    rows, width = own[0].shape
    turn = anti_identity(rows)
    flipped[...] = dot(turn, mirrored[0][...]).astype(BF16)
    for j in range(1, channels):
        scratch[j] = dot(turn, mirrored[j][...]).astype(BF16)
    for block in range(2):
        for i in range(channels):
            total = jnp.zeros((rows, width), F32)
            for j in range(channels):
                cotangent = own[j][...] if block == 0 else scratch[j] if j else flipped[...]
                total += dot(cotangent, weights[j][part(i ^ me, width), :], LAST_DOT)
            out[block * rows : (block + 1) * rows, i * width : (i + 1) * width] = total.astype(BF16)
    down = lax.broadcasted_iota(jnp.int32, (width, width), 0)
    for j in range(channels):
        for i in range(channels):
            wanted = order[:, part(me ^ i, width)]
            choose[j * width : (j + 1) * width, i * width : (i + 1) * width] = (
                (down + (me ^ j) * width == wanted).astype(F32).astype(BF16)
            )


def combine_kernel(channels, place, *refs):
    own, mirrored = refs[:channels], refs[channels : 2 * channels]
    grad_norm, choose, gain, gate_pre, level_3 = refs[2 * channels : 2 * channels + 5]
    normalized, upstream, grad_gate_pre, first, second, gains, grad_gated = refs[2 * channels + 5 :]
    me = place[1]
    rows, width = own[0].shape
    full = channels * width
    tile = rows // 4
    for j in range(channels):
        gains[:, j * width : (j + 1) * width] = gain[:, part(me ^ j, width)]
    for block, (here, there) in enumerate(((own, mirrored), (mirrored, own))):
        for k in range(4):
            at = slice(k * tile, (k + 1) * tile)
            mine = jnp.concatenate([ref[at, :] for ref in here], axis=1)
            other = jnp.concatenate([ref[at, :] for ref in there], axis=1)
            combined = mine.astype(F32) + dot(other, choose[...])
            mean = jnp.sum(combined * combined, axis=1, keepdims=True) * (1.0 / full)
            inv_scale = lax.rsqrt(mean + EPSILON)
            hat = combined * inv_scale
            at_both = slice(block * rows + k * tile, block * rows + (k + 1) * tile)
            normalized[at_both, :] = (hat * gains[...]).astype(BF16)
            scaled = grad_norm[at_both, :].astype(F32) * gains[...]
            row_total = jnp.sum(scaled * hat, axis=1, keepdims=True) * (1.0 / full)
            if block == 0:
                grad_gated[at, :] = inv_scale * (scaled[:, :width] - hat[:, :width] * row_total)
            else:
                grad_comb = (inv_scale * (scaled - hat * row_total)).astype(BF16)
                grad_gated[at, :] += dot(grad_comb, choose[:width, :], LAST_DOT)
    gate = gate_pre[...]
    sigmoid = 1.0 / (1.0 + jnp.exp(-gate))
    total = grad_gated[...]
    upstream[...] = (total * (gate * sigmoid)).astype(BF16)
    grad_gate_pre[...] = (total * level_3[...].astype(F32) * sigmoid * (1.0 + gate * (1.0 - sigmoid))).astype(BF16)
    odd, far = place[0] % 2, rows - EDGE
    first[...] = upstream[pl.ds(pl.multiple_of((1 - odd) * far, 16), EDGE), :]
    second[...] = upstream[pl.ds(pl.multiple_of(odd * far, 16), EDGE), :]


def output_kernel(channels, place, normalized, w_out, block_in, output):
    me = place[1]
    rows, width = block_in.shape
    total = block_in[...].astype(F32)
    for j in range(channels):
        total += dot(normalized[:rows, j * width : (j + 1) * width], w_out[part(me ^ j, width), :])
    output[...] = total.astype(BF16)


def products_kernel(channels, place, normalized, cotangent, mirrored_cotangent, grad_gate_pre, *refs):
    mains = refs[:channels]
    out_sent, out_kept, gate_sent, gate_kept, whole_out, whole_gate = refs[channels:]
    me, side = place[1], place[0] % 2
    rows, width = cotangent.shape
    for j in range(channels // 2):
        block = (side * (channels // 2) + j) ^ me
        columns = part(block, width)
        whole_out[j * width : (j + 1) * width, :] = dot(
            normalized[:rows, columns], cotangent[...], ROWS_DOT
        ) + dot(normalized[rows:, columns], mirrored_cotangent[...], ROWS_DOT)
    half = whole_out.shape[0] // 2
    bit = (place[0] // 2) % 2
    out_sent[...] = whole_out[part(1 - bit, half), :].astype(BF16)
    out_kept[...] = whole_out[part(bit, half), :]
    for j in range(channels):
        whole_gate[part(me ^ j, width), :] = dot(mains[j][...], grad_gate_pre[...], ROWS_DOT)
    half = whole_gate.shape[0] // 2
    gate_sent[...] = whole_gate[part(1 - side, half), :].astype(BF16)
    gate_kept[...] = whole_gate[part(side, half), :]


def backward_kernel(channels, place, upstream, first, second, conv_w, *refs):
    mains, (saved, sent, kept, whole, grad_3, grad_2, grad_1, levels) = refs[:channels], refs[channels:]
    levels[...] = saved[...].astype(F32)
    me, odd = place[1], place[0] % 2
    rows, width = upstream.shape
    fore = BACK_FORE[3]
    even = (odd == 0).astype(F32)
    early, late = first[...].astype(F32), second[...].astype(F32)
    grad_3[:fore] = (early * (1.0 - even) + late * even)[EDGE - fore :]
    grad_3[fore : fore + rows] = upstream[...].astype(F32)
    grad_3[fore + rows :] = early * even + late * (1.0 - even)
    half = whole.shape[0] // 2
    for top in (half - SPARE, 2 * half - SPARE):
        whole[top : top + SPARE, :] = jnp.zeros((SPARE, width), F32)
    grads = (None, grad_1, grad_2, grad_3)
    grad_0 = None
    for number in (2, 1, 0):
        dilation, source = DILATIONS[number], grads[number + 1]
        top = sum(saved_rows(rows, below) for below in range(number))
        fore = BACK_FORE[number + 1]
        here = source[fore : fore + rows]
        for tap in range(4):
            begin = top + FORE[number] + (tap - 2) * dilation
            row = half - SPARE + 4 * number + tap
            whole[row : row + 1, :] = jnp.sum(here * levels[begin : begin + rows], axis=0, keepdims=True)
        count = BACK_FORE[number] + rows + BACK_AFT[number]
        total = jnp.zeros((count, width), F32)
        for tap in range(4):
            begin = fore - BACK_FORE[number] - (tap - 2) * dilation
            total += conv_w[number, tap : tap + 1, :] * source[begin : begin + count]
        if number:
            grads[number][...] = keep_inside(total, place, BACK_FORE[number], rows)
        else:
            grad_0 = total.astype(BF16)
    for j in range(channels):
        block = me ^ j
        start = (block // (channels // 2)) * half + (block % (channels // 2)) * width
        whole[pl.ds(pl.multiple_of(start, SPARE), width), :] = dot(mains[j][...], grad_0, ROWS_DOT)
    sent[...] = whole[part(1 - odd, half), :].astype(BF16)
    kept[...] = whole[part(odd, half), :]


def split(total, bit):
    half = total.shape[0] // 2
    low, high = total[:half], total[half:]
    first = jnp.broadcast_to(bit, low.shape) == 0
    return jnp.where(first, high, low), jnp.where(first, low, high)


def join(mine, other, bit):
    first = jnp.broadcast_to(bit, mine.shape) == 0
    return jnp.where(first, mine, other), jnp.where(first, other, mine)


def step_kernel(plan, place, *refs):
    sources, targets = refs[: 2 * len(plan)], list(refs[2 * len(plan) :])
    for k, (done, after) in enumerate(plan):
        mine, other = sources[2 * k][...].astype(F32), sources[2 * k + 1][...].astype(F32)
        if done[0] == "halve":
            total = mine + other
        else:
            low, high = join(mine, other, (place[0] // done[1]) % 2)
            if after is not None and after[0] == "take":
                grad, taps = targets.pop(0), targets.pop(0)
                count = low.shape[0] - SPARE
                grad[:count] = low[:count].astype(BF16)
                grad[count:] = high[:count].astype(BF16)
                taps[...] = low[count : count + taps.shape[0]]
                continue
            total = jnp.concatenate([low, high], axis=0)
        if after is not None and after[0] == "halve":
            sent, kept = split(total, (place[0] // after[1]) % 2)
            targets.pop(0)[...] = sent.astype(BF16)
            targets.pop(0)[...] = kept
        else:
            targets.pop(0)[...] = total.astype(BF16)


def advance(place, items, taps):
    width = items[0][2].shape[1]
    outs, counts = [], []
    for done, after, mine, _ in items:
        rows = mine.shape[0] * (1 if done[0] == "halve" else 2)
        if after is not None and after[0] == "halve":
            outs += [((rows // 2, width), BF16), ((rows // 2, width), F32)]
            counts.append(2)
        elif after is not None and after[0] == "take":
            outs += [((rows - 2 * SPARE, width), BF16), ((taps, width), F32)]
            counts.append(2)
        else:
            outs.append(((rows, width), BF16))
            counts.append(1)
    arrays = [array for item in items for array in item[2:]]
    plan = [item[:2] for item in items]
    if all(shape[0] % 8 == 0 or shape[0] == taps for shape, _ in outs) and all(x.shape[0] % 8 == 0 for x in arrays):
        results = run(functools.partial(step_kernel, plan), place, arrays, outs)
    else:
        results = []
        for done, after, mine, other in items:
            mine, other = mine.astype(F32), other.astype(F32)
            if done[0] == "halve":
                total = mine + other
            else:
                total = jnp.concatenate(join(mine, other, seq_bit(done[1])), axis=0)
            if after is not None and after[0] == "halve":
                sent, kept = split(total, seq_bit(after[1]))
                results += [sent.astype(BF16), kept]
            elif after is not None and after[0] == "take":
                half = total.shape[0] // 2
                results += [
                    jnp.concatenate([total[: half - SPARE], total[half:-SPARE]], axis=0).astype(BF16),
                    total[half - SPARE : half - SPARE + taps],
                ]
            else:
                results.append(total.astype(BF16))
    grouped = []
    for count in counts:
        grouped.append(results[:count])
        results = results[count:]
    return grouped


def exchange(block, axis, distance):
    count = lax.axis_size(axis)
    return lax.ppermute(block, axis, [(i, i ^ distance) for i in range(count)])


def distances(axis):
    return [1 << bit for bit in range(lax.axis_size(axis).bit_length() - 1)]


def mirror(block):
    count = lax.axis_size("seq")
    return lax.ppermute(block, "seq", [(i, count - 1 - i) for i in range(count)])


def swap_edges(first, second, far=0):
    count, channels = lax.axis_size("seq"), lax.axis_size("ch")
    received = []
    for turn, block in enumerate((first, second)):
        route = []
        for low in range(turn, count - 1, 2):
            for c in range(channels):
                route.append((low * channels + c, (low + 1) * channels + (c ^ far)))
                route.append(((low + 1) * channels + c, low * channels + (c ^ far)))
        received.append(lax.ppermute(block, ("seq", "ch"), route))
    return received


def together(*values):
    return lax.optimization_barrier(values)


def seq_bit(distance):
    return (lax.axis_index("seq") & distance) // distance


def local(tokens, hidden, embedding, w_in, w_gate, conv_w, channel_order, gain, w_out, cotangent):
    rows, width = hidden.shape
    full = gain.shape[0]
    channels = full // width
    cross = channels // 2
    taps = conv_w.shape[0] * conv_w.shape[1]
    steps = distances("seq")
    block = ((rows, width), BF16)
    place = jnp.stack([lax.axis_index("seq"), lax.axis_index("ch"), lax.axis_size("seq")]).astype(jnp.int32)

    cotangent_x = exchange(cotangent, "ch", cross)
    mirrored_cotangent = mirror(cotangent)
    inputs = (tokens.reshape(1, rows), hidden, embedding)
    local_input, first, second = run(
        input_kernel,
        place,
        inputs,
        [block, ((EDGE, width), BF16), ((EDGE, width), BF16)],
        [pltpu.VMEM((16, width), F32), *fetch_scratch(inputs)],
        megabytes=60,
        fetched=3,
    )
    input_x = exchange(local_input, "ch", cross)
    input_core = exchange(local_input, "ch", 1)
    first, second, cotangent_x = together(first, second, cotangent_x)
    near = swap_edges(first, second)
    first, second, mirrored_cotangent = together(first, second, mirrored_cotangent)
    edges = jnp.concatenate(near + swap_edges(first, second, cross), axis=0)
    edges_core = exchange(edges, "ch", 1)
    mirrored_cotangent_x = exchange(mirrored_cotangent, "ch", cross)
    early_w_out, mirrored_cotangent_x = together(w_out, mirrored_cotangent_x)
    w_out_x = exchange(early_w_out, "ch", cross)
    mains = [local_input, input_core, input_x, exchange(input_x, "ch", 1)]

    projected, gate_pre, w_in_on = run(
        functools.partial(project_kernel, channels),
        place,
        (*mains, w_in, w_gate),
        [((rows, width), F32)] * 2 + [(w_in.shape, BF16)],
        gflop=6.0,
    )
    levels, level_3, gated = run(
        functools.partial(forward_kernel, channels),
        place,
        (edges, edges_core, w_in_on, projected, gate_pre, conv_w),
        [((sum(saved_rows(rows, number) for number in range(3)), width), BF16), block, block],
        [pltpu.VMEM((saved_rows(rows, number), width), F32) for number in range(4)],
        gflop=0.4,
    )
    mirrored, w_out_x = together(mirror(gated), w_out_x)
    mirrored = run(flip_kernel, place, (mirrored,), [block], gflop=12.0)[0]
    gated_x = exchange(gated, "ch", cross)
    mirrored, gated_x = together(mirrored, gated_x)
    mirrored_x = exchange(mirrored, "ch", cross)
    gated_all = [gated, exchange(gated, "ch", 1), gated_x, exchange(gated_x, "ch", 1)]
    cotangent_all = [cotangent, exchange(cotangent, "ch", 1), cotangent_x, exchange(cotangent_x, "ch", 1)]
    mirrored_cotangent_all = [
        mirrored_cotangent,
        exchange(mirrored_cotangent, "ch", 1),
        mirrored_cotangent_x,
        exchange(mirrored_cotangent_x, "ch", 1),
    ]
    grad_norm, flipped_cotangent, choose = run(
        functools.partial(norm_grad_kernel, channels),
        place,
        (
            *cotangent_all,
            *mirrored_cotangent_all,
            w_out,
            exchange(w_out, "ch", 1),
            w_out_x,
            exchange(w_out_x, "ch", 1),
            channel_order.reshape(1, full),
        ),
        [((2 * rows, full), BF16), block, ((full, full), BF16)],
        [pltpu.VMEM((channels, rows, width), BF16)],
        gflop=2.1,
    )
    mirrored_x, grad_norm = together(mirrored_x, grad_norm)
    mirrored_all = [mirrored, exchange(mirrored, "ch", 1), mirrored_x, exchange(mirrored_x, "ch", 1)]

    normalized, upstream, grad_gate_pre, first, second = run(
        functools.partial(combine_kernel, channels),
        place,
        (*gated_all, *mirrored_all, grad_norm, choose, gain.reshape(1, full), gate_pre, level_3),
        [((2 * rows, full), BF16), block, block, ((EDGE, width), BF16), ((EDGE, width), BF16)],
        [pltpu.VMEM((1, full), F32), pltpu.VMEM((rows, width), F32)],
        gflop=2.5,
    )
    first, second = swap_edges(first, second)
    out_sent, out_kept, gate_sent, gate_kept = run(
        functools.partial(products_kernel, channels),
        place,
        (normalized, cotangent, flipped_cotangent, grad_gate_pre, *mains),
        [
            ((full // 4, width), BF16),
            ((full // 4, width), F32),
            ((full // 2, width), BF16),
            ((full // 2, width), F32),
        ],
        [pltpu.VMEM((full // 2, width), F32), pltpu.VMEM((full, width), F32)],
        gflop=0.8,
    )
    out_sent, gate_sent, first, second = together(out_sent, gate_sent, first, second)
    out_other = exchange(out_sent, "seq", steps[1])
    gate_other = exchange(gate_sent, "seq", steps[0])
    half = full // 2 + SPARE
    in_sent, in_kept = run(
        functools.partial(backward_kernel, channels),
        place,
        (upstream, first, second, conv_w, *mains, levels),
        [((half, width), BF16), ((half, width), F32)],
        [pltpu.VMEM((2 * half, width), F32)]
        + [pltpu.VMEM((BACK_FORE[k] + rows + BACK_AFT[k], width), F32) for k in (3, 2, 1)]
        + [pltpu.VMEM(levels.shape, F32)],
        gflop=0.5,
    )
    output = run(
        functools.partial(output_kernel, channels),
        place,
        (normalized, w_out, local_input),
        [block],
        gflop=0.3,
    )[0]

    down = [("halve", distance) for distance in steps]
    up = [("double", distance) for distance in steps[::-1]]
    routes = [down + up + [("take",)], down + up + [None], down[1:] + up + [None]]
    state = [None, (gate_kept, gate_other), (out_kept, out_other)]
    results = [None, None, None]
    for turn in range(len(routes[0]) - 1):
        live = [k for k in range(3) if state[k] is not None]
        places = [turn - 1 if k == 0 else turn for k in live]
        items = [(routes[k][at], routes[k][at + 1], *state[k]) for k, at in zip(live, places)]
        prepared = dict(zip(live, advance(place, items, taps)))
        if turn == 0:
            prepared[0] = (in_sent, in_kept)
        for k, at in zip([0] * (turn == 0) + live, [-1] * (turn == 0) + places):
            upcoming = routes[k][at + 1]
            if upcoming is None:
                results[k], state[k] = prepared[k][0], None
            else:
                sent, kept = prepared[k] if len(prepared[k]) == 2 else prepared[k] * 2
                state[k] = (kept, exchange(sent, "seq", upcoming[1]))
    last = len(routes[0]) - 2
    (grad_in, grad_conv), = advance(place, [(routes[0][last], routes[0][last + 1], *state[0])], taps)
    sum_gate, sum_out = results[1:]
    grad_conv = grad_conv.reshape(conv_w.shape)
    return output, grad_in, sum_gate, sum_out, grad_conv


def solution(mesh):
    placed = (
        P("seq"),
        P("seq", "ch"),
        P(None, "ch"),
        P(None, "ch"),
        P(None, "ch"),
        P(None, None, "ch"),
        P(),
        P(),
        P(None, "ch"),
        P("seq", "ch"),
    )
    return jax.shard_map(
        local,
        mesh=mesh,
        in_specs=placed,
        out_specs=(
            P("seq", "ch"),
            P(None, "ch"),
            P(None, "ch"),
            P(None, "ch"),
            P(None, None, "ch"),
        ),
        check_vma=False,
    )
```

```python
import functools

import jax
import jax.numpy as jnp
from jax import lax
from jax.experimental import pallas as pl
from jax.experimental.pallas import tpu as pltpu
from jax.sharding import PartitionSpec as P

DILATIONS = (1, 8, 64)
EPSILON = 1e-06
FORE = (160, 144, 128, 0)
AFT = (80, 72, 64, 0)
BACK_FORE = (0, 8, 16, 80)
BACK_AFT = (0, 8, 24, 160)
EDGE = 160
SPARE = 64

BF16, F32 = jnp.bfloat16, jnp.float32
ROWS_DOT = (((0,), (0,)), ((), ()))
LAST_DOT = (((1,), (1,)), ((), ()))


def dot(left, right, dims=(((1,), (0,)), ((), ()))):
    return lax.dot_general(left, right, dims, preferred_element_type=F32)


def run(body, place, operands, outs, scratch=(), megabytes=8, gflop=0.1, fetched=0):
    moved = sum(x.size * x.dtype.itemsize for x in operands)
    return pl.pallas_call(
        body,
        out_shape=[jax.ShapeDtypeStruct(shape, dtype) for shape, dtype in outs],
        in_specs=[pl.BlockSpec(memory_space=pltpu.SMEM)]
        + [pl.BlockSpec(memory_space=pltpu.VMEM)] * (len(operands) - fetched)
        + [pl.BlockSpec(memory_space=pltpu.HBM)] * fetched,
        out_specs=[pl.BlockSpec(memory_space=pltpu.VMEM)] * len(outs),
        scratch_shapes=list(scratch),
        compiler_params=pltpu.CompilerParams(vmem_limit_bytes=megabytes << 20),
        cost_estimate=pl.CostEstimate(flops=int(gflop * 1e9), bytes_accessed=moved, transcendentals=0),
    )(place, *operands)


def fetch(sources, targets, semaphores):
    copies = [
        pltpu.make_async_copy(source, target, semaphores.at[k])
        for k, (source, target) in enumerate(zip(sources, targets))
    ]
    for copy in copies:
        copy.start()
    return copies


def fetch_scratch(operands):
    return [pltpu.VMEM(x.shape, x.dtype) for x in operands] + [pltpu.SemaphoreType.DMA((len(operands),))]


def part(index, size, multiple=None):
    return pl.ds(pl.multiple_of(index * size, multiple or size), size)


def saved_rows(rows, number):
    return -(-(FORE[number] + rows + AFT[number]) // 16) * 16


def anti_identity(rows):
    down = lax.broadcasted_iota(jnp.int32, (rows, rows), 0)
    across = lax.broadcasted_iota(jnp.int32, (rows, rows), 1)
    return (down + across == rows - 1).astype(F32).astype(BF16)


def input_kernel(place, tokens_hbm, hidden_hbm, embedding_hbm, block_in, first, second, *scratch):
    padded, tokens, hidden, embedding, semaphores = scratch
    copies = fetch((tokens_hbm, hidden_hbm, embedding_hbm), (tokens, hidden, embedding), semaphores)
    bases, rows = embedding.shape[0], hidden.shape[0]
    padded[...] = jnp.zeros_like(padded)
    for copy in copies:
        copy.wait()
    padded[:bases] = embedding[...].astype(F32)
    base = lax.broadcasted_iota(jnp.int32, (padded.shape[0], rows), 0)
    one_hot = (base == tokens[...]).astype(F32).astype(BF16)
    shift = dot(one_hot, padded[...].astype(BF16), ROWS_DOT)
    block_in[...] = (hidden[...].astype(F32) + shift).astype(BF16)
    odd, far = place[0] % 2, rows - EDGE
    first[...] = block_in[pl.ds(pl.multiple_of((1 - odd) * far, 16), EDGE), :]
    second[...] = block_in[pl.ds(pl.multiple_of(odd * far, 16), EDGE), :]


def project_kernel(channels, place, *refs):
    mains, (w_in, w_gate, projected, gate_pre, w_in_on) = refs[:channels], refs[channels:]
    me, width = place[1], mains[0].shape[1]
    for weight, out in ((w_in, projected), (w_gate, gate_pre)):
        total = dot(mains[0][...], weight[part(me, width), :])
        for j in range(1, channels):
            total += dot(mains[j][...], weight[part(me ^ j, width), :])
        out[...] = total
    w_in_on[...] = w_in[...]


def keep_inside(total, place, before, rows):
    position = lax.broadcasted_iota(jnp.int32, total.shape, 0) + (place[0] * rows - before)
    return jnp.where((position >= 0) & (position < place[2] * rows), total, 0.0)


def forward_kernel(channels, place, edges, edges_core, w_in, projected, gate_pre, conv_w, *outs):
    levels, level_3, gated, *stages = outs
    me, odd = place[1], place[0] % 2
    rows, width = projected.shape
    left = jnp.zeros((EDGE, width), F32)
    right = jnp.zeros((AFT[0], width), F32)
    for j in range(channels):
        source = edges_core if j % 2 else edges
        base = (j // 2) * 2 * EDGE
        weight = w_in[part(me ^ j, width), :]
        left += dot(source[pl.ds(pl.multiple_of(base + (1 - odd) * EDGE, 16), EDGE), :], weight)
        right += dot(source[pl.ds(pl.multiple_of(base + odd * EDGE, 16), AFT[0]), :], weight)
    source = stages[0]
    source[:EDGE] = left
    source[EDGE : EDGE + rows] = projected[...]
    source[EDGE + rows :] = right
    top = 0
    for number, dilation in enumerate(DILATIONS):
        target = stages[number + 1]
        levels[top : top + source.shape[0], :] = source[...].astype(BF16)
        top += source.shape[0]
        shift = FORE[number] - FORE[number + 1]
        count = FORE[number + 1] + rows + AFT[number + 1]
        total = jnp.zeros((count, width), F32)
        for tap in range(4):
            begin = shift + (tap - 2) * dilation
            total += conv_w[number, tap : tap + 1, :] * source[begin : begin + count]
        if FORE[number + 1]:
            total = keep_inside(total, place, FORE[number + 1], rows)
        target[:count] = total
        if count < target.shape[0]:
            target[count:] = jnp.zeros((target.shape[0] - count, width), F32)
        source = target
    gate = gate_pre[...]
    level_3[...] = source[...].astype(BF16)
    gated[...] = (source[...] * (gate / (1.0 + jnp.exp(-gate)))).astype(BF16)


def flip_kernel(place, block, flipped):
    flipped[...] = dot(anti_identity(block.shape[0]), block[...]).astype(BF16)


def norm_grad_kernel(channels, place, *refs):
    own, mirrored = refs[:channels], refs[channels : 2 * channels]
    *weights, order, out, flipped, choose, scratch = refs[2 * channels :]
    me = place[1]
    rows, width = own[0].shape
    turn = anti_identity(rows)
    flipped[...] = dot(turn, mirrored[0][...]).astype(BF16)
    for j in range(1, channels):
        scratch[j] = dot(turn, mirrored[j][...]).astype(BF16)
    for block in range(2):
        for i in range(channels):
            total = jnp.zeros((rows, width), F32)
            for j in range(channels):
                cotangent = own[j][...] if block == 0 else scratch[j] if j else flipped[...]
                total += dot(cotangent, weights[j][part(i ^ me, width), :], LAST_DOT)
            out[block * rows : (block + 1) * rows, i * width : (i + 1) * width] = total.astype(BF16)
    down = lax.broadcasted_iota(jnp.int32, (width, width), 0)
    for j in range(channels):
        for i in range(channels):
            wanted = order[:, part(me ^ i, width)]
            choose[j * width : (j + 1) * width, i * width : (i + 1) * width] = (
                (down + (me ^ j) * width == wanted).astype(F32).astype(BF16)
            )


def combine_kernel(channels, place, *refs):
    own, mirrored = refs[:channels], refs[channels : 2 * channels]
    grad_norm, choose, gain, gate_pre, level_3 = refs[2 * channels : 2 * channels + 5]
    normalized, upstream, grad_gate_pre, first, second, gains, grad_gated = refs[2 * channels + 5 :]
    me = place[1]
    rows, width = own[0].shape
    full = channels * width
    tile = rows // 4
    for j in range(channels):
        gains[:, j * width : (j + 1) * width] = gain[:, part(me ^ j, width)]
    for block, (here, there) in enumerate(((own, mirrored), (mirrored, own))):
        for k in range(4):
            at = slice(k * tile, (k + 1) * tile)
            mine = jnp.concatenate([ref[at, :] for ref in here], axis=1)
            other = jnp.concatenate([ref[at, :] for ref in there], axis=1)
            combined = mine.astype(F32) + dot(other, choose[...])
            mean = jnp.sum(combined * combined, axis=1, keepdims=True) * (1.0 / full)
            inv_scale = lax.rsqrt(mean + EPSILON)
            hat = combined * inv_scale
            at_both = slice(block * rows + k * tile, block * rows + (k + 1) * tile)
            normalized[at_both, :] = (hat * gains[...]).astype(BF16)
            scaled = grad_norm[at_both, :].astype(F32) * gains[...]
            row_total = jnp.sum(scaled * hat, axis=1, keepdims=True) * (1.0 / full)
            if block == 0:
                grad_gated[at, :] = inv_scale * (scaled[:, :width] - hat[:, :width] * row_total)
            else:
                grad_comb = (inv_scale * (scaled - hat * row_total)).astype(BF16)
                grad_gated[at, :] += dot(grad_comb, choose[:width, :], LAST_DOT)
    gate = gate_pre[...]
    sigmoid = 1.0 / (1.0 + jnp.exp(-gate))
    total = grad_gated[...]
    upstream[...] = (total * (gate * sigmoid)).astype(BF16)
    grad_gate_pre[...] = (total * level_3[...].astype(F32) * sigmoid * (1.0 + gate * (1.0 - sigmoid))).astype(BF16)
    odd, far = place[0] % 2, rows - EDGE
    first[...] = upstream[pl.ds(pl.multiple_of((1 - odd) * far, 16), EDGE), :]
    second[...] = upstream[pl.ds(pl.multiple_of(odd * far, 16), EDGE), :]


def output_kernel(channels, place, normalized, w_out, block_in, output):
    me = place[1]
    rows, width = block_in.shape
    total = block_in[...].astype(F32)
    for j in range(channels):
        total += dot(normalized[:rows, j * width : (j + 1) * width], w_out[part(me ^ j, width), :])
    output[...] = total.astype(BF16)


def products_kernel(channels, place, normalized, cotangent, mirrored_cotangent, grad_gate_pre, *refs):
    mains = refs[:channels]
    out_sent, out_kept, gate_sent, gate_kept, whole_out, whole_gate = refs[channels:]
    me, side = place[1], place[0] % 2
    rows, width = cotangent.shape
    for j in range(channels // 2):
        block = (side * (channels // 2) + j) ^ me
        columns = part(block, width)
        whole_out[j * width : (j + 1) * width, :] = dot(
            normalized[:rows, columns], cotangent[...], ROWS_DOT
        ) + dot(normalized[rows:, columns], mirrored_cotangent[...], ROWS_DOT)
    half = whole_out.shape[0] // 2
    bit = (place[0] // 2) % 2
    out_sent[...] = whole_out[part(1 - bit, half), :].astype(BF16)
    out_kept[...] = whole_out[part(bit, half), :]
    for j in range(channels):
        whole_gate[part(me ^ j, width), :] = dot(mains[j][...], grad_gate_pre[...], ROWS_DOT)
    half = whole_gate.shape[0] // 2
    gate_sent[...] = whole_gate[part(1 - side, half), :].astype(BF16)
    gate_kept[...] = whole_gate[part(side, half), :]


def backward_kernel(channels, place, upstream, first, second, conv_w, *refs):
    mains, (saved, sent, kept, whole, grad_3, grad_2, grad_1, levels) = refs[:channels], refs[channels:]
    levels[...] = saved[...].astype(F32)
    me, odd = place[1], place[0] % 2
    rows, width = upstream.shape
    fore = BACK_FORE[3]
    even = (odd == 0).astype(F32)
    early, late = first[...].astype(F32), second[...].astype(F32)
    grad_3[:fore] = (early * (1.0 - even) + late * even)[EDGE - fore :]
    grad_3[fore : fore + rows] = upstream[...].astype(F32)
    grad_3[fore + rows :] = early * even + late * (1.0 - even)
    half = whole.shape[0] // 2
    for top in (half - SPARE, 2 * half - SPARE):
        whole[top : top + SPARE, :] = jnp.zeros((SPARE, width), F32)
    grads = (None, grad_1, grad_2, grad_3)
    grad_0 = None
    for number in (2, 1, 0):
        dilation, source = DILATIONS[number], grads[number + 1]
        top = sum(saved_rows(rows, below) for below in range(number))
        fore = BACK_FORE[number + 1]
        here = source[fore : fore + rows]
        for tap in range(4):
            begin = top + FORE[number] + (tap - 2) * dilation
            row = half - SPARE + 4 * number + tap
            whole[row : row + 1, :] = jnp.sum(here * levels[begin : begin + rows], axis=0, keepdims=True)
        count = BACK_FORE[number] + rows + BACK_AFT[number]
        total = jnp.zeros((count, width), F32)
        for tap in range(4):
            begin = fore - BACK_FORE[number] - (tap - 2) * dilation
            total += conv_w[number, tap : tap + 1, :] * source[begin : begin + count]
        if number:
            grads[number][...] = keep_inside(total, place, BACK_FORE[number], rows)
        else:
            grad_0 = total.astype(BF16)
    for j in range(channels):
        block = me ^ j
        start = (block // (channels // 2)) * half + (block % (channels // 2)) * width
        whole[pl.ds(pl.multiple_of(start, SPARE), width), :] = dot(mains[j][...], grad_0, ROWS_DOT)
    sent[...] = whole[part(1 - odd, half), :].astype(BF16)
    kept[...] = whole[part(odd, half), :]


def split(total, bit):
    half = total.shape[0] // 2
    low, high = total[:half], total[half:]
    first = jnp.broadcast_to(bit, low.shape) == 0
    return jnp.where(first, high, low), jnp.where(first, low, high)


def join(mine, other, bit):
    first = jnp.broadcast_to(bit, mine.shape) == 0
    return jnp.where(first, mine, other), jnp.where(first, other, mine)


def step_kernel(plan, place, *refs):
    sources, targets = refs[: 2 * len(plan)], list(refs[2 * len(plan) :])
    for k, (done, after) in enumerate(plan):
        mine, other = sources[2 * k][...].astype(F32), sources[2 * k + 1][...].astype(F32)
        if done[0] == "halve":
            total = mine + other
        else:
            low, high = join(mine, other, (place[0] // done[1]) % 2)
            if after is not None and after[0] == "take":
                grad, taps = targets.pop(0), targets.pop(0)
                count = low.shape[0] - SPARE
                grad[:count] = low[:count].astype(BF16)
                grad[count:] = high[:count].astype(BF16)
                taps[...] = low[count : count + taps.shape[0]]
                continue
            total = jnp.concatenate([low, high], axis=0)
        if after is not None and after[0] == "halve":
            sent, kept = split(total, (place[0] // after[1]) % 2)
            targets.pop(0)[...] = sent.astype(BF16)
            targets.pop(0)[...] = kept
        else:
            targets.pop(0)[...] = total.astype(BF16)


def advance(place, items, taps):
    width = items[0][2].shape[1]
    outs, counts = [], []
    for done, after, mine, _ in items:
        rows = mine.shape[0] * (1 if done[0] == "halve" else 2)
        if after is not None and after[0] == "halve":
            outs += [((rows // 2, width), BF16), ((rows // 2, width), F32)]
            counts.append(2)
        elif after is not None and after[0] == "take":
            outs += [((rows - 2 * SPARE, width), BF16), ((taps, width), F32)]
            counts.append(2)
        else:
            outs.append(((rows, width), BF16))
            counts.append(1)
    arrays = [array for item in items for array in item[2:]]
    plan = [item[:2] for item in items]
    if all(shape[0] % 8 == 0 or shape[0] == taps for shape, _ in outs) and all(x.shape[0] % 8 == 0 for x in arrays):
        results = run(functools.partial(step_kernel, plan), place, arrays, outs)
    else:
        results = []
        for done, after, mine, other in items:
            mine, other = mine.astype(F32), other.astype(F32)
            if done[0] == "halve":
                total = mine + other
            else:
                total = jnp.concatenate(join(mine, other, seq_bit(done[1])), axis=0)
            if after is not None and after[0] == "halve":
                sent, kept = split(total, seq_bit(after[1]))
                results += [sent.astype(BF16), kept]
            elif after is not None and after[0] == "take":
                half = total.shape[0] // 2
                results += [
                    jnp.concatenate([total[: half - SPARE], total[half:-SPARE]], axis=0).astype(BF16),
                    total[half - SPARE : half - SPARE + taps],
                ]
            else:
                results.append(total.astype(BF16))
    grouped = []
    for count in counts:
        grouped.append(results[:count])
        results = results[count:]
    return grouped


def exchange(block, axis, distance):
    count = lax.axis_size(axis)
    return lax.ppermute(block, axis, [(i, i ^ distance) for i in range(count)])


def distances(axis):
    return [1 << bit for bit in range(lax.axis_size(axis).bit_length() - 1)]


def mirror(block):
    count = lax.axis_size("seq")
    return lax.ppermute(block, "seq", [(i, count - 1 - i) for i in range(count)])


def swap_edges(first, second, far=0):
    count, channels = lax.axis_size("seq"), lax.axis_size("ch")
    received = []
    for turn, block in enumerate((first, second)):
        route = []
        for low in range(turn, count - 1, 2):
            for c in range(channels):
                route.append((low * channels + c, (low + 1) * channels + (c ^ far)))
                route.append(((low + 1) * channels + c, low * channels + (c ^ far)))
        received.append(lax.ppermute(block, ("seq", "ch"), route))
    return received


def together(*values):
    return lax.optimization_barrier(values)


def seq_bit(distance):
    return (lax.axis_index("seq") & distance) // distance


def local(tokens, hidden, embedding, w_in, w_gate, conv_w, channel_order, gain, w_out, cotangent):
    rows, width = hidden.shape
    full = gain.shape[0]
    channels = full // width
    cross = channels // 2
    taps = conv_w.shape[0] * conv_w.shape[1]
    steps = distances("seq")
    block = ((rows, width), BF16)
    place = jnp.stack([lax.axis_index("seq"), lax.axis_index("ch"), lax.axis_size("seq")]).astype(jnp.int32)

    cotangent_x = exchange(cotangent, "ch", cross)
    mirrored_cotangent = mirror(cotangent)
    inputs = (tokens.reshape(1, rows), hidden, embedding)
    local_input, first, second = run(
        input_kernel,
        place,
        inputs,
        [block, ((EDGE, width), BF16), ((EDGE, width), BF16)],
        [pltpu.VMEM((16, width), F32), *fetch_scratch(inputs)],
        megabytes=60,
        fetched=3,
    )
    input_x = exchange(local_input, "ch", cross)
    input_core = exchange(local_input, "ch", 1)
    first, second, cotangent_x = together(first, second, cotangent_x)
    near = swap_edges(first, second)
    far = swap_edges(first, second, cross)
    mirrored_cotangent, *far = together(mirrored_cotangent, *far)
    edges = jnp.concatenate(near + far, axis=0)
    mirrored_cotangent_x = exchange(mirrored_cotangent, "ch", cross)
    early_w_out, mirrored_cotangent_x = together(w_out, mirrored_cotangent_x)
    w_out_x = exchange(early_w_out, "ch", cross)
    mains = [local_input, input_core, input_x, exchange(input_x, "ch", 1)]

    projected, gate_pre, w_in_on = run(
        functools.partial(project_kernel, channels),
        place,
        (*mains, w_in, w_gate),
        [((rows, width), F32)] * 2 + [(w_in.shape, BF16)],
        gflop=6.0,
    )
    edges, projected, gate_pre = together(edges, projected, gate_pre)
    edges_core = exchange(edges, "ch", 1)
    levels, level_3, gated = run(
        functools.partial(forward_kernel, channels),
        place,
        (edges, edges_core, w_in_on, projected, gate_pre, conv_w),
        [((sum(saved_rows(rows, number) for number in range(3)), width), BF16), block, block],
        [pltpu.VMEM((saved_rows(rows, number), width), F32) for number in range(4)],
        gflop=0.4,
    )
    mirrored, w_out_x = together(mirror(gated), w_out_x)
    mirrored = run(flip_kernel, place, (mirrored,), [block], gflop=12.0)[0]
    gated_x = exchange(gated, "ch", cross)
    mirrored, gated_x = together(mirrored, gated_x)
    mirrored_x = exchange(mirrored, "ch", cross)
    gated_all = [gated, exchange(gated, "ch", 1), gated_x, exchange(gated_x, "ch", 1)]
    cotangent_all = [cotangent, exchange(cotangent, "ch", 1), cotangent_x, exchange(cotangent_x, "ch", 1)]
    mirrored_cotangent_all = [
        mirrored_cotangent,
        exchange(mirrored_cotangent, "ch", 1),
        mirrored_cotangent_x,
        exchange(mirrored_cotangent_x, "ch", 1),
    ]
    grad_norm, flipped_cotangent, choose = run(
        functools.partial(norm_grad_kernel, channels),
        place,
        (
            *cotangent_all,
            *mirrored_cotangent_all,
            w_out,
            exchange(w_out, "ch", 1),
            w_out_x,
            exchange(w_out_x, "ch", 1),
            channel_order.reshape(1, full),
        ),
        [((2 * rows, full), BF16), block, ((full, full), BF16)],
        [pltpu.VMEM((channels, rows, width), BF16)],
        gflop=2.1,
    )
    mirrored_x, grad_norm = together(mirrored_x, grad_norm)
    mirrored_all = [mirrored, exchange(mirrored, "ch", 1), mirrored_x, exchange(mirrored_x, "ch", 1)]

    normalized, upstream, grad_gate_pre, first, second = run(
        functools.partial(combine_kernel, channels),
        place,
        (*gated_all, *mirrored_all, grad_norm, choose, gain.reshape(1, full), gate_pre, level_3),
        [((2 * rows, full), BF16), block, block, ((EDGE, width), BF16), ((EDGE, width), BF16)],
        [pltpu.VMEM((1, full), F32), pltpu.VMEM((rows, width), F32)],
        gflop=2.5,
    )
    first, second = swap_edges(first, second)
    out_sent, out_kept, gate_sent, gate_kept = run(
        functools.partial(products_kernel, channels),
        place,
        (normalized, cotangent, flipped_cotangent, grad_gate_pre, *mains),
        [
            ((full // 4, width), BF16),
            ((full // 4, width), F32),
            ((full // 2, width), BF16),
            ((full // 2, width), F32),
        ],
        [pltpu.VMEM((full // 2, width), F32), pltpu.VMEM((full, width), F32)],
        gflop=0.8,
    )
    out_sent, gate_sent, first, second = together(out_sent, gate_sent, first, second)
    out_other = exchange(out_sent, "seq", steps[1])
    gate_other = exchange(gate_sent, "seq", steps[0])
    half = full // 2 + SPARE
    in_sent, in_kept = run(
        functools.partial(backward_kernel, channels),
        place,
        (upstream, first, second, conv_w, *mains, levels),
        [((half, width), BF16), ((half, width), F32)],
        [pltpu.VMEM((2 * half, width), F32)]
        + [pltpu.VMEM((BACK_FORE[k] + rows + BACK_AFT[k], width), F32) for k in (3, 2, 1)]
        + [pltpu.VMEM(levels.shape, F32)],
        gflop=0.5,
    )
    output = run(
        functools.partial(output_kernel, channels),
        place,
        (normalized, w_out, local_input),
        [block],
        gflop=0.3,
    )[0]

    down = [("halve", distance) for distance in steps]
    up = [("double", distance) for distance in steps[::-1]]
    routes = [down + up + [("take",)], down + up + [None], down[1:] + up + [None]]
    in_sent, gate_other, out_other = together(in_sent, gate_other, out_other)
    results = []
    for route, sent, kept, other in zip(
        routes, (in_sent, None, None), (in_kept, gate_kept, out_kept), (None, gate_other, out_other)
    ):
        if other is None:
            other = exchange(sent, "seq", route[0][1])
        for done, upcoming in zip(route, route[1:]):
            prepared = advance(place, [(done, upcoming, kept, other)], taps)[0]
            if upcoming is not None and upcoming[0] != "take":
                sent, kept = prepared if len(prepared) == 2 else prepared * 2
                other = exchange(sent, "seq", upcoming[1])
        results.append(prepared)
    (grad_in, grad_conv), (sum_gate,), (sum_out,) = results
    grad_conv = grad_conv.reshape(conv_w.shape)
    return output, grad_in, sum_gate, sum_out, grad_conv


def solution(mesh):
    placed = (
        P("seq"),
        P("seq", "ch"),
        P(None, "ch"),
        P(None, "ch"),
        P(None, "ch"),
        P(None, None, "ch"),
        P(),
        P(),
        P(None, "ch"),
        P("seq", "ch"),
    )
    return jax.shard_map(
        local,
        mesh=mesh,
        in_specs=placed,
        out_specs=(
            P("seq", "ch"),
            P(None, "ch"),
            P(None, "ch"),
            P(None, "ch"),
            P(None, None, "ch"),
        ),
        check_vma=False,
    )
```

```python
import functools

import jax
import jax.numpy as jnp
from jax import lax
from jax.experimental import pallas as pl
from jax.experimental.pallas import tpu as pltpu
from jax.sharding import PartitionSpec as P

DILATIONS = (1, 8, 64)
EPSILON = 1e-06
FORE = (160, 144, 128, 0)
AFT = (80, 72, 64, 0)
BACK_FORE = (0, 8, 16, 80)
BACK_AFT = (0, 8, 24, 160)
EDGE = 160
SPARE = 64

BF16, F32 = jnp.bfloat16, jnp.float32
ROWS_DOT = (((0,), (0,)), ((), ()))
LAST_DOT = (((1,), (1,)), ((), ()))


def dot(left, right, dims=(((1,), (0,)), ((), ()))):
    return lax.dot_general(left, right, dims, preferred_element_type=F32)


def run(body, place, operands, outs, scratch=(), megabytes=8, gflop=0.1, fetched=0):
    moved = sum(x.size * x.dtype.itemsize for x in operands)
    return pl.pallas_call(
        body,
        out_shape=[jax.ShapeDtypeStruct(shape, dtype) for shape, dtype in outs],
        in_specs=[pl.BlockSpec(memory_space=pltpu.SMEM)]
        + [pl.BlockSpec(memory_space=pltpu.VMEM)] * (len(operands) - fetched)
        + [pl.BlockSpec(memory_space=pltpu.HBM)] * fetched,
        out_specs=[pl.BlockSpec(memory_space=pltpu.VMEM)] * len(outs),
        scratch_shapes=list(scratch),
        compiler_params=pltpu.CompilerParams(vmem_limit_bytes=megabytes << 20),
        cost_estimate=pl.CostEstimate(flops=int(gflop * 1e9), bytes_accessed=moved, transcendentals=0),
    )(place, *operands)


def fetch(sources, targets, semaphores):
    copies = [
        pltpu.make_async_copy(source, target, semaphores.at[k])
        for k, (source, target) in enumerate(zip(sources, targets))
    ]
    for copy in copies:
        copy.start()
    return copies


def fetch_scratch(operands):
    return [pltpu.VMEM(x.shape, x.dtype) for x in operands] + [pltpu.SemaphoreType.DMA((len(operands),))]


def part(index, size, multiple=None):
    return pl.ds(pl.multiple_of(index * size, multiple or size), size)


def saved_rows(rows, number):
    return -(-(FORE[number] + rows + AFT[number]) // 16) * 16


def anti_identity(rows):
    down = lax.broadcasted_iota(jnp.int32, (rows, rows), 0)
    across = lax.broadcasted_iota(jnp.int32, (rows, rows), 1)
    return (down + across == rows - 1).astype(F32).astype(BF16)


def input_kernel(place, tokens_hbm, hidden_hbm, embedding_hbm, block_in, first, second, *scratch):
    padded, tokens, hidden, embedding, semaphores = scratch
    copies = fetch((tokens_hbm, hidden_hbm, embedding_hbm), (tokens, hidden, embedding), semaphores)
    bases, rows = embedding.shape[0], hidden.shape[0]
    padded[...] = jnp.zeros_like(padded)
    for copy in copies:
        copy.wait()
    padded[:bases] = embedding[...].astype(F32)
    base = lax.broadcasted_iota(jnp.int32, (padded.shape[0], rows), 0)
    one_hot = (base == tokens[...]).astype(F32).astype(BF16)
    shift = dot(one_hot, padded[...].astype(BF16), ROWS_DOT)
    block_in[...] = (hidden[...].astype(F32) + shift).astype(BF16)
    odd, far = place[0] % 2, rows - EDGE
    first[...] = block_in[pl.ds(pl.multiple_of((1 - odd) * far, 16), EDGE), :]
    second[...] = block_in[pl.ds(pl.multiple_of(odd * far, 16), EDGE), :]


def keep_inside(total, place, before, rows):
    position = lax.broadcasted_iota(jnp.int32, total.shape, 0) + (place[0] * rows - before)
    return jnp.where((position >= 0) & (position < place[2] * rows), total, 0.0)


def forward_kernel(channels, place, *refs):
    count = channels + 5
    gate_pre, levels, level_3, gated, *held = refs[count:]
    copies = fetch(refs[:count], held[:count], held[count])
    w_in, w_gate, conv_w, edges, edges_core, *mains = held[:count]
    stages = held[count + 1 :]
    me, odd = place[1], place[0] % 2
    rows, width = mains[0].shape
    for copy in copies:
        copy.wait()
    projected, gate = (
        sum(dot(mains[j][...], weight[part(me ^ j, width), :]) for j in range(channels)) for weight in (w_in, w_gate)
    )
    gate_pre[...] = gate
    left = jnp.zeros((EDGE, width), F32)
    right = jnp.zeros((AFT[0], width), F32)
    for j in range(channels):
        source = edges_core if j % 2 else edges
        base = (j // 2) * 2 * EDGE
        weight = w_in[part(me ^ j, width), :]
        left += dot(source[pl.ds(pl.multiple_of(base + (1 - odd) * EDGE, 16), EDGE), :], weight)
        right += dot(source[pl.ds(pl.multiple_of(base + odd * EDGE, 16), AFT[0]), :], weight)
    source = stages[0]
    source[:EDGE] = left
    source[EDGE : EDGE + rows] = projected
    source[EDGE + rows :] = right
    top = 0
    for number, dilation in enumerate(DILATIONS):
        target = stages[number + 1]
        levels[top : top + source.shape[0], :] = source[...].astype(BF16)
        top += source.shape[0]
        shift = FORE[number] - FORE[number + 1]
        count = FORE[number + 1] + rows + AFT[number + 1]
        total = jnp.zeros((count, width), F32)
        for tap in range(4):
            begin = shift + (tap - 2) * dilation
            total += conv_w[number, tap : tap + 1, :] * source[begin : begin + count]
        if FORE[number + 1]:
            total = keep_inside(total, place, FORE[number + 1], rows)
        target[:count] = total
        if count < target.shape[0]:
            target[count:] = jnp.zeros((target.shape[0] - count, width), F32)
        source = target
    level_3[...] = source[...].astype(BF16)
    gated[...] = (source[...] * (gate / (1.0 + jnp.exp(-gate)))).astype(BF16)


def flip_kernel(place, block, flipped):
    flipped[...] = dot(anti_identity(block.shape[0]), block[...]).astype(BF16)


def norm_grad_kernel(channels, place, *refs):
    own, mirrored = refs[:channels], refs[channels : 2 * channels]
    *weights, order, out, flipped, choose, scratch = refs[2 * channels :]
    me = place[1]
    rows, width = own[0].shape
    turn = anti_identity(rows)
    flipped[...] = dot(turn, mirrored[0][...]).astype(BF16)
    for j in range(1, channels):
        scratch[j] = dot(turn, mirrored[j][...]).astype(BF16)
    for block in range(2):
        for i in range(channels):
            total = jnp.zeros((rows, width), F32)
            for j in range(channels):
                cotangent = own[j][...] if block == 0 else scratch[j] if j else flipped[...]
                total += dot(cotangent, weights[j][part(i ^ me, width), :], LAST_DOT)
            out[block * rows : (block + 1) * rows, i * width : (i + 1) * width] = total.astype(BF16)
    down = lax.broadcasted_iota(jnp.int32, (width, width), 0)
    for j in range(channels):
        for i in range(channels):
            wanted = order[:, part(me ^ i, width)]
            choose[j * width : (j + 1) * width, i * width : (i + 1) * width] = (
                (down + (me ^ j) * width == wanted).astype(F32).astype(BF16)
            )


def combine_kernel(channels, place, *refs):
    own, mirrored = refs[:channels], refs[channels : 2 * channels]
    grad_norm, choose, gain, gate_pre, level_3 = refs[2 * channels : 2 * channels + 5]
    normalized, upstream, grad_gate_pre, first, second, gains, grad_gated = refs[2 * channels + 5 :]
    me = place[1]
    rows, width = own[0].shape
    full = channels * width
    tile = rows // 4
    for j in range(channels):
        gains[:, j * width : (j + 1) * width] = gain[:, part(me ^ j, width)]
    for block, (here, there) in enumerate(((own, mirrored), (mirrored, own))):
        for k in range(4):
            at = slice(k * tile, (k + 1) * tile)
            mine = jnp.concatenate([ref[at, :] for ref in here], axis=1)
            other = jnp.concatenate([ref[at, :] for ref in there], axis=1)
            combined = mine.astype(F32) + dot(other, choose[...])
            mean = jnp.sum(combined * combined, axis=1, keepdims=True) * (1.0 / full)
            inv_scale = lax.rsqrt(mean + EPSILON)
            hat = combined * inv_scale
            at_both = slice(block * rows + k * tile, block * rows + (k + 1) * tile)
            normalized[at_both, :] = (hat * gains[...]).astype(BF16)
            scaled = grad_norm[at_both, :].astype(F32) * gains[...]
            row_total = jnp.sum(scaled * hat, axis=1, keepdims=True) * (1.0 / full)
            if block == 0:
                grad_gated[at, :] = inv_scale * (scaled[:, :width] - hat[:, :width] * row_total)
            else:
                grad_comb = (inv_scale * (scaled - hat * row_total)).astype(BF16)
                grad_gated[at, :] += dot(grad_comb, choose[:width, :], LAST_DOT)
    gate = gate_pre[...]
    sigmoid = 1.0 / (1.0 + jnp.exp(-gate))
    total = grad_gated[...]
    upstream[...] = (total * (gate * sigmoid)).astype(BF16)
    grad_gate_pre[...] = (total * level_3[...].astype(F32) * sigmoid * (1.0 + gate * (1.0 - sigmoid))).astype(BF16)
    odd, far = place[0] % 2, rows - EDGE
    first[...] = upstream[pl.ds(pl.multiple_of((1 - odd) * far, 16), EDGE), :]
    second[...] = upstream[pl.ds(pl.multiple_of(odd * far, 16), EDGE), :]


def output_kernel(channels, place, normalized, w_out, block_in, output):
    me = place[1]
    rows, width = block_in.shape
    total = block_in[...].astype(F32)
    for j in range(channels):
        total += dot(normalized[:rows, j * width : (j + 1) * width], w_out[part(me ^ j, width), :])
    output[...] = total.astype(BF16)


def products_kernel(channels, place, normalized, cotangent, mirrored_cotangent, grad_gate_pre, *refs):
    mains = refs[:channels]
    out_sent, out_kept, gate_sent, gate_kept, whole_out, whole_gate = refs[channels:]
    me, side = place[1], place[0] % 2
    rows, width = cotangent.shape
    for j in range(channels // 2):
        block = (side * (channels // 2) + j) ^ me
        columns = part(block, width)
        whole_out[j * width : (j + 1) * width, :] = dot(
            normalized[:rows, columns], cotangent[...], ROWS_DOT
        ) + dot(normalized[rows:, columns], mirrored_cotangent[...], ROWS_DOT)
    half = whole_out.shape[0] // 2
    bit = (place[0] // 2) % 2
    out_sent[...] = whole_out[part(1 - bit, half), :].astype(BF16)
    out_kept[...] = whole_out[part(bit, half), :]
    for j in range(channels):
        whole_gate[part(me ^ j, width), :] = dot(mains[j][...], grad_gate_pre[...], ROWS_DOT)
    half = whole_gate.shape[0] // 2
    gate_sent[...] = whole_gate[part(1 - side, half), :].astype(BF16)
    gate_kept[...] = whole_gate[part(side, half), :]


def backward_kernel(channels, place, upstream, first, second, conv_w, *refs):
    mains, (saved, sent, kept, whole, grad_3, grad_2, grad_1, levels) = refs[:channels], refs[channels:]
    levels[...] = saved[...].astype(F32)
    me, odd = place[1], place[0] % 2
    rows, width = upstream.shape
    fore = BACK_FORE[3]
    even = (odd == 0).astype(F32)
    early, late = first[...].astype(F32), second[...].astype(F32)
    grad_3[:fore] = (early * (1.0 - even) + late * even)[EDGE - fore :]
    grad_3[fore : fore + rows] = upstream[...].astype(F32)
    grad_3[fore + rows :] = early * even + late * (1.0 - even)
    half = whole.shape[0] // 2
    for top in (half - SPARE, 2 * half - SPARE):
        whole[top : top + SPARE, :] = jnp.zeros((SPARE, width), F32)
    grads = (None, grad_1, grad_2, grad_3)
    grad_0 = None
    for number in (2, 1, 0):
        dilation, source = DILATIONS[number], grads[number + 1]
        top = sum(saved_rows(rows, below) for below in range(number))
        fore = BACK_FORE[number + 1]
        here = source[fore : fore + rows]
        for tap in range(4):
            begin = top + FORE[number] + (tap - 2) * dilation
            row = half - SPARE + 4 * number + tap
            whole[row : row + 1, :] = jnp.sum(here * levels[begin : begin + rows], axis=0, keepdims=True)
        count = BACK_FORE[number] + rows + BACK_AFT[number]
        total = jnp.zeros((count, width), F32)
        for tap in range(4):
            begin = fore - BACK_FORE[number] - (tap - 2) * dilation
            total += conv_w[number, tap : tap + 1, :] * source[begin : begin + count]
        if number:
            grads[number][...] = keep_inside(total, place, BACK_FORE[number], rows)
        else:
            grad_0 = total.astype(BF16)
    for j in range(channels):
        block = me ^ j
        start = (block // (channels // 2)) * half + (block % (channels // 2)) * width
        whole[pl.ds(pl.multiple_of(start, SPARE), width), :] = dot(mains[j][...], grad_0, ROWS_DOT)
    sent[...] = whole[part(1 - odd, half), :].astype(BF16)
    kept[...] = whole[part(odd, half), :]


def split(total, bit):
    half = total.shape[0] // 2
    low, high = total[:half], total[half:]
    first = jnp.broadcast_to(bit, low.shape) == 0
    return jnp.where(first, high, low), jnp.where(first, low, high)


def join(mine, other, bit):
    first = jnp.broadcast_to(bit, mine.shape) == 0
    return jnp.where(first, mine, other), jnp.where(first, other, mine)


def step_kernel(plan, place, *refs):
    sources, targets = refs[: 2 * len(plan)], list(refs[2 * len(plan) :])
    for k, (done, after) in enumerate(plan):
        mine, other = sources[2 * k][...].astype(F32), sources[2 * k + 1][...].astype(F32)
        if done[0] == "halve":
            total = mine + other
        else:
            low, high = join(mine, other, (place[0] // done[1]) % 2)
            if after is not None and after[0] == "take":
                grad, taps = targets.pop(0), targets.pop(0)
                count = low.shape[0] - SPARE
                grad[:count] = low[:count].astype(BF16)
                grad[count:] = high[:count].astype(BF16)
                taps[...] = low[count : count + taps.shape[0]]
                continue
            total = jnp.concatenate([low, high], axis=0)
        if after is not None and after[0] == "halve":
            sent, kept = split(total, (place[0] // after[1]) % 2)
            targets.pop(0)[...] = sent.astype(BF16)
            targets.pop(0)[...] = kept
        else:
            targets.pop(0)[...] = total.astype(BF16)


def advance(place, items, taps):
    width = items[0][2].shape[1]
    outs, counts = [], []
    for done, after, mine, _ in items:
        rows = mine.shape[0] * (1 if done[0] == "halve" else 2)
        if after is not None and after[0] == "halve":
            outs += [((rows // 2, width), BF16), ((rows // 2, width), F32)]
            counts.append(2)
        elif after is not None and after[0] == "take":
            outs += [((rows - 2 * SPARE, width), BF16), ((taps, width), F32)]
            counts.append(2)
        else:
            outs.append(((rows, width), BF16))
            counts.append(1)
    arrays = [array for item in items for array in item[2:]]
    plan = [item[:2] for item in items]
    if all(shape[0] % 8 == 0 or shape[0] == taps for shape, _ in outs) and all(x.shape[0] % 8 == 0 for x in arrays):
        results = run(functools.partial(step_kernel, plan), place, arrays, outs)
    else:
        results = []
        for done, after, mine, other in items:
            mine, other = mine.astype(F32), other.astype(F32)
            if done[0] == "halve":
                total = mine + other
            else:
                total = jnp.concatenate(join(mine, other, seq_bit(done[1])), axis=0)
            if after is not None and after[0] == "halve":
                sent, kept = split(total, seq_bit(after[1]))
                results += [sent.astype(BF16), kept]
            elif after is not None and after[0] == "take":
                half = total.shape[0] // 2
                results += [
                    jnp.concatenate([total[: half - SPARE], total[half:-SPARE]], axis=0).astype(BF16),
                    total[half - SPARE : half - SPARE + taps],
                ]
            else:
                results.append(total.astype(BF16))
    grouped = []
    for count in counts:
        grouped.append(results[:count])
        results = results[count:]
    return grouped


def exchange(block, axis, distance):
    count = lax.axis_size(axis)
    return lax.ppermute(block, axis, [(i, i ^ distance) for i in range(count)])


def distances(axis):
    return [1 << bit for bit in range(lax.axis_size(axis).bit_length() - 1)]


def mirror(block):
    count = lax.axis_size("seq")
    return lax.ppermute(block, "seq", [(i, count - 1 - i) for i in range(count)])


def swap_edges(first, second, far=0):
    count, channels = lax.axis_size("seq"), lax.axis_size("ch")
    received = []
    for turn, block in enumerate((first, second)):
        route = []
        for low in range(turn, count - 1, 2):
            for c in range(channels):
                route.append((low * channels + c, (low + 1) * channels + (c ^ far)))
                route.append(((low + 1) * channels + c, low * channels + (c ^ far)))
        received.append(lax.ppermute(block, ("seq", "ch"), route))
    return received


def together(*values):
    return lax.optimization_barrier(values)


def seq_bit(distance):
    return (lax.axis_index("seq") & distance) // distance


def local(tokens, hidden, embedding, w_in, w_gate, conv_w, channel_order, gain, w_out, cotangent):
    rows, width = hidden.shape
    full = gain.shape[0]
    channels = full // width
    cross = channels // 2
    taps = conv_w.shape[0] * conv_w.shape[1]
    steps = distances("seq")
    block = ((rows, width), BF16)
    place = jnp.stack([lax.axis_index("seq"), lax.axis_index("ch"), lax.axis_size("seq")]).astype(jnp.int32)

    cotangent_x = exchange(cotangent, "ch", cross)
    mirrored_cotangent = mirror(cotangent)
    inputs = (tokens.reshape(1, rows), hidden, embedding)
    local_input, first, second = run(
        input_kernel,
        place,
        inputs,
        [block, ((EDGE, width), BF16), ((EDGE, width), BF16)],
        [pltpu.VMEM((16, width), F32), *fetch_scratch(inputs)],
        megabytes=60,
        fetched=3,
    )
    input_x = exchange(local_input, "ch", cross)
    input_core = exchange(local_input, "ch", 1)
    near = swap_edges(first, second)
    far = swap_edges(first, second, cross)
    input_x, cotangent_x, *near = together(input_x, cotangent_x, *near)
    edges = jnp.concatenate(near + far, axis=0)
    mirrored_cotangent_x = exchange(mirrored_cotangent, "ch", cross)
    early_w_out, mirrored_cotangent_x = together(w_out, mirrored_cotangent_x)
    w_out_x = exchange(early_w_out, "ch", cross)
    mains = [local_input, input_core, input_x, exchange(input_x, "ch", 1)]

    operands = (w_in, w_gate, conv_w, edges, exchange(edges, "ch", 1), *mains)
    gate_pre, levels, level_3, gated = run(
        functools.partial(forward_kernel, channels),
        place,
        operands,
        [((rows, width), F32), ((sum(saved_rows(rows, number) for number in range(3)), width), BF16), block, block],
        fetch_scratch(operands) + [pltpu.VMEM((saved_rows(rows, number), width), F32) for number in range(4)],
        megabytes=60,
        gflop=1.0,
        fetched=len(operands),
    )
    mirrored, w_out_x = together(mirror(gated), w_out_x)
    mirrored = run(flip_kernel, place, (mirrored,), [block], gflop=12.0)[0]
    gated_x = exchange(gated, "ch", cross)
    mirrored, gated_x = together(mirrored, gated_x)
    mirrored_x = exchange(mirrored, "ch", cross)
    gated_all = [gated, exchange(gated, "ch", 1), gated_x, exchange(gated_x, "ch", 1)]
    cotangent_all = [cotangent, exchange(cotangent, "ch", 1), cotangent_x, exchange(cotangent_x, "ch", 1)]
    mirrored_cotangent_all = [
        mirrored_cotangent,
        exchange(mirrored_cotangent, "ch", 1),
        mirrored_cotangent_x,
        exchange(mirrored_cotangent_x, "ch", 1),
    ]
    grad_norm, flipped_cotangent, choose = run(
        functools.partial(norm_grad_kernel, channels),
        place,
        (
            *cotangent_all,
            *mirrored_cotangent_all,
            w_out,
            exchange(w_out, "ch", 1),
            w_out_x,
            exchange(w_out_x, "ch", 1),
            channel_order.reshape(1, full),
        ),
        [((2 * rows, full), BF16), block, ((full, full), BF16)],
        [pltpu.VMEM((channels, rows, width), BF16)],
        gflop=2.1,
    )
    mirrored_x, grad_norm = together(mirrored_x, grad_norm)
    mirrored_all = [mirrored, exchange(mirrored, "ch", 1), mirrored_x, exchange(mirrored_x, "ch", 1)]

    normalized, upstream, grad_gate_pre, first, second = run(
        functools.partial(combine_kernel, channels),
        place,
        (*gated_all, *mirrored_all, grad_norm, choose, gain.reshape(1, full), gate_pre, level_3),
        [((2 * rows, full), BF16), block, block, ((EDGE, width), BF16), ((EDGE, width), BF16)],
        [pltpu.VMEM((1, full), F32), pltpu.VMEM((rows, width), F32)],
        gflop=2.5,
    )
    first, second = swap_edges(first, second)
    out_sent, out_kept, gate_sent, gate_kept = run(
        functools.partial(products_kernel, channels),
        place,
        (normalized, cotangent, flipped_cotangent, grad_gate_pre, *mains),
        [
            ((full // 4, width), BF16),
            ((full // 4, width), F32),
            ((full // 2, width), BF16),
            ((full // 2, width), F32),
        ],
        [pltpu.VMEM((full // 2, width), F32), pltpu.VMEM((full, width), F32)],
        gflop=0.8,
    )
    out_sent, gate_sent, first, second = together(out_sent, gate_sent, first, second)
    out_other = exchange(out_sent, "seq", steps[1])
    gate_other = exchange(gate_sent, "seq", steps[0])
    half = full // 2 + SPARE
    in_sent, in_kept = run(
        functools.partial(backward_kernel, channels),
        place,
        (upstream, first, second, conv_w, *mains, levels),
        [((half, width), BF16), ((half, width), F32)],
        [pltpu.VMEM((2 * half, width), F32)]
        + [pltpu.VMEM((BACK_FORE[k] + rows + BACK_AFT[k], width), F32) for k in (3, 2, 1)]
        + [pltpu.VMEM(levels.shape, F32)],
        gflop=0.5,
    )
    output = run(
        functools.partial(output_kernel, channels),
        place,
        (normalized, w_out, local_input),
        [block],
        gflop=0.3,
    )[0]

    down = [("halve", distance) for distance in steps]
    up = [("double", distance) for distance in steps[::-1]]
    routes = [down + up + [("take",)], down + up + [None], down[1:] + up + [None]]
    sends = [(in_sent, in_kept), (None, gate_kept, gate_other), (None, out_kept, out_other)]
    results = [None, None, None]

    def move_on(k, at):
        if results[k] is not None:
            return
        done, upcoming = routes[k][at], routes[k][at + 1]
        prepared = advance(place, [(done, upcoming, *sends[k][1:])], taps)[0]
        if upcoming is None or upcoming[0] == "take":
            results[k] = prepared
        else:
            sends[k] = tuple(prepared) if len(prepared) == 2 else (prepared[0], prepared[0])

    def send(k, at):
        if results[k] is None:
            sent, kept = sends[k]
            sends[k] = (sent, kept, exchange(sent, "seq", routes[k][at][1]))

    for at in range(len(routes[0]) - 1):
        open_sums = [k for k in range(3) if results[k] is None]
        ending = [k for k in open_sums if k and routes[k][at + 1] is None]
        for k in open_sums:
            if k and k not in ending:
                move_on(k, at)
        tied = together(*[sends[k][2 if k in ending else 0] for k in open_sums])
        for k, array in zip(open_sums, tied):
            sends[k] = (*sends[k][:2], array) if k in ending else (array, *sends[k][1:])
        for k in ending:
            move_on(k, at)
        for k in (2, 1):
            send(k, at + 1)
        send(0, at)
        move_on(0, at)
    (grad_in, grad_conv), (sum_gate,), (sum_out,) = results
    grad_conv = grad_conv.reshape(conv_w.shape)
    return output, grad_in, sum_gate, sum_out, grad_conv


def solution(mesh):
    placed = (
        P("seq"),
        P("seq", "ch"),
        P(None, "ch"),
        P(None, "ch"),
        P(None, "ch"),
        P(None, None, "ch"),
        P(),
        P(),
        P(None, "ch"),
        P("seq", "ch"),
    )
    return jax.shard_map(
        local,
        mesh=mesh,
        in_specs=placed,
        out_specs=(
            P("seq", "ch"),
            P(None, "ch"),
            P(None, "ch"),
            P(None, "ch"),
            P(None, None, "ch"),
        ),
        check_vma=False,
    )
```

```python
import functools

import jax
import jax.numpy as jnp
from jax import lax
from jax.experimental import pallas as pl
from jax.experimental.pallas import tpu as pltpu
from jax.sharding import PartitionSpec as P

DILATIONS = (1, 8, 64)
EPSILON = 1e-06
FORE = (160, 144, 128, 0)
AFT = (80, 72, 64, 0)
BACK_FORE = (0, 8, 16, 80)
BACK_AFT = (0, 8, 24, 160)
EDGE = 160
SPARE = 64

BF16, F32 = jnp.bfloat16, jnp.float32
ROWS_DOT = (((0,), (0,)), ((), ()))
LAST_DOT = (((1,), (1,)), ((), ()))


def dot(left, right, dims=(((1,), (0,)), ((), ()))):
    return lax.dot_general(left, right, dims, preferred_element_type=F32)


def run(body, place, operands, outs, scratch=(), megabytes=8, gflop=0.1, fetched=0):
    moved = sum(x.size * x.dtype.itemsize for x in operands)
    return pl.pallas_call(
        body,
        out_shape=[jax.ShapeDtypeStruct(shape, dtype) for shape, dtype in outs],
        in_specs=[pl.BlockSpec(memory_space=pltpu.SMEM)]
        + [pl.BlockSpec(memory_space=pltpu.VMEM)] * (len(operands) - fetched)
        + [pl.BlockSpec(memory_space=pltpu.HBM)] * fetched,
        out_specs=[pl.BlockSpec(memory_space=pltpu.VMEM)] * len(outs),
        scratch_shapes=list(scratch),
        compiler_params=pltpu.CompilerParams(vmem_limit_bytes=megabytes << 20),
        cost_estimate=pl.CostEstimate(flops=int(gflop * 1e9), bytes_accessed=moved, transcendentals=0),
    )(place, *operands)


def fetch(sources, targets, semaphores):
    copies = [
        pltpu.make_async_copy(source, target, semaphores.at[k])
        for k, (source, target) in enumerate(zip(sources, targets))
    ]
    for copy in copies:
        copy.start()
    return copies


def fetch_scratch(operands):
    return [pltpu.VMEM(x.shape, x.dtype) for x in operands] + [pltpu.SemaphoreType.DMA((len(operands),))]


def part(index, size, multiple=None):
    return pl.ds(pl.multiple_of(index * size, multiple or size), size)


def saved_rows(rows, number):
    return -(-(FORE[number] + rows + AFT[number]) // 16) * 16


def anti_identity(rows):
    down = lax.broadcasted_iota(jnp.int32, (rows, rows), 0)
    across = lax.broadcasted_iota(jnp.int32, (rows, rows), 1)
    return (down + across == rows - 1).astype(F32).astype(BF16)


def input_kernel(place, tokens_hbm, hidden_hbm, embedding_hbm, block_in, first, second, *scratch):
    padded, tokens, hidden, embedding, semaphores = scratch
    copies = fetch((tokens_hbm, hidden_hbm, embedding_hbm), (tokens, hidden, embedding), semaphores)
    bases, rows = embedding.shape[0], hidden.shape[0]
    padded[...] = jnp.zeros_like(padded)
    for copy in copies:
        copy.wait()
    padded[:bases] = embedding[...].astype(F32)
    base = lax.broadcasted_iota(jnp.int32, (padded.shape[0], rows), 0)
    one_hot = (base == tokens[...]).astype(F32).astype(BF16)
    shift = dot(one_hot, padded[...].astype(BF16), ROWS_DOT)
    block_in[...] = (hidden[...].astype(F32) + shift).astype(BF16)
    odd, far = place[0] % 2, rows - EDGE
    first[...] = block_in[pl.ds(pl.multiple_of((1 - odd) * far, 16), EDGE), :]
    second[...] = block_in[pl.ds(pl.multiple_of(odd * far, 16), EDGE), :]


def setup_kernel(width, place, order, choose):
    me, full = place[1], order.shape[1]
    down = lax.broadcasted_iota(jnp.int32, (width, width), 0)
    for j in range(full // width):
        for i in range(full // width):
            wanted = order[:, part(me ^ i, width)]
            choose[j * width : (j + 1) * width, i * width : (i + 1) * width] = (
                (down + (me ^ j) * width == wanted).astype(F32).astype(BF16)
            )


def project_kernel(channels, place, *refs):
    mains, (w_in, w_gate, projected, gate_pre, w_in_on) = refs[:channels], refs[channels:]
    me, width = place[1], mains[0].shape[1]
    for weight, out in ((w_in, projected), (w_gate, gate_pre)):
        total = dot(mains[0][...], weight[part(me, width), :])
        for j in range(1, channels):
            total += dot(mains[j][...], weight[part(me ^ j, width), :])
        out[...] = total
    w_in_on[...] = w_in[...]


def keep_inside(total, place, before, rows):
    position = lax.broadcasted_iota(jnp.int32, total.shape, 0) + (place[0] * rows - before)
    return jnp.where((position >= 0) & (position < place[2] * rows), total, 0.0)


def forward_kernel(channels, place, edges, edges_core, w_in, projected, gate_pre, conv_w, *outs):
    levels, level_3, gated, *stages = outs
    me, odd = place[1], place[0] % 2
    rows, width = projected.shape
    left = jnp.zeros((EDGE, width), F32)
    right = jnp.zeros((AFT[0], width), F32)
    for j in range(channels):
        source = edges_core if j % 2 else edges
        base = (j // 2) * 2 * EDGE
        weight = w_in[part(me ^ j, width), :]
        left += dot(source[pl.ds(pl.multiple_of(base + (1 - odd) * EDGE, 16), EDGE), :], weight)
        right += dot(source[pl.ds(pl.multiple_of(base + odd * EDGE, 16), AFT[0]), :], weight)
    source = stages[0]
    source[:EDGE] = left
    source[EDGE : EDGE + rows] = projected[...]
    source[EDGE + rows :] = right
    top = 0
    for number, dilation in enumerate(DILATIONS):
        target = stages[number + 1]
        levels[top : top + source.shape[0], :] = source[...].astype(BF16)
        top += source.shape[0]
        shift = FORE[number] - FORE[number + 1]
        count = FORE[number + 1] + rows + AFT[number + 1]
        total = jnp.zeros((count, width), F32)
        for tap in range(4):
            begin = shift + (tap - 2) * dilation
            total += conv_w[number, tap : tap + 1, :] * source[begin : begin + count]
        if FORE[number + 1]:
            total = keep_inside(total, place, FORE[number + 1], rows)
        target[:count] = total
        if count < target.shape[0]:
            target[count:] = jnp.zeros((target.shape[0] - count, width), F32)
        source = target
    gate = gate_pre[...]
    level_3[...] = source[...].astype(BF16)
    gated[...] = (source[...] * (gate / (1.0 + jnp.exp(-gate)))).astype(BF16)


def flip_kernel(place, block, flipped):
    flipped[...] = dot(anti_identity(block.shape[0]), block[...]).astype(BF16)


def norm_grad_kernel(channels, place, *refs):
    own, mirrored = refs[:channels], refs[channels : 2 * channels]
    *weights, out = refs[2 * channels :]
    me = place[1]
    rows, width = own[0].shape
    for block, cotangents in enumerate((own, mirrored)):
        for i in range(channels):
            total = jnp.zeros((rows, width), F32)
            for j in range(channels):
                total += dot(cotangents[j][...], weights[j][part(i ^ me, width), :], LAST_DOT)
            out[block * rows : (block + 1) * rows, i * width : (i + 1) * width] = total.astype(BF16)


def combine_kernel(channels, place, *refs):
    own, mirrored = refs[:channels], refs[channels : 2 * channels]
    grad_norm, choose, gain, gate_pre, level_3 = refs[2 * channels : 2 * channels + 5]
    normalized, upstream, grad_gate_pre, first, second, gains, grad_gated = refs[2 * channels + 5 :]
    me = place[1]
    rows, width = own[0].shape
    full = channels * width
    tile = rows // 4
    for j in range(channels):
        gains[:, j * width : (j + 1) * width] = gain[:, part(me ^ j, width)]
    for block, (here, there) in enumerate(((own, mirrored), (mirrored, own))):
        for k in range(4):
            at = slice(k * tile, (k + 1) * tile)
            mine = jnp.concatenate([ref[at, :] for ref in here], axis=1)
            other = jnp.concatenate([ref[at, :] for ref in there], axis=1)
            combined = mine.astype(F32) + dot(other, choose[...])
            mean = jnp.sum(combined * combined, axis=1, keepdims=True) * (1.0 / full)
            inv_scale = lax.rsqrt(mean + EPSILON)
            hat = combined * inv_scale
            at_both = slice(block * rows + k * tile, block * rows + (k + 1) * tile)
            normalized[at_both, :] = (hat * gains[...]).astype(BF16)
            scaled = grad_norm[at_both, :].astype(F32) * gains[...]
            row_total = jnp.sum(scaled * hat, axis=1, keepdims=True) * (1.0 / full)
            if block == 0:
                grad_gated[at, :] = inv_scale * (scaled[:, :width] - hat[:, :width] * row_total)
            else:
                grad_comb = (inv_scale * (scaled - hat * row_total)).astype(BF16)
                grad_gated[at, :] += dot(grad_comb, choose[:width, :], LAST_DOT)
    gate = gate_pre[...]
    sigmoid = 1.0 / (1.0 + jnp.exp(-gate))
    total = grad_gated[...]
    upstream[...] = (total * (gate * sigmoid)).astype(BF16)
    grad_gate_pre[...] = (total * level_3[...].astype(F32) * sigmoid * (1.0 + gate * (1.0 - sigmoid))).astype(BF16)
    odd, far = place[0] % 2, rows - EDGE
    first[...] = upstream[pl.ds(pl.multiple_of((1 - odd) * far, 16), EDGE), :]
    second[...] = upstream[pl.ds(pl.multiple_of(odd * far, 16), EDGE), :]


def output_kernel(channels, place, normalized, w_out, block_in, output):
    me = place[1]
    rows, width = block_in.shape
    total = block_in[...].astype(F32)
    for j in range(channels):
        total += dot(normalized[:rows, j * width : (j + 1) * width], w_out[part(me ^ j, width), :])
    output[...] = total.astype(BF16)


def products_kernel(channels, place, normalized, cotangent, mirrored_cotangent, grad_gate_pre, *refs):
    mains = refs[:channels]
    out_sent, out_kept, gate_sent, gate_kept, whole_out, whole_gate = refs[channels:]
    me, side = place[1], (place[0] // 2) % 2
    rows, width = cotangent.shape
    for j in range(channels // 2):
        block = (side * (channels // 2) + j) ^ me
        columns = part(block, width)
        whole_out[j * width : (j + 1) * width, :] = dot(
            normalized[:rows, columns], cotangent[...], ROWS_DOT
        ) + dot(normalized[rows:, columns], mirrored_cotangent[...], ROWS_DOT)
    half = whole_out.shape[0] // 2
    bit = place[0] % 2
    out_sent[...] = whole_out[part(1 - bit, half), :].astype(BF16)
    out_kept[...] = whole_out[part(bit, half), :]
    for j in range(channels):
        whole_gate[part(me ^ j, width), :] = dot(mains[j][...], grad_gate_pre[...], ROWS_DOT)
    half = whole_gate.shape[0] // 2
    gate_sent[...] = whole_gate[part(1 - bit, half), :].astype(BF16)
    gate_kept[...] = whole_gate[part(bit, half), :]


def backward_kernel(channels, place, upstream, first, second, conv_w, *refs):
    mains, (saved, sent, kept, whole, grad_3, grad_2, grad_1, levels) = refs[:channels], refs[channels:]
    levels[...] = saved[...].astype(F32)
    me, odd = place[1], place[0] % 2
    rows, width = upstream.shape
    fore = BACK_FORE[3]
    even = (odd == 0).astype(F32)
    early, late = first[...].astype(F32), second[...].astype(F32)
    grad_3[:fore] = (early * (1.0 - even) + late * even)[EDGE - fore :]
    grad_3[fore : fore + rows] = upstream[...].astype(F32)
    grad_3[fore + rows :] = early * even + late * (1.0 - even)
    half = whole.shape[0] // 2
    for top in (half - SPARE, 2 * half - SPARE):
        whole[top : top + SPARE, :] = jnp.zeros((SPARE, width), F32)
    grads = (None, grad_1, grad_2, grad_3)
    grad_0 = None
    for number in (2, 1, 0):
        dilation, source = DILATIONS[number], grads[number + 1]
        top = sum(saved_rows(rows, below) for below in range(number))
        fore = BACK_FORE[number + 1]
        here = source[fore : fore + rows]
        for tap in range(4):
            begin = top + FORE[number] + (tap - 2) * dilation
            row = half - SPARE + 4 * number + tap
            whole[row : row + 1, :] = jnp.sum(here * levels[begin : begin + rows], axis=0, keepdims=True)
        count = BACK_FORE[number] + rows + BACK_AFT[number]
        total = jnp.zeros((count, width), F32)
        for tap in range(4):
            begin = fore - BACK_FORE[number] - (tap - 2) * dilation
            total += conv_w[number, tap : tap + 1, :] * source[begin : begin + count]
        if number:
            grads[number][...] = keep_inside(total, place, BACK_FORE[number], rows)
        else:
            grad_0 = total.astype(BF16)
    for j in range(channels):
        block = me ^ j
        start = (block // (channels // 2)) * half + (block % (channels // 2)) * width
        whole[pl.ds(pl.multiple_of(start, SPARE), width), :] = dot(mains[j][...], grad_0, ROWS_DOT)
    sent[...] = whole[part(1 - odd, half), :].astype(BF16)
    kept[...] = whole[part(odd, half), :]


def split(total, bit):
    half = total.shape[0] // 2
    low, high = total[:half], total[half:]
    first = jnp.broadcast_to(bit, low.shape) == 0
    return jnp.where(first, high, low), jnp.where(first, low, high)


def join(mine, other, bit):
    first = jnp.broadcast_to(bit, mine.shape) == 0
    return jnp.where(first, mine, other), jnp.where(first, other, mine)


def step_kernel(plan, place, *refs):
    sources, targets = refs[: 2 * len(plan)], list(refs[2 * len(plan) :])
    for k, (done, after) in enumerate(plan):
        mine, other = sources[2 * k][...].astype(F32), sources[2 * k + 1][...].astype(F32)
        if done[0] == "halve":
            total = mine + other
        else:
            low, high = join(mine, other, (place[0] // done[1]) % 2)
            if after is not None and after[0] == "take":
                grad, taps = targets.pop(0), targets.pop(0)
                count = low.shape[0] - SPARE
                grad[:count] = low[:count].astype(BF16)
                grad[count:] = high[:count].astype(BF16)
                taps[...] = low[count : count + taps.shape[0]]
                continue
            total = jnp.concatenate([low, high], axis=0)
        if after is not None and after[0] == "halve":
            sent, kept = split(total, (place[0] // after[1]) % 2)
            targets.pop(0)[...] = sent.astype(BF16)
            targets.pop(0)[...] = kept
        else:
            targets.pop(0)[...] = total.astype(BF16)


def advance(place, items, taps):
    width = items[0][2].shape[1]
    outs, counts = [], []
    for done, after, mine, _ in items:
        rows = mine.shape[0] * (1 if done[0] == "halve" else 2)
        if after is not None and after[0] == "halve":
            outs += [((rows // 2, width), BF16), ((rows // 2, width), F32)]
            counts.append(2)
        elif after is not None and after[0] == "take":
            outs += [((rows - 2 * SPARE, width), BF16), ((taps, width), F32)]
            counts.append(2)
        else:
            outs.append(((rows, width), BF16))
            counts.append(1)
    arrays = [array for item in items for array in item[2:]]
    plan = [item[:2] for item in items]
    if all(shape[0] % 8 == 0 or shape[0] == taps for shape, _ in outs) and all(x.shape[0] % 8 == 0 for x in arrays):
        results = run(functools.partial(step_kernel, plan), place, arrays, outs)
    else:
        results = []
        for done, after, mine, other in items:
            mine, other = mine.astype(F32), other.astype(F32)
            if done[0] == "halve":
                total = mine + other
            else:
                total = jnp.concatenate(join(mine, other, seq_bit(done[1])), axis=0)
            if after is not None and after[0] == "halve":
                sent, kept = split(total, seq_bit(after[1]))
                results += [sent.astype(BF16), kept]
            elif after is not None and after[0] == "take":
                half = total.shape[0] // 2
                results += [
                    jnp.concatenate([total[: half - SPARE], total[half:-SPARE]], axis=0).astype(BF16),
                    total[half - SPARE : half - SPARE + taps],
                ]
            else:
                results.append(total.astype(BF16))
    grouped = []
    for count in counts:
        grouped.append(results[:count])
        results = results[count:]
    return grouped


def exchange(block, axis, distance):
    count = lax.axis_size(axis)
    return lax.ppermute(block, axis, [(i, i ^ distance) for i in range(count)])


def distances(axis):
    return [1 << bit for bit in range(lax.axis_size(axis).bit_length() - 1)]


def mirror(block):
    count = lax.axis_size("seq")
    return lax.ppermute(block, "seq", [(i, count - 1 - i) for i in range(count)])


def swap_edges(first, second, far=0):
    count, channels = lax.axis_size("seq"), lax.axis_size("ch")
    received = []
    for turn, block in enumerate((first, second)):
        route = []
        for low in range(turn, count - 1, 2):
            for c in range(channels):
                route.append((low * channels + c, (low + 1) * channels + (c ^ far)))
                route.append(((low + 1) * channels + c, low * channels + (c ^ far)))
        received.append(lax.ppermute(block, ("seq", "ch"), route))
    return received


def together(*values):
    return lax.optimization_barrier(values)


def seq_bit(distance):
    return (lax.axis_index("seq") & distance) // distance


def local(tokens, hidden, embedding, w_in, w_gate, conv_w, channel_order, gain, w_out, cotangent):
    rows, width = hidden.shape
    full = gain.shape[0]
    channels = full // width
    cross = channels // 2
    taps = conv_w.shape[0] * conv_w.shape[1]
    steps = distances("seq")
    block = ((rows, width), BF16)
    place = jnp.stack([lax.axis_index("seq"), lax.axis_index("ch"), lax.axis_size("seq")]).astype(jnp.int32)

    cotangent_x = exchange(cotangent, "ch", cross)
    mirrored_cotangent = mirror(cotangent)
    inputs = (tokens.reshape(1, rows), hidden, embedding)
    local_input, first, second = run(
        input_kernel,
        place,
        inputs,
        [block, ((EDGE, width), BF16), ((EDGE, width), BF16)],
        [pltpu.VMEM((16, width), F32), *fetch_scratch(inputs)],
        megabytes=60,
        fetched=3,
    )
    input_x = exchange(local_input, "ch", cross)
    input_core = exchange(local_input, "ch", 1)
    choose = run(
        functools.partial(setup_kernel, width),
        place,
        (channel_order.reshape(1, full),),
        [((full, full), BF16)],
        gflop=2.0,
    )[0]
    first, second, cotangent_x = together(first, second, cotangent_x)
    near = swap_edges(first, second)
    first, second, mirrored_cotangent = together(first, second, mirrored_cotangent)
    far = swap_edges(first, second, cross)
    edges = jnp.concatenate(near + far, axis=0)
    early_w_out, input_x = together(w_out, input_x)
    w_out_x = exchange(early_w_out, "ch", cross)
    mirrored_cotangent = run(flip_kernel, place, (mirrored_cotangent,), [block], gflop=1.0)[0]
    mirrored_cotangent, input_core, choose = together(mirrored_cotangent, input_core, choose)
    mains = [local_input, input_core, input_x, exchange(input_x, "ch", 1)]

    projected, gate_pre, w_in_on = run(
        functools.partial(project_kernel, channels),
        place,
        (*mains, w_in, w_gate),
        [((rows, width), F32)] * 2 + [(w_in.shape, BF16)],
        gflop=6.0,
    )
    edges_core = exchange(edges, "ch", 1)
    levels, level_3, gated = run(
        functools.partial(forward_kernel, channels),
        place,
        (edges, edges_core, w_in_on, projected, gate_pre, conv_w),
        [((sum(saved_rows(rows, number) for number in range(3)), width), BF16), block, block],
        [pltpu.VMEM((saved_rows(rows, number), width), F32) for number in range(4)],
        gflop=0.4,
    )
    mirrored = run(flip_kernel, place, (mirror(gated),), [block], gflop=12.0)[0]
    gated_x = exchange(gated, "ch", cross)
    mirrored_cotangent, w_out_x = together(mirrored_cotangent, w_out_x)
    mirrored_cotangent_x = exchange(mirrored_cotangent, "ch", cross)
    mirrored, gated_x, mirrored_cotangent_x = together(mirrored, gated_x, mirrored_cotangent_x)
    mirrored_x = exchange(mirrored, "ch", cross)
    gated_all = [gated, exchange(gated, "ch", 1), gated_x, exchange(gated_x, "ch", 1)]
    cotangent_all = [cotangent, exchange(cotangent, "ch", 1), cotangent_x, exchange(cotangent_x, "ch", 1)]
    mirrored_cotangent_all = [
        mirrored_cotangent,
        exchange(mirrored_cotangent, "ch", 1),
        mirrored_cotangent_x,
        exchange(mirrored_cotangent_x, "ch", 1),
    ]
    grad_norm = run(
        functools.partial(norm_grad_kernel, channels),
        place,
        (
            *cotangent_all,
            *mirrored_cotangent_all,
            w_out,
            exchange(w_out, "ch", 1),
            w_out_x,
            exchange(w_out_x, "ch", 1),
        ),
        [((2 * rows, full), BF16)],
        gflop=2.1,
    )[0]
    mirrored_x, grad_norm = together(mirrored_x, grad_norm)
    mirrored_all = [mirrored, exchange(mirrored, "ch", 1), mirrored_x, exchange(mirrored_x, "ch", 1)]

    normalized, upstream, grad_gate_pre, first, second = run(
        functools.partial(combine_kernel, channels),
        place,
        (*gated_all, *mirrored_all, grad_norm, choose, gain.reshape(1, full), gate_pre, level_3),
        [((2 * rows, full), BF16), block, block, ((EDGE, width), BF16), ((EDGE, width), BF16)],
        [pltpu.VMEM((1, full), F32), pltpu.VMEM((rows, width), F32)],
        gflop=2.5,
    )
    first, second = swap_edges(first, second)
    out_sent, out_kept, gate_sent, gate_kept = run(
        functools.partial(products_kernel, channels),
        place,
        (normalized, cotangent, mirrored_cotangent, grad_gate_pre, *mains),
        [
            ((full // 4, width), BF16),
            ((full // 4, width), F32),
            ((full // 2, width), BF16),
            ((full // 2, width), F32),
        ],
        [pltpu.VMEM((full // 2, width), F32), pltpu.VMEM((full, width), F32)],
        gflop=0.8,
    )
    out_sent, gate_sent, first, second = together(out_sent, gate_sent, first, second)
    out_other = exchange(out_sent, "seq", steps[0])
    gate_other = exchange(gate_sent, "seq", steps[0])
    half = full // 2 + SPARE
    in_sent, in_kept = run(
        functools.partial(backward_kernel, channels),
        place,
        (upstream, first, second, conv_w, *mains, levels),
        [((half, width), BF16), ((half, width), F32)],
        [pltpu.VMEM((2 * half, width), F32)]
        + [pltpu.VMEM((BACK_FORE[k] + rows + BACK_AFT[k], width), F32) for k in (3, 2, 1)]
        + [pltpu.VMEM(levels.shape, F32)],
        gflop=0.5,
    )
    output = run(
        functools.partial(output_kernel, channels),
        place,
        (normalized, w_out, local_input),
        [block],
        gflop=0.3,
    )[0]

    down = [("halve", distance) for distance in steps]
    up = [("double", distance) for distance in steps[::-1]]
    out_down, out_up = down[:1] + down[2:], up[:-2] + up[-1:] + up[-2:-1]
    routes = [down + up + [("take",)], down + up + [None], out_down + out_up + [None]]
    in_sent, gate_other, out_other = together(in_sent, gate_other, out_other)
    results = []
    for route, sent, kept, other in zip(
        routes, (in_sent, None, None), (in_kept, gate_kept, out_kept), (None, gate_other, out_other)
    ):
        if other is None:
            other = exchange(sent, "seq", route[0][1])
        for done, upcoming in zip(route, route[1:]):
            prepared = advance(place, [(done, upcoming, kept, other)], taps)[0]
            if upcoming is not None and upcoming[0] != "take":
                sent, kept = prepared if len(prepared) == 2 else prepared * 2
                other = exchange(sent, "seq", upcoming[1])
        results.append(prepared)
    (grad_in, grad_conv), (sum_gate,), (sum_out,) = results
    grad_conv = grad_conv.reshape(conv_w.shape)
    return output, grad_in, sum_gate, sum_out, grad_conv


def solution(mesh):
    placed = (
        P("seq"),
        P("seq", "ch"),
        P(None, "ch"),
        P(None, "ch"),
        P(None, "ch"),
        P(None, None, "ch"),
        P(),
        P(),
        P(None, "ch"),
        P("seq", "ch"),
    )
    return jax.shard_map(
        local,
        mesh=mesh,
        in_specs=placed,
        out_specs=(
            P("seq", "ch"),
            P(None, "ch"),
            P(None, "ch"),
            P(None, "ch"),
            P(None, None, "ch"),
        ),
        check_vma=False,
    )
```

```python
import functools

import jax
import jax.numpy as jnp
from jax import lax
from jax.experimental import pallas as pl
from jax.experimental.pallas import tpu as pltpu
from jax.sharding import PartitionSpec as P

DILATIONS = (1, 8, 64)
EPSILON = 1e-06
FORE = (160, 144, 128, 0)
AFT = (80, 72, 64, 0)
BACK_FORE = (0, 8, 16, 80)
BACK_AFT = (0, 8, 24, 160)
EDGE = 160
SPARE = 64

BF16, F32 = jnp.bfloat16, jnp.float32
ROWS_DOT = (((0,), (0,)), ((), ()))
LAST_DOT = (((1,), (1,)), ((), ()))


def dot(left, right, dims=(((1,), (0,)), ((), ()))):
    return lax.dot_general(left, right, dims, preferred_element_type=F32)


def run(body, place, operands, outs, scratch=(), megabytes=8, gflop=0.1, fetched=0):
    moved = sum(x.size * x.dtype.itemsize for x in operands)
    return pl.pallas_call(
        body,
        out_shape=[jax.ShapeDtypeStruct(shape, dtype) for shape, dtype in outs],
        in_specs=[pl.BlockSpec(memory_space=pltpu.SMEM)]
        + [pl.BlockSpec(memory_space=pltpu.VMEM)] * (len(operands) - fetched)
        + [pl.BlockSpec(memory_space=pltpu.HBM)] * fetched,
        out_specs=[pl.BlockSpec(memory_space=pltpu.VMEM)] * len(outs),
        scratch_shapes=list(scratch),
        compiler_params=pltpu.CompilerParams(vmem_limit_bytes=megabytes << 20),
        cost_estimate=pl.CostEstimate(flops=int(gflop * 1e9), bytes_accessed=moved, transcendentals=0),
    )(place, *operands)


def fetch(sources, targets, semaphores):
    copies = [
        pltpu.make_async_copy(source, target, semaphores.at[k])
        for k, (source, target) in enumerate(zip(sources, targets))
    ]
    for copy in copies:
        copy.start()
    return copies


def fetch_scratch(operands):
    return [pltpu.VMEM(x.shape, x.dtype) for x in operands] + [pltpu.SemaphoreType.DMA((len(operands),))]


def part(index, size, multiple=None):
    return pl.ds(pl.multiple_of(index * size, multiple or size), size)


def saved_rows(rows, number):
    return -(-(FORE[number] + rows + AFT[number]) // 16) * 16


def anti_identity(rows):
    down = lax.broadcasted_iota(jnp.int32, (rows, rows), 0)
    across = lax.broadcasted_iota(jnp.int32, (rows, rows), 1)
    return (down + across == rows - 1).astype(F32).astype(BF16)


def input_kernel(place, tokens_hbm, hidden_hbm, embedding_hbm, block_in, first, second, *scratch):
    padded, tokens, hidden, embedding, semaphores = scratch
    copies = fetch((tokens_hbm, hidden_hbm, embedding_hbm), (tokens, hidden, embedding), semaphores)
    bases, rows = embedding.shape[0], hidden.shape[0]
    padded[...] = jnp.zeros_like(padded)
    for copy in copies:
        copy.wait()
    padded[:bases] = embedding[...].astype(F32)
    base = lax.broadcasted_iota(jnp.int32, (padded.shape[0], rows), 0)
    one_hot = (base == tokens[...]).astype(F32).astype(BF16)
    shift = dot(one_hot, padded[...].astype(BF16), ROWS_DOT)
    block_in[...] = (hidden[...].astype(F32) + shift).astype(BF16)
    odd, far = place[0] % 2, rows - EDGE
    first[...] = block_in[pl.ds(pl.multiple_of((1 - odd) * far, 16), EDGE), :]
    second[...] = block_in[pl.ds(pl.multiple_of(odd * far, 16), EDGE), :]


def setup_kernel(width, place, order, choose):
    me, full = place[1], order.shape[1]
    down = lax.broadcasted_iota(jnp.int32, (width, width), 0)
    for j in range(full // width):
        for i in range(full // width):
            wanted = order[:, part(me ^ i, width)]
            choose[j * width : (j + 1) * width, i * width : (i + 1) * width] = (
                (down + (me ^ j) * width == wanted).astype(F32).astype(BF16)
            )


def project_kernel(channels, place, *refs):
    mains, (w_in, w_gate, projected, gate_pre, w_in_on) = refs[:channels], refs[channels:]
    me, width = place[1], mains[0].shape[1]
    for weight, out in ((w_in, projected), (w_gate, gate_pre)):
        total = dot(mains[0][...], weight[part(me, width), :])
        for j in range(1, channels):
            total += dot(mains[j][...], weight[part(me ^ j, width), :])
        out[...] = total
    w_in_on[...] = w_in[...]


def keep_inside(total, place, before, rows):
    position = lax.broadcasted_iota(jnp.int32, total.shape, 0) + (place[0] * rows - before)
    return jnp.where((position >= 0) & (position < place[2] * rows), total, 0.0)


def forward_kernel(channels, place, edges, edges_core, w_in, projected, gate_pre, conv_w, *outs):
    levels, level_3, gated, *stages = outs
    me, odd = place[1], place[0] % 2
    rows, width = projected.shape
    left = jnp.zeros((EDGE, width), F32)
    right = jnp.zeros((AFT[0], width), F32)
    for j in range(channels):
        source = edges_core if j % 2 else edges
        base = (j // 2) * 2 * EDGE
        weight = w_in[part(me ^ j, width), :]
        left += dot(source[pl.ds(pl.multiple_of(base + (1 - odd) * EDGE, 16), EDGE), :], weight)
        right += dot(source[pl.ds(pl.multiple_of(base + odd * EDGE, 16), AFT[0]), :], weight)
    source = stages[0]
    source[:EDGE] = left
    source[EDGE : EDGE + rows] = projected[...]
    source[EDGE + rows :] = right
    top = 0
    for number, dilation in enumerate(DILATIONS):
        target = stages[number + 1]
        levels[top : top + source.shape[0], :] = source[...].astype(BF16)
        top += source.shape[0]
        shift = FORE[number] - FORE[number + 1]
        count = FORE[number + 1] + rows + AFT[number + 1]
        total = jnp.zeros((count, width), F32)
        for tap in range(4):
            begin = shift + (tap - 2) * dilation
            total += conv_w[number, tap : tap + 1, :] * source[begin : begin + count]
        if FORE[number + 1]:
            total = keep_inside(total, place, FORE[number + 1], rows)
        target[:count] = total
        if count < target.shape[0]:
            target[count:] = jnp.zeros((target.shape[0] - count, width), F32)
        source = target
    gate = gate_pre[...]
    level_3[...] = source[...].astype(BF16)
    gated[...] = (source[...] * (gate / (1.0 + jnp.exp(-gate)))).astype(BF16)


def flip_kernel(place, block, flipped):
    flipped[...] = dot(anti_identity(block.shape[0]), block[...]).astype(BF16)


def norm_grad_kernel(channels, place, *refs):
    own, mirrored = refs[:channels], refs[channels : 2 * channels]
    *weights, out = refs[2 * channels :]
    me = place[1]
    rows, width = own[0].shape
    for block, cotangents in enumerate((own, mirrored)):
        for i in range(channels):
            total = jnp.zeros((rows, width), F32)
            for j in range(channels):
                total += dot(cotangents[j][...], weights[j][part(i ^ me, width), :], LAST_DOT)
            out[block * rows : (block + 1) * rows, i * width : (i + 1) * width] = total.astype(BF16)


def combine_kernel(channels, place, *refs):
    own, mirrored = refs[:channels], refs[channels : 2 * channels]
    grad_norm, choose, gain, gate_pre, level_3 = refs[2 * channels : 2 * channels + 5]
    normalized, upstream, grad_gate_pre, first, second, gains, grad_gated = refs[2 * channels + 5 :]
    me = place[1]
    rows, width = own[0].shape
    full = channels * width
    tile = rows // 4
    for j in range(channels):
        gains[:, j * width : (j + 1) * width] = gain[:, part(me ^ j, width)]
    for block, (here, there) in enumerate(((own, mirrored), (mirrored, own))):
        for k in range(4):
            at = slice(k * tile, (k + 1) * tile)
            mine = jnp.concatenate([ref[at, :] for ref in here], axis=1)
            other = jnp.concatenate([ref[at, :] for ref in there], axis=1)
            combined = mine.astype(F32) + dot(other, choose[...])
            mean = jnp.sum(combined * combined, axis=1, keepdims=True) * (1.0 / full)
            inv_scale = lax.rsqrt(mean + EPSILON)
            hat = combined * inv_scale
            at_both = slice(block * rows + k * tile, block * rows + (k + 1) * tile)
            normalized[at_both, :] = (hat * gains[...]).astype(BF16)
            scaled = grad_norm[at_both, :].astype(F32) * gains[...]
            row_total = jnp.sum(scaled * hat, axis=1, keepdims=True) * (1.0 / full)
            if block == 0:
                grad_gated[at, :] = inv_scale * (scaled[:, :width] - hat[:, :width] * row_total)
            else:
                grad_comb = (inv_scale * (scaled - hat * row_total)).astype(BF16)
                grad_gated[at, :] += dot(grad_comb, choose[:width, :], LAST_DOT)
    gate = gate_pre[...]
    sigmoid = 1.0 / (1.0 + jnp.exp(-gate))
    total = grad_gated[...]
    upstream[...] = (total * (gate * sigmoid)).astype(BF16)
    grad_gate_pre[...] = (total * level_3[...].astype(F32) * sigmoid * (1.0 + gate * (1.0 - sigmoid))).astype(BF16)
    odd, far = place[0] % 2, rows - EDGE
    first[...] = upstream[pl.ds(pl.multiple_of((1 - odd) * far, 16), EDGE), :]
    second[...] = upstream[pl.ds(pl.multiple_of(odd * far, 16), EDGE), :]


def output_kernel(channels, place, normalized, w_out, block_in, output):
    me = place[1]
    rows, width = block_in.shape
    total = block_in[...].astype(F32)
    for j in range(channels):
        total += dot(normalized[:rows, j * width : (j + 1) * width], w_out[part(me ^ j, width), :])
    output[...] = total.astype(BF16)


def products_kernel(channels, place, normalized, cotangent, mirrored_cotangent, grad_gate_pre, *refs):
    mains = refs[:channels]
    out_sent, out_kept, gate_sent, gate_kept, whole_out, whole_gate = refs[channels:]
    me, side = place[1], (place[0] // 2) % 2
    rows, width = cotangent.shape
    for j in range(channels // 2):
        block = (side * (channels // 2) + j) ^ me
        columns = part(block, width)
        whole_out[j * width : (j + 1) * width, :] = dot(
            normalized[:rows, columns], cotangent[...], ROWS_DOT
        ) + dot(normalized[rows:, columns], mirrored_cotangent[...], ROWS_DOT)
    half = whole_out.shape[0] // 2
    bit = place[0] % 2
    out_sent[...] = whole_out[part(1 - bit, half), :].astype(BF16)
    out_kept[...] = whole_out[part(bit, half), :]
    for j in range(channels):
        whole_gate[part(me ^ j, width), :] = dot(mains[j][...], grad_gate_pre[...], ROWS_DOT)
    half = whole_gate.shape[0] // 2
    gate_sent[...] = whole_gate[part(1 - side, half), :].astype(BF16)
    gate_kept[...] = whole_gate[part(side, half), :]


def backward_kernel(channels, place, upstream, first, second, conv_w, *refs):
    mains, (saved, sent, kept, whole, grad_3, grad_2, grad_1, levels) = refs[:channels], refs[channels:]
    levels[...] = saved[...].astype(F32)
    me, odd = place[1], place[0] % 2
    rows, width = upstream.shape
    fore = BACK_FORE[3]
    even = (odd == 0).astype(F32)
    early, late = first[...].astype(F32), second[...].astype(F32)
    grad_3[:fore] = (early * (1.0 - even) + late * even)[EDGE - fore :]
    grad_3[fore : fore + rows] = upstream[...].astype(F32)
    grad_3[fore + rows :] = early * even + late * (1.0 - even)
    half = whole.shape[0] // 2
    for top in (half - SPARE, 2 * half - SPARE):
        whole[top : top + SPARE, :] = jnp.zeros((SPARE, width), F32)
    grads = (None, grad_1, grad_2, grad_3)
    grad_0 = None
    for number in (2, 1, 0):
        dilation, source = DILATIONS[number], grads[number + 1]
        top = sum(saved_rows(rows, below) for below in range(number))
        fore = BACK_FORE[number + 1]
        here = source[fore : fore + rows]
        for tap in range(4):
            begin = top + FORE[number] + (tap - 2) * dilation
            row = half - SPARE + 4 * number + tap
            whole[row : row + 1, :] = jnp.sum(here * levels[begin : begin + rows], axis=0, keepdims=True)
        count = BACK_FORE[number] + rows + BACK_AFT[number]
        total = jnp.zeros((count, width), F32)
        for tap in range(4):
            begin = fore - BACK_FORE[number] - (tap - 2) * dilation
            total += conv_w[number, tap : tap + 1, :] * source[begin : begin + count]
        if number:
            grads[number][...] = keep_inside(total, place, BACK_FORE[number], rows)
        else:
            grad_0 = total.astype(BF16)
    for j in range(channels):
        block = me ^ j
        start = (block // (channels // 2)) * half + (block % (channels // 2)) * width
        whole[pl.ds(pl.multiple_of(start, SPARE), width), :] = dot(mains[j][...], grad_0, ROWS_DOT)
    sent[...] = whole[part(1 - odd, half), :].astype(BF16)
    kept[...] = whole[part(odd, half), :]


def split(total, bit):
    half = total.shape[0] // 2
    low, high = total[:half], total[half:]
    first = jnp.broadcast_to(bit, low.shape) == 0
    return jnp.where(first, high, low), jnp.where(first, low, high)


def join(mine, other, bit):
    first = jnp.broadcast_to(bit, mine.shape) == 0
    return jnp.where(first, mine, other), jnp.where(first, other, mine)


def step_kernel(plan, place, *refs):
    sources, targets = refs[: 2 * len(plan)], list(refs[2 * len(plan) :])
    for k, (done, after) in enumerate(plan):
        mine, other = sources[2 * k][...].astype(F32), sources[2 * k + 1][...].astype(F32)
        if done[0] == "halve":
            total = mine + other
        else:
            low, high = join(mine, other, (place[0] // done[1]) % 2)
            if after is not None and after[0] == "take":
                grad, taps = targets.pop(0), targets.pop(0)
                count = low.shape[0] - SPARE
                grad[:count] = low[:count].astype(BF16)
                grad[count:] = high[:count].astype(BF16)
                for number in range(taps.shape[0]):
                    start = count + number * taps.shape[1]
                    taps[number] = low[start : start + taps.shape[1]]
                continue
            total = jnp.concatenate([low, high], axis=0)
        if after is not None and after[0] == "halve":
            sent, kept = split(total, (place[0] // after[1]) % 2)
            targets.pop(0)[...] = sent.astype(BF16)
            targets.pop(0)[...] = kept
        else:
            targets.pop(0)[...] = total.astype(BF16)


def advance(place, items, taps):
    width = items[0][2].shape[1]
    outs, counts = [], []
    for done, after, mine, _ in items:
        rows = mine.shape[0] * (1 if done[0] == "halve" else 2)
        if after is not None and after[0] == "halve":
            outs += [((rows // 2, width), BF16), ((rows // 2, width), F32)]
            counts.append(2)
        elif after is not None and after[0] == "take":
            outs += [((rows - 2 * SPARE, width), BF16), ((*taps, width), F32)]
            counts.append(2)
        else:
            outs.append(((rows, width), BF16))
            counts.append(1)
    arrays = [array for item in items for array in item[2:]]
    plan = [item[:2] for item in items]
    if all(shape[0] % 8 == 0 or len(shape) == 3 for shape, _ in outs) and all(x.shape[0] % 8 == 0 for x in arrays):
        results = run(functools.partial(step_kernel, plan), place, arrays, outs)
    else:
        results = []
        for done, after, mine, other in items:
            mine, other = mine.astype(F32), other.astype(F32)
            if done[0] == "halve":
                total = mine + other
            else:
                total = jnp.concatenate(join(mine, other, seq_bit(done[1])), axis=0)
            if after is not None and after[0] == "halve":
                sent, kept = split(total, seq_bit(after[1]))
                results += [sent.astype(BF16), kept]
            elif after is not None and after[0] == "take":
                half = total.shape[0] // 2
                results += [
                    jnp.concatenate([total[: half - SPARE], total[half:-SPARE]], axis=0).astype(BF16),
                    total[half - SPARE : half - SPARE + taps[0] * taps[1]].reshape(*taps, width),
                ]
            else:
                results.append(total.astype(BF16))
    grouped = []
    for count in counts:
        grouped.append(results[:count])
        results = results[count:]
    return grouped


def exchange(block, axis, distance):
    count = lax.axis_size(axis)
    return lax.ppermute(block, axis, [(i, i ^ distance) for i in range(count)])


def distances(axis):
    return [1 << bit for bit in range(lax.axis_size(axis).bit_length() - 1)]


def mirror(block):
    count = lax.axis_size("seq")
    return lax.ppermute(block, "seq", [(i, count - 1 - i) for i in range(count)])


def swap_edges(first, second, far=0):
    count, channels = lax.axis_size("seq"), lax.axis_size("ch")
    received = []
    for turn, block in enumerate((first, second)):
        route = []
        for low in range(turn, count - 1, 2):
            for c in range(channels):
                route.append((low * channels + c, (low + 1) * channels + (c ^ far)))
                route.append(((low + 1) * channels + c, low * channels + (c ^ far)))
        received.append(lax.ppermute(block, ("seq", "ch"), route))
    return received


def together(*values):
    return lax.optimization_barrier(values)


def seq_bit(distance):
    return (lax.axis_index("seq") & distance) // distance


def local(tokens, hidden, embedding, w_in, w_gate, conv_w, channel_order, gain, w_out, cotangent):
    rows, width = hidden.shape
    full = gain.shape[0]
    channels = full // width
    cross = channels // 2
    steps = distances("seq")
    block = ((rows, width), BF16)
    place = jnp.stack([lax.axis_index("seq"), lax.axis_index("ch"), lax.axis_size("seq")]).astype(jnp.int32)

    cotangent_x = exchange(cotangent, "ch", cross)
    mirrored_cotangent = mirror(cotangent)
    inputs = (tokens.reshape(1, rows), hidden, embedding)
    local_input, first, second = run(
        input_kernel,
        place,
        inputs,
        [block, ((EDGE, width), BF16), ((EDGE, width), BF16)],
        [pltpu.VMEM((16, width), F32), *fetch_scratch(inputs)],
        megabytes=60,
        fetched=3,
    )
    input_x = exchange(local_input, "ch", cross)
    input_core = exchange(local_input, "ch", 1)
    choose = run(
        functools.partial(setup_kernel, width),
        place,
        (channel_order.reshape(1, full),),
        [((full, full), BF16)],
        gflop=2.0,
    )[0]
    first, second, early_w_out, cotangent_x = together(first, second, w_out, cotangent_x)
    near = swap_edges(first, second)
    first, second, mirrored_cotangent = together(first, second, mirrored_cotangent)
    far = swap_edges(first, second, cross)
    edges = jnp.concatenate(near + far, axis=0)
    w_out_x = exchange(early_w_out, "ch", cross)
    mirrored_cotangent = run(flip_kernel, place, (mirrored_cotangent,), [block], gflop=1.0)[0]
    mirrored_cotangent, input_core, choose = together(mirrored_cotangent, input_core, choose)
    mains = [local_input, input_core, input_x, exchange(input_x, "ch", 1)]

    projected, gate_pre, w_in_on = run(
        functools.partial(project_kernel, channels),
        place,
        (*mains, w_in, w_gate),
        [((rows, width), F32)] * 2 + [(w_in.shape, BF16)],
        gflop=6.0,
    )
    edges_core = exchange(edges, "ch", 1)
    levels, level_3, gated = run(
        functools.partial(forward_kernel, channels),
        place,
        (edges, edges_core, w_in_on, projected, gate_pre, conv_w),
        [((sum(saved_rows(rows, number) for number in range(3)), width), BF16), block, block],
        [pltpu.VMEM((saved_rows(rows, number), width), F32) for number in range(4)],
        gflop=0.4,
    )
    mirrored_cotangent, w_out_x = together(mirrored_cotangent, w_out_x)
    mirrored_cotangent_x = exchange(mirrored_cotangent, "ch", cross)
    mirrored, mirrored_cotangent_x = together(mirror(gated), mirrored_cotangent_x)
    mirrored = run(flip_kernel, place, (mirrored,), [block], gflop=12.0)[0]
    gated_x = exchange(gated, "ch", cross)
    mirrored, gated_x = together(mirrored, gated_x)
    mirrored_x = exchange(mirrored, "ch", cross)
    gated_all = [gated, exchange(gated, "ch", 1), gated_x, exchange(gated_x, "ch", 1)]
    cotangent_all = [cotangent, exchange(cotangent, "ch", 1), cotangent_x, exchange(cotangent_x, "ch", 1)]
    mirrored_cotangent_all = [
        mirrored_cotangent,
        exchange(mirrored_cotangent, "ch", 1),
        mirrored_cotangent_x,
        exchange(mirrored_cotangent_x, "ch", 1),
    ]
    grad_norm = run(
        functools.partial(norm_grad_kernel, channels),
        place,
        (
            *cotangent_all,
            *mirrored_cotangent_all,
            w_out,
            exchange(w_out, "ch", 1),
            w_out_x,
            exchange(w_out_x, "ch", 1),
        ),
        [((2 * rows, full), BF16)],
        gflop=2.1,
    )[0]
    mirrored_x, grad_norm = together(mirrored_x, grad_norm)
    mirrored_all = [mirrored, exchange(mirrored, "ch", 1), mirrored_x, exchange(mirrored_x, "ch", 1)]

    normalized, upstream, grad_gate_pre, first, second = run(
        functools.partial(combine_kernel, channels),
        place,
        (*gated_all, *mirrored_all, grad_norm, choose, gain.reshape(1, full), gate_pre, level_3),
        [((2 * rows, full), BF16), block, block, ((EDGE, width), BF16), ((EDGE, width), BF16)],
        [pltpu.VMEM((1, full), F32), pltpu.VMEM((rows, width), F32)],
        gflop=2.5,
    )
    first, second = swap_edges(first, second)
    out_sent, out_kept, gate_sent, gate_kept = run(
        functools.partial(products_kernel, channels),
        place,
        (normalized, cotangent, mirrored_cotangent, grad_gate_pre, *mains),
        [
            ((full // 4, width), BF16),
            ((full // 4, width), F32),
            ((full // 2, width), BF16),
            ((full // 2, width), F32),
        ],
        [pltpu.VMEM((full // 2, width), F32), pltpu.VMEM((full, width), F32)],
        gflop=0.8,
    )
    out_sent, gate_sent, first, second = together(out_sent, gate_sent, first, second)
    out_other = exchange(out_sent, "seq", steps[0])
    gate_other = exchange(gate_sent, "seq", steps[1])
    half = full // 2 + SPARE
    in_sent, in_kept = run(
        functools.partial(backward_kernel, channels),
        place,
        (upstream, first, second, conv_w, *mains, levels),
        [((half, width), BF16), ((half, width), F32)],
        [pltpu.VMEM((2 * half, width), F32)]
        + [pltpu.VMEM((BACK_FORE[k] + rows + BACK_AFT[k], width), F32) for k in (3, 2, 1)]
        + [pltpu.VMEM(levels.shape, F32)],
        gflop=0.5,
    )
    output = run(
        functools.partial(output_kernel, channels),
        place,
        (normalized, w_out, local_input),
        [block],
        gflop=0.3,
    )[0]

    down = [("halve", distance) for distance in steps]
    up = [("double", distance) for distance in steps[::-1]]
    out_down, out_up = down[:1] + down[2:], up[:-2] + up[-1:] + up[-2:-1]
    gate_down, gate_up = down[1:] + down[:1], up[-1:] + up[:-1]
    routes = [down + up + [("take",)], gate_down + gate_up + [None], out_down + out_up + [None]]
    in_sent, out_other = together(in_sent, out_other)
    results = []
    for route, sent, kept, other in zip(
        routes, (in_sent, None, None), (in_kept, gate_kept, out_kept), (None, gate_other, out_other)
    ):
        if other is None:
            other = exchange(sent, "seq", route[0][1])
        elif len(results) == 1:
            other = gate_other
        for number, (done, upcoming) in enumerate(zip(route, route[1:])):
            prepared = advance(place, [(done, upcoming, kept, other)], conv_w.shape[:2])[0]
            if upcoming is not None and upcoming[0] != "take":
                sent, kept = prepared if len(prepared) == 2 else prepared * 2
                if not results and number == 0:
                    sent, gate_other = together(sent, gate_other)
                other = exchange(sent, "seq", upcoming[1])
        results.append(prepared)
    (grad_in, grad_conv), (sum_gate,), (sum_out,) = results
    return output, grad_in, sum_gate, sum_out, grad_conv


def solution(mesh):
    placed = (
        P("seq"),
        P("seq", "ch"),
        P(None, "ch"),
        P(None, "ch"),
        P(None, "ch"),
        P(None, None, "ch"),
        P(),
        P(),
        P(None, "ch"),
        P("seq", "ch"),
    )
    return jax.shard_map(
        local,
        mesh=mesh,
        in_specs=placed,
        out_specs=(
            P("seq", "ch"),
            P(None, "ch"),
            P(None, "ch"),
            P(None, "ch"),
            P(None, None, "ch"),
        ),
        check_vma=False,
    )
```

```python
import functools

import jax
import jax.numpy as jnp
from jax import lax
from jax.experimental import pallas as pl
from jax.experimental.pallas import tpu as pltpu
from jax.sharding import PartitionSpec as P

DILATIONS = (1, 8, 64)
EPSILON = 1e-06
FORE = (160, 144, 128, 0)
AFT = (80, 72, 64, 0)
BACK_FORE = (0, 8, 16, 80)
BACK_AFT = (0, 8, 24, 160)
EDGE = 160
SPARE = 64

BF16, F32 = jnp.bfloat16, jnp.float32
ROWS_DOT = (((0,), (0,)), ((), ()))
LAST_DOT = (((1,), (1,)), ((), ()))


def dot(left, right, dims=(((1,), (0,)), ((), ()))):
    return lax.dot_general(left, right, dims, preferred_element_type=F32)


def run(body, place, operands, outs, scratch=(), megabytes=8, gflop=0.1, fetched=0):
    moved = sum(x.size * x.dtype.itemsize for x in operands)
    return pl.pallas_call(
        body,
        out_shape=[jax.ShapeDtypeStruct(shape, dtype) for shape, dtype in outs],
        in_specs=[pl.BlockSpec(memory_space=pltpu.SMEM)]
        + [pl.BlockSpec(memory_space=pltpu.VMEM)] * (len(operands) - fetched)
        + [pl.BlockSpec(memory_space=pltpu.HBM)] * fetched,
        out_specs=[pl.BlockSpec(memory_space=pltpu.VMEM)] * len(outs),
        scratch_shapes=list(scratch),
        compiler_params=pltpu.CompilerParams(vmem_limit_bytes=megabytes << 20),
        cost_estimate=pl.CostEstimate(flops=int(gflop * 1e9), bytes_accessed=moved, transcendentals=0),
    )(place, *operands)


def fetch(sources, targets, semaphores):
    copies = [
        pltpu.make_async_copy(source, target, semaphores.at[k])
        for k, (source, target) in enumerate(zip(sources, targets))
    ]
    for copy in copies:
        copy.start()
    return copies


def fetch_scratch(operands):
    return [pltpu.VMEM(x.shape, x.dtype) for x in operands] + [pltpu.SemaphoreType.DMA((len(operands),))]


def part(index, size, multiple=None):
    return pl.ds(pl.multiple_of(index * size, multiple or size), size)


def saved_rows(rows, number):
    return -(-(FORE[number] + rows + AFT[number]) // 16) * 16


def anti_identity(rows):
    down = lax.broadcasted_iota(jnp.int32, (rows, rows), 0)
    across = lax.broadcasted_iota(jnp.int32, (rows, rows), 1)
    return (down + across == rows - 1).astype(F32).astype(BF16)


def input_kernel(place, tokens_hbm, hidden_hbm, embedding_hbm, block_in, first, second, *scratch):
    padded, tokens, hidden, embedding, semaphores = scratch
    copies = fetch((tokens_hbm, hidden_hbm, embedding_hbm), (tokens, hidden, embedding), semaphores)
    bases, rows = embedding.shape[0], hidden.shape[0]
    padded[...] = jnp.zeros_like(padded)
    for copy in copies:
        copy.wait()
    padded[:bases] = embedding[...].astype(F32)
    base = lax.broadcasted_iota(jnp.int32, (padded.shape[0], rows), 0)
    one_hot = (base == tokens[...]).astype(F32).astype(BF16)
    shift = dot(one_hot, padded[...].astype(BF16), ROWS_DOT)
    block_in[...] = (hidden[...].astype(F32) + shift).astype(BF16)
    odd, far = place[0] % 2, rows - EDGE
    first[...] = block_in[pl.ds(pl.multiple_of((1 - odd) * far, 16), EDGE), :]
    second[...] = block_in[pl.ds(pl.multiple_of(odd * far, 16), EDGE), :]


def setup_kernel(width, place, order, choose):
    me, full = place[1], order.shape[1]
    down = lax.broadcasted_iota(jnp.int32, (width, width), 0)
    for j in range(full // width):
        for i in range(full // width):
            wanted = order[:, part(me ^ i, width)]
            choose[j * width : (j + 1) * width, i * width : (i + 1) * width] = (
                (down + (me ^ j) * width == wanted).astype(F32).astype(BF16)
            )


def project_kernel(channels, place, *refs):
    mains, (w_in, w_gate, projected, gate_pre, w_in_on) = refs[:channels], refs[channels:]
    me, width = place[1], mains[0].shape[1]
    for weight, out in ((w_in, projected), (w_gate, gate_pre)):
        total = dot(mains[0][...], weight[part(me, width), :])
        for j in range(1, channels):
            total += dot(mains[j][...], weight[part(me ^ j, width), :])
        out[...] = total
    w_in_on[...] = w_in[...]


def keep_inside(total, place, before, rows):
    position = lax.broadcasted_iota(jnp.int32, total.shape, 0) + (place[0] * rows - before)
    return jnp.where((position >= 0) & (position < place[2] * rows), total, 0.0)


def forward_kernel(channels, place, edges, edges_core, w_in, projected, gate_pre, conv_w, *outs):
    levels, level_3, gated, *stages = outs
    me, odd = place[1], place[0] % 2
    rows, width = projected.shape
    left = jnp.zeros((EDGE, width), F32)
    right = jnp.zeros((AFT[0], width), F32)
    for j in range(channels):
        source = edges_core if j % 2 else edges
        base = (j // 2) * 2 * EDGE
        weight = w_in[part(me ^ j, width), :]
        left += dot(source[pl.ds(pl.multiple_of(base + (1 - odd) * EDGE, 16), EDGE), :], weight)
        right += dot(source[pl.ds(pl.multiple_of(base + odd * EDGE, 16), AFT[0]), :], weight)
    source = stages[0]
    source[:EDGE] = left
    source[EDGE : EDGE + rows] = projected[...]
    source[EDGE + rows :] = right
    top = 0
    for number, dilation in enumerate(DILATIONS):
        target = stages[number + 1]
        levels[top : top + source.shape[0], :] = source[...].astype(BF16)
        top += source.shape[0]
        shift = FORE[number] - FORE[number + 1]
        count = FORE[number + 1] + rows + AFT[number + 1]
        total = jnp.zeros((count, width), F32)
        for tap in range(4):
            begin = shift + (tap - 2) * dilation
            total += conv_w[number, tap : tap + 1, :] * source[begin : begin + count]
        if FORE[number + 1]:
            total = keep_inside(total, place, FORE[number + 1], rows)
        target[:count] = total
        if count < target.shape[0]:
            target[count:] = jnp.zeros((target.shape[0] - count, width), F32)
        source = target
    gate = gate_pre[...]
    level_3[...] = source[...].astype(BF16)
    gated[...] = (source[...] * (gate / (1.0 + jnp.exp(-gate)))).astype(BF16)


def flip_kernel(place, block, flipped):
    flipped[...] = dot(anti_identity(block.shape[0]), block[...]).astype(BF16)


def norm_grad_kernel(channels, place, *refs):
    own, mirrored = refs[:channels], refs[channels : 2 * channels]
    *weights, out = refs[2 * channels :]
    me = place[1]
    rows, width = own[0].shape
    for block, cotangents in enumerate((own, mirrored)):
        for i in range(channels):
            total = jnp.zeros((rows, width), F32)
            for j in range(channels):
                total += dot(cotangents[j][...], weights[j][part(i ^ me, width), :], LAST_DOT)
            out[block * rows : (block + 1) * rows, i * width : (i + 1) * width] = total.astype(BF16)


def combine_kernel(channels, place, *refs):
    own, mirrored = refs[:channels], refs[channels : 2 * channels]
    grad_norm, choose, gain, gate_pre, level_3 = refs[2 * channels : 2 * channels + 5]
    normalized, upstream, grad_gate_pre, first, second, gains, grad_gated = refs[2 * channels + 5 :]
    me = place[1]
    rows, width = own[0].shape
    full = channels * width
    tile = rows // 4
    for j in range(channels):
        gains[:, j * width : (j + 1) * width] = gain[:, part(me ^ j, width)]
    for block, (here, there) in enumerate(((own, mirrored), (mirrored, own))):
        for k in range(4):
            at = slice(k * tile, (k + 1) * tile)
            mine = jnp.concatenate([ref[at, :] for ref in here], axis=1)
            other = jnp.concatenate([ref[at, :] for ref in there], axis=1)
            combined = mine.astype(F32) + dot(other, choose[...])
            mean = jnp.sum(combined * combined, axis=1, keepdims=True) * (1.0 / full)
            inv_scale = lax.rsqrt(mean + EPSILON)
            hat = combined * inv_scale
            at_both = slice(block * rows + k * tile, block * rows + (k + 1) * tile)
            normalized[at_both, :] = (hat * gains[...]).astype(BF16)
            scaled = grad_norm[at_both, :].astype(F32) * gains[...]
            row_total = jnp.sum(scaled * hat, axis=1, keepdims=True) * (1.0 / full)
            if block == 0:
                grad_gated[at, :] = inv_scale * (scaled[:, :width] - hat[:, :width] * row_total)
            else:
                grad_comb = (inv_scale * (scaled - hat * row_total)).astype(BF16)
                grad_gated[at, :] += dot(grad_comb, choose[:width, :], LAST_DOT)
    gate = gate_pre[...]
    sigmoid = 1.0 / (1.0 + jnp.exp(-gate))
    total = grad_gated[...]
    upstream[...] = (total * (gate * sigmoid)).astype(BF16)
    grad_gate_pre[...] = (total * level_3[...].astype(F32) * sigmoid * (1.0 + gate * (1.0 - sigmoid))).astype(BF16)
    odd, far = place[0] % 2, rows - EDGE
    first[...] = upstream[pl.ds(pl.multiple_of((1 - odd) * far, 16), EDGE), :]
    second[...] = upstream[pl.ds(pl.multiple_of(odd * far, 16), EDGE), :]


def output_kernel(channels, place, normalized, w_out, block_in, output):
    me = place[1]
    rows, width = block_in.shape
    total = block_in[...].astype(F32)
    for j in range(channels):
        total += dot(normalized[:rows, j * width : (j + 1) * width], w_out[part(me ^ j, width), :])
    output[...] = total.astype(BF16)


def products_kernel(channels, place, normalized, cotangent, mirrored_cotangent, grad_gate_pre, *refs):
    mains = refs[:channels]
    out_sent, out_kept, gate_sent, gate_kept, whole_out, whole_gate = refs[channels:]
    me, side = place[1], (place[0] // 2) % 2
    rows, width = cotangent.shape
    for j in range(channels // 2):
        block = (side * (channels // 2) + j) ^ me
        columns = part(block, width)
        whole_out[j * width : (j + 1) * width, :] = dot(
            normalized[:rows, columns], cotangent[...], ROWS_DOT
        ) + dot(normalized[rows:, columns], mirrored_cotangent[...], ROWS_DOT)
    half = whole_out.shape[0] // 2
    bit = place[0] % 2
    out_sent[...] = whole_out[part(1 - bit, half), :].astype(BF16)
    out_kept[...] = whole_out[part(bit, half), :]
    for j in range(channels):
        whole_gate[part(me ^ j, width), :] = dot(mains[j][...], grad_gate_pre[...], ROWS_DOT)
    half = whole_gate.shape[0] // 2
    gate_sent[...] = whole_gate[part(1 - side, half), :].astype(BF16)
    gate_kept[...] = whole_gate[part(side, half), :]


def backward_kernel(channels, place, upstream, first, second, conv_w, *refs):
    mains, (saved, sent, kept, whole, grad_3, grad_2, grad_1, levels) = refs[:channels], refs[channels:]
    levels[...] = saved[...].astype(F32)
    me, odd = place[1], place[0] % 2
    rows, width = upstream.shape
    fore = BACK_FORE[3]
    even = (odd == 0).astype(F32)
    early, late = first[...].astype(F32), second[...].astype(F32)
    grad_3[:fore] = (early * (1.0 - even) + late * even)[EDGE - fore :]
    grad_3[fore : fore + rows] = upstream[...].astype(F32)
    grad_3[fore + rows :] = early * even + late * (1.0 - even)
    half = whole.shape[0] // 2
    for top in (half - SPARE, 2 * half - SPARE):
        whole[top : top + SPARE, :] = jnp.zeros((SPARE, width), F32)
    grads = (None, grad_1, grad_2, grad_3)
    grad_0 = None
    for number in (2, 1, 0):
        dilation, source = DILATIONS[number], grads[number + 1]
        top = sum(saved_rows(rows, below) for below in range(number))
        fore = BACK_FORE[number + 1]
        here = source[fore : fore + rows]
        for tap in range(4):
            begin = top + FORE[number] + (tap - 2) * dilation
            row = half - SPARE + 4 * number + tap
            whole[row : row + 1, :] = jnp.sum(here * levels[begin : begin + rows], axis=0, keepdims=True)
        count = BACK_FORE[number] + rows + BACK_AFT[number]
        total = jnp.zeros((count, width), F32)
        for tap in range(4):
            begin = fore - BACK_FORE[number] - (tap - 2) * dilation
            total += conv_w[number, tap : tap + 1, :] * source[begin : begin + count]
        if number:
            grads[number][...] = keep_inside(total, place, BACK_FORE[number], rows)
        else:
            grad_0 = total.astype(BF16)
    for j in range(channels):
        block = me ^ j
        start = (block // (channels // 2)) * half + (block % (channels // 2)) * width
        whole[pl.ds(pl.multiple_of(start, SPARE), width), :] = dot(mains[j][...], grad_0, ROWS_DOT)
    sent[...] = whole[part(1 - odd, half), :].astype(BF16)
    kept[...] = whole[part(odd, half), :]


def split(total, bit):
    half = total.shape[0] // 2
    low, high = total[:half], total[half:]
    first = jnp.broadcast_to(bit, low.shape) == 0
    return jnp.where(first, high, low), jnp.where(first, low, high)


def join(mine, other, bit):
    first = jnp.broadcast_to(bit, mine.shape) == 0
    return jnp.where(first, mine, other), jnp.where(first, other, mine)


def step_kernel(plan, place, *refs):
    sources, targets = refs[: 2 * len(plan)], list(refs[2 * len(plan) :])
    for k, (done, after) in enumerate(plan):
        mine, other = sources[2 * k : 2 * k + 2]
        rows = mine.shape[0]
        if done[0] == "double":
            bit = (place[0] // done[1]) % 2
            target = targets.pop(0)
            count = rows - SPARE if after is not None and after[0] == "take" else rows
            target[part(bit, count, 16), :] = mine[:count]
            target[part(1 - bit, count, 16), :] = other[:count]
            if count < rows:
                taps = targets.pop(0)
                first = mine[count:].astype(F32), other[count:].astype(F32)
                low, _ = join(*first, bit)
                for number in range(taps.shape[0]):
                    taps[number] = low[number * taps.shape[1] : (number + 1) * taps.shape[1]]
        elif after is not None and after[0] == "halve":
            half = rows // 2
            bit = (place[0] // after[1]) % 2
            for way in (1 - bit, bit):
                at = part(way, half, 16)
                target = targets.pop(0)
                target[...] = (mine[at, :] + other[at, :].astype(F32)).astype(target.dtype)
        else:
            targets.pop(0)[...] = (mine[...] + other[...].astype(F32)).astype(BF16)


def advance(place, items, taps):
    width = items[0][2].shape[1]
    outs, counts = [], []
    for done, after, mine, _ in items:
        rows = mine.shape[0] * (1 if done[0] == "halve" else 2)
        if after is not None and after[0] == "halve":
            outs += [((rows // 2, width), BF16), ((rows // 2, width), F32)]
            counts.append(2)
        elif after is not None and after[0] == "take":
            outs += [((rows - 2 * SPARE, width), BF16), ((*taps, width), F32)]
            counts.append(2)
        else:
            outs.append(((rows, width), BF16))
            counts.append(1)
    arrays = [array for item in items for array in item[2:]]
    plan = [item[:2] for item in items]
    fits = True
    for done, after, mine, _ in items:
        rows = mine.shape[0]
        if done[0] == "double":
            fits &= rows % 16 == 0
        elif after is not None and after[0] == "halve":
            fits &= rows % 32 == 0
        else:
            fits &= rows % 8 == 0
    if fits:
        results = run(functools.partial(step_kernel, plan), place, arrays, outs)
    else:
        results = []
        for done, after, mine, other in items:
            mine, other = mine.astype(F32), other.astype(F32)
            if done[0] == "halve":
                total = mine + other
            else:
                total = jnp.concatenate(join(mine, other, seq_bit(done[1])), axis=0)
            if after is not None and after[0] == "halve":
                sent, kept = split(total, seq_bit(after[1]))
                results += [sent.astype(BF16), kept]
            elif after is not None and after[0] == "take":
                half = total.shape[0] // 2
                results += [
                    jnp.concatenate([total[: half - SPARE], total[half:-SPARE]], axis=0).astype(BF16),
                    total[half - SPARE : half - SPARE + taps[0] * taps[1]].reshape(*taps, width),
                ]
            else:
                results.append(total.astype(BF16))
    grouped = []
    for count in counts:
        grouped.append(results[:count])
        results = results[count:]
    return grouped


def exchange(block, axis, distance):
    count = lax.axis_size(axis)
    return lax.ppermute(block, axis, [(i, i ^ distance) for i in range(count)])


def distances(axis):
    return [1 << bit for bit in range(lax.axis_size(axis).bit_length() - 1)]


def mirror(block):
    count = lax.axis_size("seq")
    return lax.ppermute(block, "seq", [(i, count - 1 - i) for i in range(count)])


def swap_edges(first, second):
    count = lax.axis_size("seq")
    received = []
    for turn, block in enumerate((first, second)):
        route = []
        for low in range(turn, count - 1, 2):
            route += [(low, low + 1), (low + 1, low)]
        received.append(lax.ppermute(block, "seq", route))
    return received


def together(*values):
    return lax.optimization_barrier(values)


def seq_bit(distance):
    return (lax.axis_index("seq") & distance) // distance


def local(tokens, hidden, embedding, w_in, w_gate, conv_w, channel_order, gain, w_out, cotangent):
    rows, width = hidden.shape
    full = gain.shape[0]
    channels = full // width
    cross = channels // 2
    steps = distances("seq")
    block = ((rows, width), BF16)
    place = jnp.stack([lax.axis_index("seq"), lax.axis_index("ch"), lax.axis_size("seq")]).astype(jnp.int32)

    cotangent_x = exchange(cotangent, "ch", cross)
    mirrored_cotangent = mirror(cotangent)
    inputs = (tokens.reshape(1, rows), hidden, embedding)
    local_input, first, second = run(
        input_kernel,
        place,
        inputs,
        [block, ((EDGE, width), BF16), ((EDGE, width), BF16)],
        [pltpu.VMEM((16, width), F32), *fetch_scratch(inputs)],
        megabytes=60,
        fetched=3,
    )
    input_x = exchange(local_input, "ch", cross)
    input_core = exchange(local_input, "ch", 1)
    choose = run(
        functools.partial(setup_kernel, width),
        place,
        (channel_order.reshape(1, full),),
        [((full, full), BF16)],
        gflop=2.0,
    )[0]
    first, second, cotangent_x = together(first, second, cotangent_x)
    near = swap_edges(first, second)
    near = jnp.concatenate(near, axis=0)
    far = exchange(near, "ch", cross)
    early_w_out, far = together(w_out, far)
    edges = jnp.concatenate([near, far], axis=0)
    w_out_x = exchange(early_w_out, "ch", cross)
    mirrored_cotangent = run(flip_kernel, place, (mirrored_cotangent,), [block], gflop=1.0)[0]
    mirrored_cotangent, input_core, choose = together(mirrored_cotangent, input_core, choose)
    mains = [local_input, input_core, input_x, exchange(input_x, "ch", 1)]

    projected, gate_pre, w_in_on = run(
        functools.partial(project_kernel, channels),
        place,
        (*mains, w_in, w_gate),
        [((rows, width), F32)] * 2 + [(w_in.shape, BF16)],
        gflop=6.0,
    )
    edges_core = exchange(edges, "ch", 1)
    levels, level_3, gated = run(
        functools.partial(forward_kernel, channels),
        place,
        (edges, edges_core, w_in_on, projected, gate_pre, conv_w),
        [((sum(saved_rows(rows, number) for number in range(3)), width), BF16), block, block],
        [pltpu.VMEM((saved_rows(rows, number), width), F32) for number in range(4)],
        gflop=0.4,
    )
    mirrored_cotangent, w_out_x = together(mirrored_cotangent, w_out_x)
    mirrored_cotangent_x = exchange(mirrored_cotangent, "ch", cross)
    gated_x = exchange(gated, "ch", cross)
    mirrored, mirrored_cotangent_x, gated_x = together(mirror(gated), mirrored_cotangent_x, gated_x)
    mirrored = run(flip_kernel, place, (mirrored,), [block], gflop=12.0)[0]
    mirrored_x = exchange(mirrored, "ch", cross)
    gated_all = [gated, exchange(gated, "ch", 1), gated_x, exchange(gated_x, "ch", 1)]
    cotangent_all = [cotangent, exchange(cotangent, "ch", 1), cotangent_x, exchange(cotangent_x, "ch", 1)]
    mirrored_cotangent_all = [
        mirrored_cotangent,
        exchange(mirrored_cotangent, "ch", 1),
        mirrored_cotangent_x,
        exchange(mirrored_cotangent_x, "ch", 1),
    ]
    grad_norm = run(
        functools.partial(norm_grad_kernel, channels),
        place,
        (
            *cotangent_all,
            *mirrored_cotangent_all,
            w_out,
            exchange(w_out, "ch", 1),
            w_out_x,
            exchange(w_out_x, "ch", 1),
        ),
        [((2 * rows, full), BF16)],
        gflop=2.1,
    )[0]
    mirrored_x, grad_norm = together(mirrored_x, grad_norm)
    mirrored_all = [mirrored, exchange(mirrored, "ch", 1), mirrored_x, exchange(mirrored_x, "ch", 1)]

    normalized, upstream, grad_gate_pre, first, second = run(
        functools.partial(combine_kernel, channels),
        place,
        (*gated_all, *mirrored_all, grad_norm, choose, gain.reshape(1, full), gate_pre, level_3),
        [((2 * rows, full), BF16), block, block, ((EDGE, width), BF16), ((EDGE, width), BF16)],
        [pltpu.VMEM((1, full), F32), pltpu.VMEM((rows, width), F32)],
        gflop=2.5,
    )
    first, second = swap_edges(first, second)
    out_sent, out_kept, gate_sent, gate_kept = run(
        functools.partial(products_kernel, channels),
        place,
        (normalized, cotangent, mirrored_cotangent, grad_gate_pre, *mains),
        [
            ((full // 4, width), BF16),
            ((full // 4, width), F32),
            ((full // 2, width), BF16),
            ((full // 2, width), F32),
        ],
        [pltpu.VMEM((full // 2, width), F32), pltpu.VMEM((full, width), F32)],
        gflop=0.8,
    )
    out_sent, gate_sent, first, second = together(out_sent, gate_sent, first, second)
    out_other = exchange(out_sent, "seq", steps[0])
    gate_other = exchange(gate_sent, "seq", steps[1])
    half = full // 2 + SPARE
    in_sent, in_kept = run(
        functools.partial(backward_kernel, channels),
        place,
        (upstream, first, second, conv_w, *mains, levels),
        [((half, width), BF16), ((half, width), F32)],
        [pltpu.VMEM((2 * half, width), F32)]
        + [pltpu.VMEM((BACK_FORE[k] + rows + BACK_AFT[k], width), F32) for k in (3, 2, 1)]
        + [pltpu.VMEM(levels.shape, F32)],
        gflop=0.5,
    )
    output = run(
        functools.partial(output_kernel, channels),
        place,
        (normalized, w_out, local_input),
        [block],
        gflop=0.3,
    )[0]

    down = [("halve", distance) for distance in steps]
    up = [("double", distance) for distance in steps[::-1]]
    out_down, out_up = down[:1] + down[2:], up[:-2] + up[-1:] + up[-2:-1]
    gate_down, gate_up = down[1:] + down[:1], up[-1:] + up[:-1]
    routes = [down + up + [("take",)], gate_down + gate_up + [None], out_down + out_up + [None]]
    in_sent, out_other = together(in_sent, out_other)
    results = []
    for route, sent, kept, other in zip(
        routes, (in_sent, None, None), (in_kept, gate_kept, out_kept), (None, gate_other, out_other)
    ):
        if other is None:
            other = exchange(sent, "seq", route[0][1])
        elif len(results) == 1:
            other = gate_other
        for number, (done, upcoming) in enumerate(zip(route, route[1:])):
            prepared = advance(place, [(done, upcoming, kept, other)], conv_w.shape[:2])[0]
            if upcoming is not None and upcoming[0] != "take":
                sent, kept = prepared if len(prepared) == 2 else prepared * 2
                if not results and number == 0:
                    sent, gate_other = together(sent, gate_other)
                other = exchange(sent, "seq", upcoming[1])
        results.append(prepared)
    (grad_in, grad_conv), (sum_gate,), (sum_out,) = results
    return output, grad_in, sum_gate, sum_out, grad_conv


def solution(mesh):
    placed = (
        P("seq"),
        P("seq", "ch"),
        P(None, "ch"),
        P(None, "ch"),
        P(None, "ch"),
        P(None, None, "ch"),
        P(),
        P(),
        P(None, "ch"),
        P("seq", "ch"),
    )
    return jax.shard_map(
        local,
        mesh=mesh,
        in_specs=placed,
        out_specs=(
            P("seq", "ch"),
            P(None, "ch"),
            P(None, "ch"),
            P(None, "ch"),
            P(None, None, "ch"),
        ),
        check_vma=False,
    )
```

```python
import functools

import jax
import jax.numpy as jnp
from jax import lax
from jax.experimental import pallas as pl
from jax.experimental.pallas import tpu as pltpu
from jax.sharding import PartitionSpec as P

DILATIONS = (1, 8, 64)
EPSILON = 1e-06
FORE = (160, 144, 128, 0)
AFT = (80, 72, 64, 0)
BACK_FORE = (0, 8, 16, 80)
BACK_AFT = (0, 8, 24, 160)
EDGE = 160
SPARE = 64

BF16, F32 = jnp.bfloat16, jnp.float32
ROWS_DOT = (((0,), (0,)), ((), ()))
LAST_DOT = (((1,), (1,)), ((), ()))


def dot(left, right, dims=(((1,), (0,)), ((), ()))):
    return lax.dot_general(left, right, dims, preferred_element_type=F32)


def run(body, place, operands, outs, scratch=(), megabytes=8, gflop=0.1, fetched=0):
    moved = sum(x.size * x.dtype.itemsize for x in operands)
    return pl.pallas_call(
        body,
        out_shape=[jax.ShapeDtypeStruct(shape, dtype) for shape, dtype in outs],
        in_specs=[pl.BlockSpec(memory_space=pltpu.SMEM)]
        + [pl.BlockSpec(memory_space=pltpu.VMEM)] * (len(operands) - fetched)
        + [pl.BlockSpec(memory_space=pltpu.HBM)] * fetched,
        out_specs=[pl.BlockSpec(memory_space=pltpu.VMEM)] * len(outs),
        scratch_shapes=list(scratch),
        compiler_params=pltpu.CompilerParams(vmem_limit_bytes=megabytes << 20),
        cost_estimate=pl.CostEstimate(flops=int(gflop * 1e9), bytes_accessed=moved, transcendentals=0),
    )(place, *operands)


def fetch(sources, targets, semaphores):
    copies = [
        pltpu.make_async_copy(source, target, semaphores.at[k])
        for k, (source, target) in enumerate(zip(sources, targets))
    ]
    for copy in copies:
        copy.start()
    return copies


def fetch_scratch(operands):
    return [pltpu.VMEM(x.shape, x.dtype) for x in operands] + [pltpu.SemaphoreType.DMA((len(operands),))]


def part(index, size, multiple=None):
    return pl.ds(pl.multiple_of(index * size, multiple or size), size)


def saved_rows(rows, number):
    return -(-(FORE[number] + rows + AFT[number]) // 16) * 16


def anti_identity(rows):
    down = lax.broadcasted_iota(jnp.int32, (rows, rows), 0)
    across = lax.broadcasted_iota(jnp.int32, (rows, rows), 1)
    return (down + across == rows - 1).astype(F32).astype(BF16)


def input_kernel(place, tokens_hbm, hidden_hbm, embedding_hbm, w_out_hbm, block_in, first, second, w_half, *scratch):
    padded, tokens, hidden, embedding, w_out, semaphores = scratch
    copies = fetch(
        (tokens_hbm, hidden_hbm, embedding_hbm, w_out_hbm), (tokens, hidden, embedding, w_out), semaphores
    )
    bases, rows = embedding.shape[0], hidden.shape[0]
    padded[...] = jnp.zeros_like(padded)
    for copy in copies[:3]:
        copy.wait()
    padded[:bases] = embedding[...].astype(F32)
    base = lax.broadcasted_iota(jnp.int32, (padded.shape[0], rows), 0)
    one_hot = (base == tokens[...]).astype(F32).astype(BF16)
    shift = dot(one_hot, padded[...].astype(BF16), ROWS_DOT)
    block_in[...] = (hidden[...].astype(F32) + shift).astype(BF16)
    odd, far = place[0] % 2, rows - EDGE
    first[...] = block_in[pl.ds(pl.multiple_of((1 - odd) * far, 16), EDGE), :]
    second[...] = block_in[pl.ds(pl.multiple_of(odd * far, 16), EDGE), :]
    copies[3].wait()
    w_half[...] = w_out[part(odd, w_half.shape[0]), :]


def setup_kernel(width, place, order, choose):
    me, full = place[1], order.shape[1]
    down = lax.broadcasted_iota(jnp.int32, (width, width), 0)
    for j in range(full // width):
        for i in range(full // width):
            wanted = order[:, part(me ^ i, width)]
            choose[j * width : (j + 1) * width, i * width : (i + 1) * width] = (
                (down + (me ^ j) * width == wanted).astype(F32).astype(BF16)
            )


def project_kernel(channels, place, *refs):
    mains, (w_in, w_gate, projected, gate_pre, w_in_on) = refs[:channels], refs[channels:]
    me, width = place[1], mains[0].shape[1]
    for weight, out in ((w_in, projected), (w_gate, gate_pre)):
        total = dot(mains[0][...], weight[part(me, width), :])
        for j in range(1, channels):
            total += dot(mains[j][...], weight[part(me ^ j, width), :])
        out[...] = total
    w_in_on[...] = w_in[...]


def keep_inside(total, place, before, rows):
    position = lax.broadcasted_iota(jnp.int32, total.shape, 0) + (place[0] * rows - before)
    return jnp.where((position >= 0) & (position < place[2] * rows), total, 0.0)


def forward_kernel(channels, place, edges, edges_core, w_in, projected, gate_pre, conv_w, *outs):
    levels, level_3, gated, *stages = outs
    me, odd = place[1], place[0] % 2
    rows, width = projected.shape
    left = jnp.zeros((EDGE, width), F32)
    right = jnp.zeros((AFT[0], width), F32)
    for j in range(channels):
        source = edges_core if j % 2 else edges
        base = (j // 2) * 2 * EDGE
        weight = w_in[part(me ^ j, width), :]
        left += dot(source[pl.ds(pl.multiple_of(base + (1 - odd) * EDGE, 16), EDGE), :], weight)
        right += dot(source[pl.ds(pl.multiple_of(base + odd * EDGE, 16), AFT[0]), :], weight)
    source = stages[0]
    source[:EDGE] = left
    source[EDGE : EDGE + rows] = projected[...]
    source[EDGE + rows :] = right
    top = 0
    for number, dilation in enumerate(DILATIONS):
        target = stages[number + 1]
        levels[top : top + source.shape[0], :] = source[...].astype(BF16)
        top += source.shape[0]
        shift = FORE[number] - FORE[number + 1]
        count = FORE[number + 1] + rows + AFT[number + 1]
        total = jnp.zeros((count, width), F32)
        for tap in range(4):
            begin = shift + (tap - 2) * dilation
            total += conv_w[number, tap : tap + 1, :] * source[begin : begin + count]
        if FORE[number + 1]:
            total = keep_inside(total, place, FORE[number + 1], rows)
        target[:count] = total
        if count < target.shape[0]:
            target[count:] = jnp.zeros((target.shape[0] - count, width), F32)
        source = target
    gate = gate_pre[...]
    level_3[...] = source[...].astype(BF16)
    gated[...] = (source[...] * (gate / (1.0 + jnp.exp(-gate)))).astype(BF16)


def flip_kernel(place, block, flipped):
    flipped[...] = dot(anti_identity(block.shape[0]), block[...]).astype(BF16)


def norm_grad_kernel(channels, place, *refs):
    own, mirrored = refs[:channels], refs[channels : 2 * channels]
    near, near_core, mine, other, mine_core, other_core, out, far, far_core = refs[2 * channels :]
    me, side, half = place[1], place[0] % 2, mine.shape[0]
    for whole, first, second in ((far, mine, other), (far_core, mine_core, other_core)):
        whole[part(side, half), :] = first[...]
        whole[part(1 - side, half), :] = second[...]
    weights = (near, near_core, far, far_core)
    rows, width = own[0].shape
    for block, cotangents in enumerate((own, mirrored)):
        for i in range(channels):
            total = jnp.zeros((rows, width), F32)
            for j in range(channels):
                total += dot(cotangents[j][...], weights[j][part(i ^ me, width), :], LAST_DOT)
            out[block * rows : (block + 1) * rows, i * width : (i + 1) * width] = total.astype(BF16)


def combine_kernel(channels, place, *refs):
    own, mirrored = refs[:channels], refs[channels : 2 * channels]
    grad_norm, choose, gain, gate_pre, level_3 = refs[2 * channels : 2 * channels + 5]
    normalized, upstream, grad_gate_pre, first, second, gains, grad_gated = refs[2 * channels + 5 :]
    me = place[1]
    rows, width = own[0].shape
    full = channels * width
    tile = rows // 4
    for j in range(channels):
        gains[:, j * width : (j + 1) * width] = gain[:, part(me ^ j, width)]
    for block, (here, there) in enumerate(((own, mirrored), (mirrored, own))):
        for k in range(4):
            at = slice(k * tile, (k + 1) * tile)
            mine = jnp.concatenate([ref[at, :] for ref in here], axis=1)
            other = jnp.concatenate([ref[at, :] for ref in there], axis=1)
            combined = mine.astype(F32) + dot(other, choose[...])
            mean = jnp.sum(combined * combined, axis=1, keepdims=True) * (1.0 / full)
            inv_scale = lax.rsqrt(mean + EPSILON)
            hat = combined * inv_scale
            at_both = slice(block * rows + k * tile, block * rows + (k + 1) * tile)
            normalized[at_both, :] = (hat * gains[...]).astype(BF16)
            scaled = grad_norm[at_both, :].astype(F32) * gains[...]
            row_total = jnp.sum(scaled * hat, axis=1, keepdims=True) * (1.0 / full)
            if block == 0:
                grad_gated[at, :] = inv_scale * (scaled[:, :width] - hat[:, :width] * row_total)
            else:
                grad_comb = (inv_scale * (scaled - hat * row_total)).astype(BF16)
                grad_gated[at, :] += dot(grad_comb, choose[:width, :], LAST_DOT)
    gate = gate_pre[...]
    sigmoid = 1.0 / (1.0 + jnp.exp(-gate))
    total = grad_gated[...]
    upstream[...] = (total * (gate * sigmoid)).astype(BF16)
    grad_gate_pre[...] = (total * level_3[...].astype(F32) * sigmoid * (1.0 + gate * (1.0 - sigmoid))).astype(BF16)
    odd, far = place[0] % 2, rows - EDGE
    first[...] = upstream[pl.ds(pl.multiple_of((1 - odd) * far, 16), EDGE), :]
    second[...] = upstream[pl.ds(pl.multiple_of(odd * far, 16), EDGE), :]


def output_kernel(channels, place, normalized, w_out, block_in, output):
    me = place[1]
    rows, width = block_in.shape
    total = block_in[...].astype(F32)
    for j in range(channels):
        total += dot(normalized[:rows, j * width : (j + 1) * width], w_out[part(me ^ j, width), :])
    output[...] = total.astype(BF16)


def products_kernel(channels, place, normalized, cotangent, mirrored_cotangent, grad_gate_pre, *refs):
    mains = refs[:channels]
    out_sent, out_kept, gate_sent, gate_kept, whole_out, whole_gate = refs[channels:]
    me, side = place[1], (place[0] // 2) % 2
    rows, width = cotangent.shape
    for j in range(channels // 2):
        block = (side * (channels // 2) + j) ^ me
        columns = part(block, width)
        whole_out[j * width : (j + 1) * width, :] = dot(
            normalized[:rows, columns], cotangent[...], ROWS_DOT
        ) + dot(normalized[rows:, columns], mirrored_cotangent[...], ROWS_DOT)
    half = whole_out.shape[0] // 2
    bit = place[0] % 2
    out_sent[...] = whole_out[part(1 - bit, half), :].astype(BF16)
    out_kept[...] = whole_out[part(bit, half), :]
    for j in range(channels):
        whole_gate[part(me ^ j, width), :] = dot(mains[j][...], grad_gate_pre[...], ROWS_DOT)
    half = whole_gate.shape[0] // 2
    gate_sent[...] = whole_gate[part(1 - side, half), :].astype(BF16)
    gate_kept[...] = whole_gate[part(side, half), :]


def backward_kernel(channels, place, upstream, first, second, conv_w, *refs):
    mains, (saved, sent, kept, whole, grad_3, grad_2, grad_1, levels) = refs[:channels], refs[channels:]
    levels[...] = saved[...].astype(F32)
    me, odd = place[1], place[0] % 2
    rows, width = upstream.shape
    fore = BACK_FORE[3]
    even = (odd == 0).astype(F32)
    early, late = first[...].astype(F32), second[...].astype(F32)
    grad_3[:fore] = (early * (1.0 - even) + late * even)[EDGE - fore :]
    grad_3[fore : fore + rows] = upstream[...].astype(F32)
    grad_3[fore + rows :] = early * even + late * (1.0 - even)
    half = whole.shape[0] // 2
    for top in (half - SPARE, 2 * half - SPARE):
        whole[top : top + SPARE, :] = jnp.zeros((SPARE, width), F32)
    grads = (None, grad_1, grad_2, grad_3)
    grad_0 = None
    for number in (2, 1, 0):
        dilation, source = DILATIONS[number], grads[number + 1]
        top = sum(saved_rows(rows, below) for below in range(number))
        fore = BACK_FORE[number + 1]
        here = source[fore : fore + rows]
        for tap in range(4):
            begin = top + FORE[number] + (tap - 2) * dilation
            row = half - SPARE + 4 * number + tap
            whole[row : row + 1, :] = jnp.sum(here * levels[begin : begin + rows], axis=0, keepdims=True)
        count = BACK_FORE[number] + rows + BACK_AFT[number]
        total = jnp.zeros((count, width), F32)
        for tap in range(4):
            begin = fore - BACK_FORE[number] - (tap - 2) * dilation
            total += conv_w[number, tap : tap + 1, :] * source[begin : begin + count]
        if number:
            grads[number][...] = keep_inside(total, place, BACK_FORE[number], rows)
        else:
            grad_0 = total.astype(BF16)
    for j in range(channels):
        block = me ^ j
        start = (block // (channels // 2)) * half + (block % (channels // 2)) * width
        whole[pl.ds(pl.multiple_of(start, SPARE), width), :] = dot(mains[j][...], grad_0, ROWS_DOT)
    sent[...] = whole[part(1 - odd, half), :].astype(BF16)
    kept[...] = whole[part(odd, half), :]


def split(total, bit):
    half = total.shape[0] // 2
    low, high = total[:half], total[half:]
    first = jnp.broadcast_to(bit, low.shape) == 0
    return jnp.where(first, high, low), jnp.where(first, low, high)


def join(mine, other, bit):
    first = jnp.broadcast_to(bit, mine.shape) == 0
    return jnp.where(first, mine, other), jnp.where(first, other, mine)


def step_kernel(plan, place, *refs):
    sources, targets = refs[: 2 * len(plan)], list(refs[2 * len(plan) :])
    for k, (done, after) in enumerate(plan):
        mine, other = sources[2 * k : 2 * k + 2]
        rows = mine.shape[0]
        if done[0] == "double":
            bit = (place[0] // done[1]) % 2
            target = targets.pop(0)
            count = rows - SPARE if after is not None and after[0] == "take" else rows
            target[part(bit, count, 16), :] = mine[:count]
            target[part(1 - bit, count, 16), :] = other[:count]
            if count < rows:
                taps = targets.pop(0)
                first = mine[count:].astype(F32), other[count:].astype(F32)
                low, _ = join(*first, bit)
                for number in range(taps.shape[0]):
                    taps[number] = low[number * taps.shape[1] : (number + 1) * taps.shape[1]]
        elif after is not None and after[0] == "halve":
            half = rows // 2
            bit = (place[0] // after[1]) % 2
            for way in (1 - bit, bit):
                at = part(way, half, 16)
                target = targets.pop(0)
                target[...] = (mine[at, :] + other[at, :].astype(F32)).astype(target.dtype)
        else:
            targets.pop(0)[...] = (mine[...] + other[...].astype(F32)).astype(BF16)


def advance(place, items, taps):
    width = items[0][2].shape[1]
    outs, counts = [], []
    for done, after, mine, _ in items:
        rows = mine.shape[0] * (1 if done[0] == "halve" else 2)
        if after is not None and after[0] == "halve":
            outs += [((rows // 2, width), BF16), ((rows // 2, width), F32)]
            counts.append(2)
        elif after is not None and after[0] == "take":
            outs += [((rows - 2 * SPARE, width), BF16), ((*taps, width), F32)]
            counts.append(2)
        else:
            outs.append(((rows, width), BF16))
            counts.append(1)
    arrays = [array for item in items for array in item[2:]]
    plan = [item[:2] for item in items]
    fits = True
    for done, after, mine, _ in items:
        rows = mine.shape[0]
        if done[0] == "double":
            fits &= rows % 16 == 0
        elif after is not None and after[0] == "halve":
            fits &= rows % 32 == 0
        else:
            fits &= rows % 8 == 0
    if fits:
        results = run(functools.partial(step_kernel, plan), place, arrays, outs)
    else:
        results = []
        for done, after, mine, other in items:
            mine, other = mine.astype(F32), other.astype(F32)
            if done[0] == "halve":
                total = mine + other
            else:
                total = jnp.concatenate(join(mine, other, seq_bit(done[1])), axis=0)
            if after is not None and after[0] == "halve":
                sent, kept = split(total, seq_bit(after[1]))
                results += [sent.astype(BF16), kept]
            elif after is not None and after[0] == "take":
                half = total.shape[0] // 2
                results += [
                    jnp.concatenate([total[: half - SPARE], total[half:-SPARE]], axis=0).astype(BF16),
                    total[half - SPARE : half - SPARE + taps[0] * taps[1]].reshape(*taps, width),
                ]
            else:
                results.append(total.astype(BF16))
    grouped = []
    for count in counts:
        grouped.append(results[:count])
        results = results[count:]
    return grouped


def exchange(block, axis, distance):
    count = lax.axis_size(axis)
    return lax.ppermute(block, axis, [(i, i ^ distance) for i in range(count)])


def distances(axis):
    return [1 << bit for bit in range(lax.axis_size(axis).bit_length() - 1)]


def mirror(block):
    count = lax.axis_size("seq")
    return lax.ppermute(block, "seq", [(i, count - 1 - i) for i in range(count)])


def swap_edges(first, second):
    count = lax.axis_size("seq")
    received = []
    for turn, block in enumerate((first, second)):
        route = []
        for low in range(turn, count - 1, 2):
            route += [(low, low + 1), (low + 1, low)]
        received.append(lax.ppermute(block, "seq", route))
    return received


def together(*values):
    return lax.optimization_barrier(values)


def seq_bit(distance):
    return (lax.axis_index("seq") & distance) // distance


def local(tokens, hidden, embedding, w_in, w_gate, conv_w, channel_order, gain, w_out, cotangent):
    rows, width = hidden.shape
    full = gain.shape[0]
    channels = full // width
    cross = channels // 2
    steps = distances("seq")
    block = ((rows, width), BF16)
    place = jnp.stack([lax.axis_index("seq"), lax.axis_index("ch"), lax.axis_size("seq")]).astype(jnp.int32)

    cotangent_x = exchange(cotangent, "ch", cross)
    mirrored_cotangent = mirror(cotangent)
    inputs = (tokens.reshape(1, rows), hidden, embedding, w_out)
    local_input, first, second, w_half = run(
        input_kernel,
        place,
        inputs,
        [block, ((EDGE, width), BF16), ((EDGE, width), BF16), ((full // 2, width), BF16)],
        [pltpu.VMEM((16, width), F32), *fetch_scratch(inputs)],
        megabytes=60,
        fetched=4,
    )
    input_x = exchange(local_input, "ch", cross)
    input_core = exchange(local_input, "ch", 1)
    choose = run(
        functools.partial(setup_kernel, width),
        place,
        (channel_order.reshape(1, full),),
        [((full, full), BF16)],
        gflop=2.0,
    )[0]
    first, second, cotangent_x = together(first, second, cotangent_x)
    near = swap_edges(first, second)
    mirrored_cotangent, *near = together(mirrored_cotangent, *near)
    near = jnp.concatenate(near, axis=0)
    far = exchange(near, "ch", cross)
    w_half, far = together(w_half, far)
    w_x_mine = exchange(w_half, "ch", cross)
    w_x_other = exchange(w_x_mine, "seq", 1)
    edges = jnp.concatenate([near, far], axis=0)
    mirrored_cotangent = run(flip_kernel, place, (mirrored_cotangent,), [block], gflop=1.0)[0]
    mirrored_cotangent, input_core, choose = together(mirrored_cotangent, input_core, choose)
    mains = [local_input, input_core, input_x, exchange(input_x, "ch", 1)]

    projected, gate_pre, w_in_on = run(
        functools.partial(project_kernel, channels),
        place,
        (*mains, w_in, w_gate),
        [((rows, width), F32)] * 2 + [(w_in.shape, BF16)],
        gflop=6.0,
    )
    edges_core = exchange(edges, "ch", 1)
    levels, level_3, gated = run(
        functools.partial(forward_kernel, channels),
        place,
        (edges, edges_core, w_in_on, projected, gate_pre, conv_w),
        [((sum(saved_rows(rows, number) for number in range(3)), width), BF16), block, block],
        [pltpu.VMEM((saved_rows(rows, number), width), F32) for number in range(4)],
        gflop=0.4,
    )
    mirrored_cotangent_x = exchange(mirrored_cotangent, "ch", cross)
    gated_x = exchange(gated, "ch", cross)
    mirrored, mirrored_cotangent_x, gated_x = together(mirror(gated), mirrored_cotangent_x, gated_x)
    mirrored = run(flip_kernel, place, (mirrored,), [block], gflop=12.0)[0]
    mirrored_x = exchange(mirrored, "ch", cross)
    gated_all = [gated, exchange(gated, "ch", 1), gated_x, exchange(gated_x, "ch", 1)]
    cotangent_all = [cotangent, exchange(cotangent, "ch", 1), cotangent_x, exchange(cotangent_x, "ch", 1)]
    mirrored_cotangent_all = [
        mirrored_cotangent,
        exchange(mirrored_cotangent, "ch", 1),
        mirrored_cotangent_x,
        exchange(mirrored_cotangent_x, "ch", 1),
    ]
    grad_norm = run(
        functools.partial(norm_grad_kernel, channels),
        place,
        (
            *cotangent_all,
            *mirrored_cotangent_all,
            w_out,
            exchange(w_out, "ch", 1),
            w_x_mine,
            w_x_other,
            exchange(w_x_mine, "ch", 1),
            exchange(w_x_other, "ch", 1),
        ),
        [((2 * rows, full), BF16)],
        [pltpu.VMEM((full, width), BF16)] * 2,
        gflop=2.1,
    )[0]
    mirrored_x, grad_norm = together(mirrored_x, grad_norm)
    mirrored_all = [mirrored, exchange(mirrored, "ch", 1), mirrored_x, exchange(mirrored_x, "ch", 1)]

    normalized, upstream, grad_gate_pre, first, second = run(
        functools.partial(combine_kernel, channels),
        place,
        (*gated_all, *mirrored_all, grad_norm, choose, gain.reshape(1, full), gate_pre, level_3),
        [((2 * rows, full), BF16), block, block, ((EDGE, width), BF16), ((EDGE, width), BF16)],
        [pltpu.VMEM((1, full), F32), pltpu.VMEM((rows, width), F32)],
        gflop=2.5,
    )
    first, second = swap_edges(first, second)
    out_sent, out_kept, gate_sent, gate_kept = run(
        functools.partial(products_kernel, channels),
        place,
        (normalized, cotangent, mirrored_cotangent, grad_gate_pre, *mains),
        [
            ((full // 4, width), BF16),
            ((full // 4, width), F32),
            ((full // 2, width), BF16),
            ((full // 2, width), F32),
        ],
        [pltpu.VMEM((full // 2, width), F32), pltpu.VMEM((full, width), F32)],
        gflop=0.8,
    )
    out_sent, gate_sent, first, second = together(out_sent, gate_sent, first, second)
    out_other = exchange(out_sent, "seq", steps[0])
    gate_other = exchange(gate_sent, "seq", steps[1])
    half = full // 2 + SPARE
    in_sent, in_kept = run(
        functools.partial(backward_kernel, channels),
        place,
        (upstream, first, second, conv_w, *mains, levels),
        [((half, width), BF16), ((half, width), F32)],
        [pltpu.VMEM((2 * half, width), F32)]
        + [pltpu.VMEM((BACK_FORE[k] + rows + BACK_AFT[k], width), F32) for k in (3, 2, 1)]
        + [pltpu.VMEM(levels.shape, F32)],
        gflop=0.5,
    )
    output = run(
        functools.partial(output_kernel, channels),
        place,
        (normalized, w_out, local_input),
        [block],
        gflop=0.3,
    )[0]

    down = [("halve", distance) for distance in steps]
    up = [("double", distance) for distance in steps[::-1]]
    out_down, out_up = down[:1] + down[2:], up[:-2] + up[-1:] + up[-2:-1]
    gate_down, gate_up = down[1:] + down[:1], up[-1:] + up[:-1]
    routes = [down + up + [("take",)], gate_down + gate_up + [None], out_down + out_up + [None]]
    in_sent, out_other = together(in_sent, out_other)
    results = []
    for route, sent, kept, other in zip(
        routes, (in_sent, None, None), (in_kept, gate_kept, out_kept), (None, gate_other, out_other)
    ):
        if other is None:
            other = exchange(sent, "seq", route[0][1])
        elif len(results) == 1:
            other = gate_other
        for number, (done, upcoming) in enumerate(zip(route, route[1:])):
            prepared = advance(place, [(done, upcoming, kept, other)], conv_w.shape[:2])[0]
            if upcoming is not None and upcoming[0] != "take":
                sent, kept = prepared if len(prepared) == 2 else prepared * 2
                if not results and number == 0:
                    sent, gate_other = together(sent, gate_other)
                other = exchange(sent, "seq", upcoming[1])
        results.append(prepared)
    (grad_in, grad_conv), (sum_gate,), (sum_out,) = results
    return output, grad_in, sum_gate, sum_out, grad_conv


def solution(mesh):
    placed = (
        P("seq"),
        P("seq", "ch"),
        P(None, "ch"),
        P(None, "ch"),
        P(None, "ch"),
        P(None, None, "ch"),
        P(),
        P(),
        P(None, "ch"),
        P("seq", "ch"),
    )
    return jax.shard_map(
        local,
        mesh=mesh,
        in_specs=placed,
        out_specs=(
            P("seq", "ch"),
            P(None, "ch"),
            P(None, "ch"),
            P(None, "ch"),
            P(None, None, "ch"),
        ),
        check_vma=False,
    )
```

```python
import functools

import jax
import jax.numpy as jnp
from jax import lax
from jax.experimental import pallas as pl
from jax.experimental.pallas import tpu as pltpu
from jax.sharding import PartitionSpec as P

DILATIONS = (1, 8, 64)
EPSILON = 1e-06
FORE = (160, 144, 128, 0)
AFT = (80, 72, 64, 0)
BACK_FORE = (0, 8, 16, 80)
BACK_AFT = (0, 8, 24, 160)
EDGE = 160
SPARE = 64

BF16, F32 = jnp.bfloat16, jnp.float32
ROWS_DOT = (((0,), (0,)), ((), ()))
LAST_DOT = (((1,), (1,)), ((), ()))


def dot(left, right, dims=(((1,), (0,)), ((), ()))):
    return lax.dot_general(left, right, dims, preferred_element_type=F32)


def run(body, place, operands, outs, scratch=(), megabytes=8, gflop=0.1, fetched=0):
    moved = sum(x.size * x.dtype.itemsize for x in operands)
    return pl.pallas_call(
        body,
        out_shape=[jax.ShapeDtypeStruct(shape, dtype) for shape, dtype in outs],
        in_specs=[pl.BlockSpec(memory_space=pltpu.SMEM)]
        + [pl.BlockSpec(memory_space=pltpu.VMEM)] * (len(operands) - fetched)
        + [pl.BlockSpec(memory_space=pltpu.HBM)] * fetched,
        out_specs=[pl.BlockSpec(memory_space=pltpu.VMEM)] * len(outs),
        scratch_shapes=list(scratch),
        compiler_params=pltpu.CompilerParams(vmem_limit_bytes=megabytes << 20),
        cost_estimate=pl.CostEstimate(flops=int(gflop * 1e9), bytes_accessed=moved, transcendentals=0),
    )(place, *operands)


def fetch(sources, targets, semaphores):
    copies = [
        pltpu.make_async_copy(source, target, semaphores.at[k])
        for k, (source, target) in enumerate(zip(sources, targets))
    ]
    for copy in copies:
        copy.start()
    return copies


def fetch_scratch(operands):
    return [pltpu.VMEM(x.shape, x.dtype) for x in operands] + [pltpu.SemaphoreType.DMA((len(operands),))]


def part(index, size, multiple=None):
    return pl.ds(pl.multiple_of(index * size, multiple or size), size)


def saved_rows(rows, number):
    return -(-(FORE[number] + rows + AFT[number]) // 16) * 16


def anti_identity(rows):
    down = lax.broadcasted_iota(jnp.int32, (rows, rows), 0)
    across = lax.broadcasted_iota(jnp.int32, (rows, rows), 1)
    return (down + across == rows - 1).astype(F32).astype(BF16)


def input_kernel(place, tokens_hbm, hidden_hbm, embedding_hbm, w_out_hbm, block_in, first, second, w_half, *scratch):
    padded, tokens, hidden, embedding, w_out, semaphores = scratch
    copies = fetch(
        (tokens_hbm, hidden_hbm, embedding_hbm, w_out_hbm), (tokens, hidden, embedding, w_out), semaphores
    )
    bases, rows = embedding.shape[0], hidden.shape[0]
    padded[...] = jnp.zeros_like(padded)
    for copy in copies[:3]:
        copy.wait()
    padded[:bases] = embedding[...].astype(F32)
    base = lax.broadcasted_iota(jnp.int32, (padded.shape[0], rows), 0)
    one_hot = (base == tokens[...]).astype(F32).astype(BF16)
    shift = dot(one_hot, padded[...].astype(BF16), ROWS_DOT)
    block_in[...] = (hidden[...].astype(F32) + shift).astype(BF16)
    odd, far = place[0] % 2, rows - EDGE
    first[...] = block_in[pl.ds(pl.multiple_of((1 - odd) * far, 16), EDGE), :]
    second[...] = block_in[pl.ds(pl.multiple_of(odd * far, 16), EDGE), :]
    copies[3].wait()
    w_half[...] = w_out[part(odd, w_half.shape[0]), :]


def setup_kernel(width, place, order, choose):
    me, full = place[1], order.shape[1]
    down = lax.broadcasted_iota(jnp.int32, (width, width), 0)
    for j in range(full // width):
        for i in range(full // width):
            wanted = order[:, part(me ^ i, width)]
            choose[j * width : (j + 1) * width, i * width : (i + 1) * width] = (
                (down + (me ^ j) * width == wanted).astype(F32).astype(BF16)
            )


def project_kernel(channels, place, *refs):
    mains, (w_in, w_gate, projected, gate_pre, w_in_on) = refs[:channels], refs[channels:]
    me, width = place[1], mains[0].shape[1]
    for weight, out in ((w_in, projected), (w_gate, gate_pre)):
        total = dot(mains[0][...], weight[part(me, width), :])
        for j in range(1, channels):
            total += dot(mains[j][...], weight[part(me ^ j, width), :])
        out[...] = total
    w_in_on[...] = w_in[...]


def keep_inside(total, place, before, rows):
    position = lax.broadcasted_iota(jnp.int32, total.shape, 0) + (place[0] * rows - before)
    return jnp.where((position >= 0) & (position < place[2] * rows), total, 0.0)


def forward_kernel(channels, place, edges, edges_core, w_in, projected, gate_pre, conv_w, *outs):
    levels, level_3, gated, *stages = outs
    me, odd = place[1], place[0] % 2
    rows, width = projected.shape
    left = jnp.zeros((EDGE, width), F32)
    right = jnp.zeros((AFT[0], width), F32)
    for j in range(channels):
        source = edges_core if j % 2 else edges
        base = (j // 2) * 2 * EDGE
        weight = w_in[part(me ^ j, width), :]
        left += dot(source[pl.ds(pl.multiple_of(base + (1 - odd) * EDGE, 16), EDGE), :], weight)
        right += dot(source[pl.ds(pl.multiple_of(base + odd * EDGE, 16), AFT[0]), :], weight)
    source = stages[0]
    source[:EDGE] = left
    source[EDGE : EDGE + rows] = projected[...]
    source[EDGE + rows :] = right
    top = 0
    for number, dilation in enumerate(DILATIONS):
        target = stages[number + 1]
        levels[top : top + source.shape[0], :] = source[...].astype(BF16)
        top += source.shape[0]
        shift = FORE[number] - FORE[number + 1]
        count = FORE[number + 1] + rows + AFT[number + 1]
        total = jnp.zeros((count, width), F32)
        for tap in range(4):
            begin = shift + (tap - 2) * dilation
            total += conv_w[number, tap : tap + 1, :] * source[begin : begin + count]
        if FORE[number + 1]:
            total = keep_inside(total, place, FORE[number + 1], rows)
        target[:count] = total
        if count < target.shape[0]:
            target[count:] = jnp.zeros((target.shape[0] - count, width), F32)
        source = target
    gate = gate_pre[...]
    level_3[...] = source[...].astype(BF16)
    gated[...] = (source[...] * (gate / (1.0 + jnp.exp(-gate)))).astype(BF16)


def flip_kernel(place, block, flipped):
    flipped[...] = dot(anti_identity(block.shape[0]), block[...]).astype(BF16)


def norm_grad_kernel(channels, place, *refs):
    own, mirrored = refs[:channels], refs[channels : 2 * channels]
    near, near_core, mine, other, mine_core, other_core, out, far, far_core = refs[2 * channels :]
    me, side, half = place[1], place[0] % 2, mine.shape[0]
    for whole, first, second in ((far, mine, other), (far_core, mine_core, other_core)):
        whole[part(side, half), :] = first[...]
        whole[part(1 - side, half), :] = second[...]
    weights = (near, near_core, far, far_core)
    rows, width = own[0].shape
    for block, cotangents in enumerate((own, mirrored)):
        for i in range(channels):
            total = jnp.zeros((rows, width), F32)
            for j in range(channels):
                total += dot(cotangents[j][...], weights[j][part(i ^ me, width), :], LAST_DOT)
            out[block * rows : (block + 1) * rows, i * width : (i + 1) * width] = total.astype(BF16)


def combine_kernel(channels, place, *refs):
    own, mirrored = refs[:channels], refs[channels : 2 * channels]
    grad_norm, choose, gain, gate_pre, level_3 = refs[2 * channels : 2 * channels + 5]
    normalized, upstream, grad_gate_pre, first, second, gains, grad_gated = refs[2 * channels + 5 :]
    me = place[1]
    rows, width = own[0].shape
    full = channels * width
    tile = rows // 4
    for j in range(channels):
        gains[:, j * width : (j + 1) * width] = gain[:, part(me ^ j, width)]
    for block, (here, there) in enumerate(((own, mirrored), (mirrored, own))):
        for k in range(4):
            at = slice(k * tile, (k + 1) * tile)
            mine = jnp.concatenate([ref[at, :] for ref in here], axis=1)
            other = jnp.concatenate([ref[at, :] for ref in there], axis=1)
            combined = mine.astype(F32) + dot(other, choose[...])
            mean = jnp.sum(combined * combined, axis=1, keepdims=True) * (1.0 / full)
            inv_scale = lax.rsqrt(mean + EPSILON)
            hat = combined * inv_scale
            at_both = slice(block * rows + k * tile, block * rows + (k + 1) * tile)
            normalized[at_both, :] = (hat * gains[...]).astype(BF16)
            scaled = grad_norm[at_both, :].astype(F32) * gains[...]
            row_total = jnp.sum(scaled * hat, axis=1, keepdims=True) * (1.0 / full)
            if block == 0:
                grad_gated[at, :] = inv_scale * (scaled[:, :width] - hat[:, :width] * row_total)
            else:
                grad_comb = (inv_scale * (scaled - hat * row_total)).astype(BF16)
                grad_gated[at, :] += dot(grad_comb, choose[:width, :], LAST_DOT)
    gate = gate_pre[...]
    sigmoid = 1.0 / (1.0 + jnp.exp(-gate))
    total = grad_gated[...]
    upstream[...] = (total * (gate * sigmoid)).astype(BF16)
    grad_gate_pre[...] = (total * level_3[...].astype(F32) * sigmoid * (1.0 + gate * (1.0 - sigmoid))).astype(BF16)
    odd, far = place[0] % 2, rows - EDGE
    first[...] = upstream[pl.ds(pl.multiple_of((1 - odd) * far, 16), EDGE), :]
    second[...] = upstream[pl.ds(pl.multiple_of(odd * far, 16), EDGE), :]


def output_kernel(channels, place, normalized, w_out, block_in, output):
    me = place[1]
    rows, width = block_in.shape
    total = block_in[...].astype(F32)
    for j in range(channels):
        total += dot(normalized[:rows, j * width : (j + 1) * width], w_out[part(me ^ j, width), :])
    output[...] = total.astype(BF16)


def products_kernel(channels, place, normalized, cotangent, mirrored_cotangent, grad_gate_pre, *refs):
    mains = refs[:channels]
    whole_out, gate_sent, gate_kept, whole_gate = refs[channels:]
    me, side = place[1], (place[0] // 2) % 2
    rows, width = cotangent.shape
    for j in range(channels // 2):
        block = (side * (channels // 2) + j) ^ me
        columns = part(block, width)
        whole_out[j * width : (j + 1) * width, :] = dot(
            normalized[:rows, columns], cotangent[...], ROWS_DOT
        ) + dot(normalized[rows:, columns], mirrored_cotangent[...], ROWS_DOT)
    for j in range(channels):
        whole_gate[part(me ^ j, width), :] = dot(mains[j][...], grad_gate_pre[...], ROWS_DOT)
    half = whole_gate.shape[0] // 2
    gate_sent[...] = whole_gate[part(1 - side, half), :].astype(BF16)
    gate_kept[...] = whole_gate[part(side, half), :]


def backward_kernel(channels, place, upstream, first, second, conv_w, *refs):
    mains, (saved, sent, kept, whole, grad_3, grad_2, grad_1, levels) = refs[:channels], refs[channels:]
    levels[...] = saved[...].astype(F32)
    me, odd = place[1], place[0] % 2
    rows, width = upstream.shape
    fore = BACK_FORE[3]
    even = (odd == 0).astype(F32)
    early, late = first[...].astype(F32), second[...].astype(F32)
    grad_3[:fore] = (early * (1.0 - even) + late * even)[EDGE - fore :]
    grad_3[fore : fore + rows] = upstream[...].astype(F32)
    grad_3[fore + rows :] = early * even + late * (1.0 - even)
    half = whole.shape[0] // 2
    for top in (half - SPARE, 2 * half - SPARE):
        whole[top : top + SPARE, :] = jnp.zeros((SPARE, width), F32)
    grads = (None, grad_1, grad_2, grad_3)
    grad_0 = None
    for number in (2, 1, 0):
        dilation, source = DILATIONS[number], grads[number + 1]
        top = sum(saved_rows(rows, below) for below in range(number))
        fore = BACK_FORE[number + 1]
        here = source[fore : fore + rows]
        for tap in range(4):
            begin = top + FORE[number] + (tap - 2) * dilation
            row = half - SPARE + 4 * number + tap
            whole[row : row + 1, :] = jnp.sum(here * levels[begin : begin + rows], axis=0, keepdims=True)
        count = BACK_FORE[number] + rows + BACK_AFT[number]
        total = jnp.zeros((count, width), F32)
        for tap in range(4):
            begin = fore - BACK_FORE[number] - (tap - 2) * dilation
            total += conv_w[number, tap : tap + 1, :] * source[begin : begin + count]
        if number:
            grads[number][...] = keep_inside(total, place, BACK_FORE[number], rows)
        else:
            grad_0 = total.astype(BF16)
    for j in range(channels):
        block = me ^ j
        start = (block // (channels // 2)) * half + (block % (channels // 2)) * width
        whole[pl.ds(pl.multiple_of(start, SPARE), width), :] = dot(mains[j][...], grad_0, ROWS_DOT)
    sent[...] = whole[part(1 - odd, half), :].astype(BF16)
    kept[...] = whole[part(odd, half), :]


def split(total, bit):
    half = total.shape[0] // 2
    low, high = total[:half], total[half:]
    first = jnp.broadcast_to(bit, low.shape) == 0
    return jnp.where(first, high, low), jnp.where(first, low, high)


def join(mine, other, bit):
    first = jnp.broadcast_to(bit, mine.shape) == 0
    return jnp.where(first, mine, other), jnp.where(first, other, mine)


def pair_kernel(place, gate_kept, gate_other, out, sent, kept):
    gate = gate_kept[...] + gate_other[...].astype(F32)
    first = jnp.broadcast_to(place[0] % 2, gate.shape) == 0
    sent[...] = jnp.where(first, out[...], gate).astype(BF16)
    kept[...] = jnp.where(first, gate, out[...])


def step_kernel(plan, place, *refs):
    sources, targets = refs[: 2 * len(plan)], list(refs[2 * len(plan) :])
    for k, (done, after) in enumerate(plan):
        mine, other = sources[2 * k : 2 * k + 2]
        rows = mine.shape[0]
        if after is not None and after[0] == "pair":
            bit, half = (place[0] // done[1]) % 2, rows // 2
            for number in range(2):
                target = targets.pop(0)
                target[part(bit, half, 16), :] = mine[number * half : (number + 1) * half]
                target[part(1 - bit, half, 16), :] = other[number * half : (number + 1) * half]
        elif done[0] == "double":
            bit = (place[0] // done[1]) % 2
            target = targets.pop(0)
            count = rows - SPARE if after is not None and after[0] == "take" else rows
            target[part(bit, count, 16), :] = mine[:count]
            target[part(1 - bit, count, 16), :] = other[:count]
            if count < rows:
                taps = targets.pop(0)
                first = mine[count:].astype(F32), other[count:].astype(F32)
                low, _ = join(*first, bit)
                for number in range(taps.shape[0]):
                    taps[number] = low[number * taps.shape[1] : (number + 1) * taps.shape[1]]
        elif after is not None and after[0] == "halve":
            half = rows // 2
            bit = (place[0] // after[1]) % 2
            for way in (1 - bit, bit):
                at = part(way, half, 16)
                target = targets.pop(0)
                target[...] = (mine[at, :] + other[at, :].astype(F32)).astype(target.dtype)
        else:
            targets.pop(0)[...] = (mine[...] + other[...].astype(F32)).astype(BF16)


def advance(place, items, taps):
    width = items[0][2].shape[1]
    outs, counts = [], []
    for done, after, mine, _ in items:
        rows = mine.shape[0] * (1 if done[0] == "halve" else 2)
        if after is not None and after[0] == "halve":
            outs += [((rows // 2, width), BF16), ((rows // 2, width), F32)]
            counts.append(2)
        elif after is not None and after[0] == "take":
            outs += [((rows - 2 * SPARE, width), BF16), ((*taps, width), F32)]
            counts.append(2)
        elif after is not None and after[0] == "pair":
            outs += [((rows // 2, width), BF16)] * 2
            counts.append(2)
        else:
            outs.append(((rows, width), BF16))
            counts.append(1)
    arrays = [array for item in items for array in item[2:]]
    plan = [item[:2] for item in items]
    fits = True
    for done, after, mine, _ in items:
        rows = mine.shape[0]
        if done[0] == "double":
            fits &= rows % 16 == 0
        elif after is not None and after[0] == "halve":
            fits &= rows % 32 == 0
        else:
            fits &= rows % 8 == 0
    if fits:
        results = run(functools.partial(step_kernel, plan), place, arrays, outs)
    else:
        results = []
        for done, after, mine, other in items:
            mine, other = mine.astype(F32), other.astype(F32)
            if done[0] == "halve":
                total = mine + other
            else:
                total = jnp.concatenate(join(mine, other, seq_bit(done[1])), axis=0)
            if after is not None and after[0] == "halve":
                sent, kept = split(total, seq_bit(after[1]))
                results += [sent.astype(BF16), kept]
            elif after is not None and after[0] == "take":
                half = total.shape[0] // 2
                results += [
                    jnp.concatenate([total[: half - SPARE], total[half:-SPARE]], axis=0).astype(BF16),
                    total[half - SPARE : half - SPARE + taps[0] * taps[1]].reshape(*taps, width),
                ]
            else:
                results.append(total.astype(BF16))
    grouped = []
    for count in counts:
        grouped.append(results[:count])
        results = results[count:]
    return grouped


def exchange(block, axis, distance):
    count = lax.axis_size(axis)
    return lax.ppermute(block, axis, [(i, i ^ distance) for i in range(count)])


def distances(axis):
    return [1 << bit for bit in range(lax.axis_size(axis).bit_length() - 1)]


def mirror(block):
    count = lax.axis_size("seq")
    return lax.ppermute(block, "seq", [(i, count - 1 - i) for i in range(count)])


def swap_edges(first, second):
    count = lax.axis_size("seq")
    received = []
    for turn, block in enumerate((first, second)):
        route = []
        for low in range(turn, count - 1, 2):
            route += [(low, low + 1), (low + 1, low)]
        received.append(lax.ppermute(block, "seq", route))
    return received


def together(*values):
    return lax.optimization_barrier(values)


def seq_bit(distance):
    return (lax.axis_index("seq") & distance) // distance


def local(tokens, hidden, embedding, w_in, w_gate, conv_w, channel_order, gain, w_out, cotangent):
    rows, width = hidden.shape
    full = gain.shape[0]
    channels = full // width
    cross = channels // 2
    steps = distances("seq")
    block = ((rows, width), BF16)
    place = jnp.stack([lax.axis_index("seq"), lax.axis_index("ch"), lax.axis_size("seq")]).astype(jnp.int32)

    cotangent_x = exchange(cotangent, "ch", cross)
    mirrored_cotangent = mirror(cotangent)
    inputs = (tokens.reshape(1, rows), hidden, embedding, w_out)
    local_input, first, second, w_half = run(
        input_kernel,
        place,
        inputs,
        [block, ((EDGE, width), BF16), ((EDGE, width), BF16), ((full // 2, width), BF16)],
        [pltpu.VMEM((16, width), F32), *fetch_scratch(inputs)],
        megabytes=60,
        fetched=4,
    )
    input_x = exchange(local_input, "ch", cross)
    input_core = exchange(local_input, "ch", 1)
    choose = run(
        functools.partial(setup_kernel, width),
        place,
        (channel_order.reshape(1, full),),
        [((full, full), BF16)],
        gflop=2.0,
    )[0]
    first, second, cotangent_x = together(first, second, cotangent_x)
    near = swap_edges(first, second)
    mirrored_cotangent, *near = together(mirrored_cotangent, *near)
    near = jnp.concatenate(near, axis=0)
    far = exchange(near, "ch", cross)
    w_half, far = together(w_half, far)
    w_x_mine = exchange(w_half, "ch", cross)
    w_x_other = exchange(w_x_mine, "seq", 1)
    edges = jnp.concatenate([near, far], axis=0)
    mirrored_cotangent = run(flip_kernel, place, (mirrored_cotangent,), [block], gflop=1.0)[0]
    mirrored_cotangent, input_core, choose = together(mirrored_cotangent, input_core, choose)
    mains = [local_input, input_core, input_x, exchange(input_x, "ch", 1)]

    projected, gate_pre, w_in_on = run(
        functools.partial(project_kernel, channels),
        place,
        (*mains, w_in, w_gate),
        [((rows, width), F32)] * 2 + [(w_in.shape, BF16)],
        gflop=6.0,
    )
    edges_core = exchange(edges, "ch", 1)
    levels, level_3, gated = run(
        functools.partial(forward_kernel, channels),
        place,
        (edges, edges_core, w_in_on, projected, gate_pre, conv_w),
        [((sum(saved_rows(rows, number) for number in range(3)), width), BF16), block, block],
        [pltpu.VMEM((saved_rows(rows, number), width), F32) for number in range(4)],
        gflop=0.4,
    )
    mirrored_cotangent_x = exchange(mirrored_cotangent, "ch", cross)
    gated_x = exchange(gated, "ch", cross)
    mirrored, mirrored_cotangent_x, gated_x = together(mirror(gated), mirrored_cotangent_x, gated_x)
    mirrored = run(flip_kernel, place, (mirrored,), [block], gflop=12.0)[0]
    mirrored_x = exchange(mirrored, "ch", cross)
    gated_all = [gated, exchange(gated, "ch", 1), gated_x, exchange(gated_x, "ch", 1)]
    cotangent_all = [cotangent, exchange(cotangent, "ch", 1), cotangent_x, exchange(cotangent_x, "ch", 1)]
    mirrored_cotangent_all = [
        mirrored_cotangent,
        exchange(mirrored_cotangent, "ch", 1),
        mirrored_cotangent_x,
        exchange(mirrored_cotangent_x, "ch", 1),
    ]
    grad_norm = run(
        functools.partial(norm_grad_kernel, channels),
        place,
        (
            *cotangent_all,
            *mirrored_cotangent_all,
            w_out,
            exchange(w_out, "ch", 1),
            w_x_mine,
            w_x_other,
            exchange(w_x_mine, "ch", 1),
            exchange(w_x_other, "ch", 1),
        ),
        [((2 * rows, full), BF16)],
        [pltpu.VMEM((full, width), BF16)] * 2,
        gflop=2.1,
    )[0]
    mirrored_x, grad_norm = together(mirrored_x, grad_norm)
    mirrored_all = [mirrored, exchange(mirrored, "ch", 1), mirrored_x, exchange(mirrored_x, "ch", 1)]

    normalized, upstream, grad_gate_pre, first, second = run(
        functools.partial(combine_kernel, channels),
        place,
        (*gated_all, *mirrored_all, grad_norm, choose, gain.reshape(1, full), gate_pre, level_3),
        [((2 * rows, full), BF16), block, block, ((EDGE, width), BF16), ((EDGE, width), BF16)],
        [pltpu.VMEM((1, full), F32), pltpu.VMEM((rows, width), F32)],
        gflop=2.5,
    )
    first, second = swap_edges(first, second)
    out_half, gate_sent, gate_kept = run(
        functools.partial(products_kernel, channels),
        place,
        (normalized, cotangent, mirrored_cotangent, grad_gate_pre, *mains),
        [
            ((full // 2, width), F32),
            ((full // 2, width), BF16),
            ((full // 2, width), F32),
        ],
        [pltpu.VMEM((full, width), F32)],
        gflop=0.8,
    )
    gate_sent, first, second = together(gate_sent, first, second)
    gate_other = exchange(gate_sent, "seq", steps[1])
    half = full // 2 + SPARE
    in_sent, in_kept = run(
        functools.partial(backward_kernel, channels),
        place,
        (upstream, first, second, conv_w, *mains, levels),
        [((half, width), BF16), ((half, width), F32)],
        [pltpu.VMEM((2 * half, width), F32)]
        + [pltpu.VMEM((BACK_FORE[k] + rows + BACK_AFT[k], width), F32) for k in (3, 2, 1)]
        + [pltpu.VMEM(levels.shape, F32)],
        gflop=0.5,
    )
    output = run(
        functools.partial(output_kernel, channels),
        place,
        (normalized, w_out, local_input),
        [block],
        gflop=0.3,
    )[0]

    down = [("halve", distance) for distance in steps]
    up = [("double", distance) for distance in steps[::-1]]
    both_steps = steps[:1] + steps[2:]
    both_route = [("halve", distance) for distance in both_steps]
    both_route += [("double", distance) for distance in [*both_steps[::-1], steps[1]]] + [("pair",)]
    gate_other, in_kept = together(gate_other, in_kept)
    half_shape = (full // 2, width)
    both_sent, both_kept = run(
        pair_kernel, place, (gate_kept, gate_other, out_half), [(half_shape, BF16), (half_shape, F32)]
    )
    in_route = down + up + [("take",)]
    sums = [[in_route, in_sent, in_kept, None], [both_route, both_sent, both_kept, None]]
    results = [None, None]
    for number in range(len(in_route) - 1):
        for k, (route, sent, kept, _) in enumerate(sums):
            if results[k] is not None:
                continue
            done, upcoming = route[number : number + 2]
            other = exchange(sent, "seq", done[1])
            prepared = advance(place, [(done, upcoming, kept, other)], conv_w.shape[:2])[0]
            if upcoming[0] in ("halve", "double"):
                sent, kept = prepared if len(prepared) == 2 else prepared * 2
                sums[k] = [route, sent, kept, other]
            else:
                results[k] = prepared
        if number < 3 and results[1] is None:
            sums[0][1], sums[1][1] = together(sums[0][1], sums[1][1])
    (grad_in, grad_conv), (sum_gate, sum_out) = results
    return output, grad_in, sum_gate, sum_out, grad_conv


def solution(mesh):
    placed = (
        P("seq"),
        P("seq", "ch"),
        P(None, "ch"),
        P(None, "ch"),
        P(None, "ch"),
        P(None, None, "ch"),
        P(),
        P(),
        P(None, "ch"),
        P("seq", "ch"),
    )
    return jax.shard_map(
        local,
        mesh=mesh,
        in_specs=placed,
        out_specs=(
            P("seq", "ch"),
            P(None, "ch"),
            P(None, "ch"),
            P(None, "ch"),
            P(None, None, "ch"),
        ),
        check_vma=False,
    )
```

```python
import functools

import jax
import jax.numpy as jnp
from jax import lax
from jax.experimental import pallas as pl
from jax.experimental.pallas import tpu as pltpu
from jax.sharding import PartitionSpec as P

DILATIONS = (1, 8, 64)
EPSILON = 1e-06
FORE = (160, 144, 128, 0)
AFT = (80, 72, 64, 0)
BACK_FORE = (0, 8, 16, 80)
BACK_AFT = (0, 8, 24, 160)
EDGE = 160
SPARE = 64

BF16, F32 = jnp.bfloat16, jnp.float32
ROWS_DOT = (((0,), (0,)), ((), ()))
LAST_DOT = (((1,), (1,)), ((), ()))


def dot(left, right, dims=(((1,), (0,)), ((), ()))):
    return lax.dot_general(left, right, dims, preferred_element_type=F32)


def run(body, place, operands, outs, scratch=(), megabytes=8, gflop=0.1, fetched=0):
    moved = sum(x.size * x.dtype.itemsize for x in operands)
    return pl.pallas_call(
        body,
        out_shape=[jax.ShapeDtypeStruct(shape, dtype) for shape, dtype in outs],
        in_specs=[pl.BlockSpec(memory_space=pltpu.SMEM)]
        + [pl.BlockSpec(memory_space=pltpu.VMEM)] * (len(operands) - fetched)
        + [pl.BlockSpec(memory_space=pltpu.HBM)] * fetched,
        out_specs=[pl.BlockSpec(memory_space=pltpu.VMEM)] * len(outs),
        scratch_shapes=list(scratch),
        compiler_params=pltpu.CompilerParams(vmem_limit_bytes=megabytes << 20),
        cost_estimate=pl.CostEstimate(flops=int(gflop * 1e9), bytes_accessed=moved, transcendentals=0),
    )(place, *operands)


def fetch(sources, targets, semaphores):
    copies = [
        pltpu.make_async_copy(source, target, semaphores.at[k])
        for k, (source, target) in enumerate(zip(sources, targets))
    ]
    for copy in copies:
        copy.start()
    return copies


def fetch_scratch(operands):
    return [pltpu.VMEM(x.shape, x.dtype) for x in operands] + [pltpu.SemaphoreType.DMA((len(operands),))]


def part(index, size, multiple=None):
    return pl.ds(pl.multiple_of(index * size, multiple or size), size)


def saved_rows(rows, number):
    return -(-(FORE[number] + rows + AFT[number]) // 16) * 16


def anti_identity(rows):
    down = lax.broadcasted_iota(jnp.int32, (rows, rows), 0)
    across = lax.broadcasted_iota(jnp.int32, (rows, rows), 1)
    return (down + across == rows - 1).astype(F32).astype(BF16)


def input_kernel(place, tokens_hbm, hidden_hbm, embedding_hbm, w_out_hbm, block_in, first, second, w_half, *scratch):
    padded, tokens, hidden, embedding, w_out, semaphores = scratch
    copies = fetch(
        (tokens_hbm, hidden_hbm, embedding_hbm, w_out_hbm), (tokens, hidden, embedding, w_out), semaphores
    )
    bases, rows = embedding.shape[0], hidden.shape[0]
    padded[...] = jnp.zeros_like(padded)
    for copy in copies[:3]:
        copy.wait()
    padded[:bases] = embedding[...].astype(F32)
    base = lax.broadcasted_iota(jnp.int32, (padded.shape[0], rows), 0)
    one_hot = (base == tokens[...]).astype(F32).astype(BF16)
    shift = dot(one_hot, padded[...].astype(BF16), ROWS_DOT)
    block_in[...] = (hidden[...].astype(F32) + shift).astype(BF16)
    odd, far = place[0] % 2, rows - EDGE
    first[...] = block_in[pl.ds(pl.multiple_of((1 - odd) * far, 16), EDGE), :]
    second[...] = block_in[pl.ds(pl.multiple_of(odd * far, 16), EDGE), :]
    copies[3].wait()
    w_half[...] = w_out[part(odd, w_half.shape[0]), :]


def setup_kernel(width, place, order, choose):
    me, full = place[1], order.shape[1]
    down = lax.broadcasted_iota(jnp.int32, (width, width), 0)
    for j in range(full // width):
        for i in range(full // width):
            wanted = order[:, part(me ^ i, width)]
            choose[j * width : (j + 1) * width, i * width : (i + 1) * width] = (
                (down + (me ^ j) * width == wanted).astype(F32).astype(BF16)
            )


def project_kernel(channels, place, *refs):
    mains, (w_in, w_gate, projected, gate_pre, w_in_on) = refs[:channels], refs[channels:]
    me, width = place[1], mains[0].shape[1]
    for weight, out in ((w_in, projected), (w_gate, gate_pre)):
        total = dot(mains[0][...], weight[part(me, width), :])
        for j in range(1, channels):
            total += dot(mains[j][...], weight[part(me ^ j, width), :])
        out[...] = total
    w_in_on[...] = w_in[...]


def keep_inside(total, place, before, rows):
    position = lax.broadcasted_iota(jnp.int32, total.shape, 0) + (place[0] * rows - before)
    return jnp.where((position >= 0) & (position < place[2] * rows), total, 0.0)


def forward_kernel(channels, place, edges, edges_core, w_in, projected, gate_pre, conv_w, *outs):
    levels, level_3, gated, *stages = outs
    me, odd = place[1], place[0] % 2
    rows, width = projected.shape
    left = jnp.zeros((EDGE, width), F32)
    right = jnp.zeros((AFT[0], width), F32)
    for j in range(channels):
        source = edges_core if j % 2 else edges
        base = (j // 2) * 2 * EDGE
        weight = w_in[part(me ^ j, width), :]
        left += dot(source[pl.ds(pl.multiple_of(base + (1 - odd) * EDGE, 16), EDGE), :], weight)
        right += dot(source[pl.ds(pl.multiple_of(base + odd * EDGE, 16), AFT[0]), :], weight)
    source = stages[0]
    source[:EDGE] = left
    source[EDGE : EDGE + rows] = projected[...]
    source[EDGE + rows :] = right
    top = 0
    for number, dilation in enumerate(DILATIONS):
        target = stages[number + 1]
        levels[top : top + source.shape[0], :] = source[...].astype(BF16)
        top += source.shape[0]
        shift = FORE[number] - FORE[number + 1]
        count = FORE[number + 1] + rows + AFT[number + 1]
        total = jnp.zeros((count, width), F32)
        for tap in range(4):
            begin = shift + (tap - 2) * dilation
            total += conv_w[number, tap : tap + 1, :] * source[begin : begin + count]
        if FORE[number + 1]:
            total = keep_inside(total, place, FORE[number + 1], rows)
        target[:count] = total
        if count < target.shape[0]:
            target[count:] = jnp.zeros((target.shape[0] - count, width), F32)
        source = target
    gate = gate_pre[...]
    level_3[...] = source[...].astype(BF16)
    gated[...] = (source[...] * (gate / (1.0 + jnp.exp(-gate)))).astype(BF16)


def flip_kernel(place, block, flipped):
    flipped[...] = dot(anti_identity(block.shape[0]), block[...]).astype(BF16)


def norm_grad_kernel(channels, place, *refs):
    own, mirrored = refs[:channels], refs[channels : 2 * channels]
    near, near_core, mine, other, mine_core, other_core, out, far, far_core = refs[2 * channels :]
    me, side, half = place[1], place[0] % 2, mine.shape[0]
    for whole, first, second in ((far, mine, other), (far_core, mine_core, other_core)):
        whole[part(side, half), :] = first[...]
        whole[part(1 - side, half), :] = second[...]
    weights = (near, near_core, far, far_core)
    rows, width = own[0].shape
    for block, cotangents in enumerate((own, mirrored)):
        for i in range(channels):
            total = jnp.zeros((rows, width), F32)
            for j in range(channels):
                total += dot(cotangents[j][...], weights[j][part(i ^ me, width), :], LAST_DOT)
            out[block * rows : (block + 1) * rows, i * width : (i + 1) * width] = total.astype(BF16)


def combine_kernel(channels, place, *refs):
    own, mirrored = refs[:channels], refs[channels : 2 * channels]
    grad_norm, choose, gain, gate_pre, level_3 = refs[2 * channels : 2 * channels + 5]
    normalized, upstream, grad_gate_pre, first, second, gains, grad_gated = refs[2 * channels + 5 :]
    me = place[1]
    rows, width = own[0].shape
    full = channels * width
    tile = rows // 4
    for j in range(channels):
        gains[:, j * width : (j + 1) * width] = gain[:, part(me ^ j, width)]
    for block, (here, there) in enumerate(((own, mirrored), (mirrored, own))):
        for k in range(4):
            at = slice(k * tile, (k + 1) * tile)
            mine = jnp.concatenate([ref[at, :] for ref in here], axis=1)
            other = jnp.concatenate([ref[at, :] for ref in there], axis=1)
            combined = mine.astype(F32) + dot(other, choose[...])
            mean = jnp.sum(combined * combined, axis=1, keepdims=True) * (1.0 / full)
            inv_scale = lax.rsqrt(mean + EPSILON)
            hat = combined * inv_scale
            at_both = slice(block * rows + k * tile, block * rows + (k + 1) * tile)
            normalized[at_both, :] = (hat * gains[...]).astype(BF16)
            scaled = grad_norm[at_both, :].astype(F32) * gains[...]
            row_total = jnp.sum(scaled * hat, axis=1, keepdims=True) * (1.0 / full)
            if block == 0:
                grad_gated[at, :] = inv_scale * (scaled[:, :width] - hat[:, :width] * row_total)
            else:
                grad_comb = (inv_scale * (scaled - hat * row_total)).astype(BF16)
                grad_gated[at, :] += dot(grad_comb, choose[:width, :], LAST_DOT)
    gate = gate_pre[...]
    sigmoid = 1.0 / (1.0 + jnp.exp(-gate))
    total = grad_gated[...]
    upstream[...] = (total * (gate * sigmoid)).astype(BF16)
    grad_gate_pre[...] = (total * level_3[...].astype(F32) * sigmoid * (1.0 + gate * (1.0 - sigmoid))).astype(BF16)
    odd, far = place[0] % 2, rows - EDGE
    first[...] = upstream[pl.ds(pl.multiple_of((1 - odd) * far, 16), EDGE), :]
    second[...] = upstream[pl.ds(pl.multiple_of(odd * far, 16), EDGE), :]


def output_kernel(channels, place, normalized, w_out, block_in, output):
    me = place[1]
    rows, width = block_in.shape
    total = block_in[...].astype(F32)
    for j in range(channels):
        total += dot(normalized[:rows, j * width : (j + 1) * width], w_out[part(me ^ j, width), :])
    output[...] = total.astype(BF16)


def products_kernel(channels, place, normalized, cotangent, mirrored_cotangent, grad_gate_pre, *refs):
    mains = refs[:channels]
    out_sent, out_kept, gate_sent, gate_kept, whole_out, whole_gate = refs[channels:]
    me, side = place[1], (place[0] // 2) % 2
    rows, width = cotangent.shape
    for j in range(channels // 2):
        block = (side * (channels // 2) + j) ^ me
        columns = part(block, width)
        whole_out[j * width : (j + 1) * width, :] = dot(
            normalized[:rows, columns], cotangent[...], ROWS_DOT
        ) + dot(normalized[rows:, columns], mirrored_cotangent[...], ROWS_DOT)
    half = whole_out.shape[0] // 2
    bit = place[0] % 2
    out_sent[...] = whole_out[part(1 - bit, half), :].astype(BF16)
    out_kept[...] = whole_out[part(bit, half), :]
    for j in range(channels):
        whole_gate[part(me ^ j, width), :] = dot(mains[j][...], grad_gate_pre[...], ROWS_DOT)
    half = whole_gate.shape[0] // 2
    gate_sent[...] = whole_gate[part(1 - side, half), :].astype(BF16)
    gate_kept[...] = whole_gate[part(side, half), :]


def backward_kernel(channels, place, upstream, first, second, conv_w, *refs):
    mains, (saved, sent, kept, whole, grad_3, grad_2, grad_1, levels) = refs[:channels], refs[channels:]
    levels[...] = saved[...].astype(F32)
    me, odd = place[1], place[0] % 2
    rows, width = upstream.shape
    fore = BACK_FORE[3]
    even = (odd == 0).astype(F32)
    early, late = first[...].astype(F32), second[...].astype(F32)
    grad_3[:fore] = (early * (1.0 - even) + late * even)[EDGE - fore :]
    grad_3[fore : fore + rows] = upstream[...].astype(F32)
    grad_3[fore + rows :] = early * even + late * (1.0 - even)
    half = whole.shape[0] // 2
    for top in (half - SPARE, 2 * half - SPARE):
        whole[top : top + SPARE, :] = jnp.zeros((SPARE, width), F32)
    grads = (None, grad_1, grad_2, grad_3)
    grad_0 = None
    for number in (2, 1, 0):
        dilation, source = DILATIONS[number], grads[number + 1]
        top = sum(saved_rows(rows, below) for below in range(number))
        fore = BACK_FORE[number + 1]
        here = source[fore : fore + rows]
        for tap in range(4):
            begin = top + FORE[number] + (tap - 2) * dilation
            row = half - SPARE + 4 * number + tap
            whole[row : row + 1, :] = jnp.sum(here * levels[begin : begin + rows], axis=0, keepdims=True)
        count = BACK_FORE[number] + rows + BACK_AFT[number]
        total = jnp.zeros((count, width), F32)
        for tap in range(4):
            begin = fore - BACK_FORE[number] - (tap - 2) * dilation
            total += conv_w[number, tap : tap + 1, :] * source[begin : begin + count]
        if number:
            grads[number][...] = keep_inside(total, place, BACK_FORE[number], rows)
        else:
            grad_0 = total.astype(BF16)
    for j in range(channels):
        block = me ^ j
        start = (block // (channels // 2)) * half + (block % (channels // 2)) * width
        whole[pl.ds(pl.multiple_of(start, SPARE), width), :] = dot(mains[j][...], grad_0, ROWS_DOT)
    sent[...] = whole[part(1 - odd, half), :].astype(BF16)
    kept[...] = whole[part(odd, half), :]


def split(total, bit):
    half = total.shape[0] // 2
    low, high = total[:half], total[half:]
    first = jnp.broadcast_to(bit, low.shape) == 0
    return jnp.where(first, high, low), jnp.where(first, low, high)


def join(mine, other, bit):
    first = jnp.broadcast_to(bit, mine.shape) == 0
    return jnp.where(first, mine, other), jnp.where(first, other, mine)


def step_kernel(plan, place, *refs):
    sources, targets = refs[: 2 * len(plan)], list(refs[2 * len(plan) :])
    for k, (done, after) in enumerate(plan):
        mine, other = sources[2 * k : 2 * k + 2]
        rows = mine.shape[0]
        if done[0] == "double":
            bit = (place[0] // done[1]) % 2
            target = targets.pop(0)
            count = rows - SPARE if after is not None and after[0] == "take" else rows
            target[part(bit, count, 16), :] = mine[:count]
            target[part(1 - bit, count, 16), :] = other[:count]
            if count < rows:
                taps = targets.pop(0)
                first = mine[count:].astype(F32), other[count:].astype(F32)
                low, _ = join(*first, bit)
                for number in range(taps.shape[0]):
                    taps[number] = low[number * taps.shape[1] : (number + 1) * taps.shape[1]]
        elif after is not None and after[0] == "halve":
            half = rows // 2
            bit = (place[0] // after[1]) % 2
            for way in (1 - bit, bit):
                at = part(way, half, 16)
                target = targets.pop(0)
                target[...] = (mine[at, :] + other[at, :].astype(F32)).astype(target.dtype)
        else:
            targets.pop(0)[...] = (mine[...] + other[...].astype(F32)).astype(BF16)


def advance(place, items, taps):
    width = items[0][2].shape[1]
    outs, counts = [], []
    for done, after, mine, _ in items:
        rows = mine.shape[0] * (1 if done[0] == "halve" else 2)
        if after is not None and after[0] == "halve":
            outs += [((rows // 2, width), BF16), ((rows // 2, width), F32)]
            counts.append(2)
        elif after is not None and after[0] == "take":
            outs += [((rows - 2 * SPARE, width), BF16), ((*taps, width), F32)]
            counts.append(2)
        else:
            outs.append(((rows, width), BF16))
            counts.append(1)
    arrays = [array for item in items for array in item[2:]]
    plan = [item[:2] for item in items]
    fits = True
    for done, after, mine, _ in items:
        rows = mine.shape[0]
        if done[0] == "double":
            fits &= rows % 16 == 0
        elif after is not None and after[0] == "halve":
            fits &= rows % 32 == 0
        else:
            fits &= rows % 8 == 0
    if fits:
        results = run(functools.partial(step_kernel, plan), place, arrays, outs)
    else:
        results = []
        for done, after, mine, other in items:
            mine, other = mine.astype(F32), other.astype(F32)
            if done[0] == "halve":
                total = mine + other
            else:
                total = jnp.concatenate(join(mine, other, seq_bit(done[1])), axis=0)
            if after is not None and after[0] == "halve":
                sent, kept = split(total, seq_bit(after[1]))
                results += [sent.astype(BF16), kept]
            elif after is not None and after[0] == "take":
                half = total.shape[0] // 2
                results += [
                    jnp.concatenate([total[: half - SPARE], total[half:-SPARE]], axis=0).astype(BF16),
                    total[half - SPARE : half - SPARE + taps[0] * taps[1]].reshape(*taps, width),
                ]
            else:
                results.append(total.astype(BF16))
    grouped = []
    for count in counts:
        grouped.append(results[:count])
        results = results[count:]
    return grouped


def exchange(block, axis, distance):
    count = lax.axis_size(axis)
    return lax.ppermute(block, axis, [(i, i ^ distance) for i in range(count)])


def distances(axis):
    return [1 << bit for bit in range(lax.axis_size(axis).bit_length() - 1)]


def mirror(block):
    count = lax.axis_size("seq")
    return lax.ppermute(block, "seq", [(i, count - 1 - i) for i in range(count)])


def swap_edges(first, second):
    count = lax.axis_size("seq")
    received = []
    for turn, block in enumerate((first, second)):
        route = []
        for low in range(turn, count - 1, 2):
            route += [(low, low + 1), (low + 1, low)]
        received.append(lax.ppermute(block, "seq", route))
    return received


def together(*values):
    return lax.optimization_barrier(values)


def seq_bit(distance):
    return (lax.axis_index("seq") & distance) // distance


def local(tokens, hidden, embedding, w_in, w_gate, conv_w, channel_order, gain, w_out, cotangent):
    rows, width = hidden.shape
    full = gain.shape[0]
    channels = full // width
    cross = channels // 2
    steps = distances("seq")
    block = ((rows, width), BF16)
    place = jnp.stack([lax.axis_index("seq"), lax.axis_index("ch"), lax.axis_size("seq")]).astype(jnp.int32)

    cotangent_x = exchange(cotangent, "ch", cross)
    mirrored_cotangent = mirror(cotangent)
    inputs = (tokens.reshape(1, rows), hidden, embedding, w_out)
    local_input, first, second, w_half = run(
        input_kernel,
        place,
        inputs,
        [block, ((EDGE, width), BF16), ((EDGE, width), BF16), ((full // 2, width), BF16)],
        [pltpu.VMEM((16, width), F32), *fetch_scratch(inputs)],
        megabytes=60,
        fetched=4,
    )
    input_x = exchange(local_input, "ch", cross)
    input_core = exchange(local_input, "ch", 1)
    choose = run(
        functools.partial(setup_kernel, width),
        place,
        (channel_order.reshape(1, full),),
        [((full, full), BF16)],
        gflop=2.0,
    )[0]
    first, second, cotangent_x = together(first, second, cotangent_x)
    near = swap_edges(first, second)
    mirrored_cotangent, *near = together(mirrored_cotangent, *near)
    near = jnp.concatenate(near, axis=0)
    far = exchange(near, "ch", cross)
    w_half, far = together(w_half, far)
    w_x_mine = exchange(w_half, "ch", cross)
    w_x_other = exchange(w_x_mine, "seq", 1)
    edges = jnp.concatenate([near, far], axis=0)
    mirrored_cotangent = run(flip_kernel, place, (mirrored_cotangent,), [block], gflop=1.0)[0]
    mirrored_cotangent, input_core, choose = together(mirrored_cotangent, input_core, choose)
    mains = [local_input, input_core, input_x, exchange(input_x, "ch", 1)]

    projected, gate_pre, w_in_on = run(
        functools.partial(project_kernel, channels),
        place,
        (*mains, w_in, w_gate),
        [((rows, width), F32)] * 2 + [(w_in.shape, BF16)],
        gflop=6.0,
    )
    edges_core = exchange(edges, "ch", 1)
    levels, level_3, gated = run(
        functools.partial(forward_kernel, channels),
        place,
        (edges, edges_core, w_in_on, projected, gate_pre, conv_w),
        [((sum(saved_rows(rows, number) for number in range(3)), width), BF16), block, block],
        [pltpu.VMEM((saved_rows(rows, number), width), F32) for number in range(4)],
        gflop=0.4,
    )
    mirrored_cotangent_x = exchange(mirrored_cotangent, "ch", cross)
    gated_x = exchange(gated, "ch", cross)
    mirrored, mirrored_cotangent_x, gated_x = together(mirror(gated), mirrored_cotangent_x, gated_x)
    mirrored = run(flip_kernel, place, (mirrored,), [block], gflop=12.0)[0]
    mirrored_x = exchange(mirrored, "ch", cross)
    gated_all = [gated, exchange(gated, "ch", 1), gated_x, exchange(gated_x, "ch", 1)]
    cotangent_all = [cotangent, exchange(cotangent, "ch", 1), cotangent_x, exchange(cotangent_x, "ch", 1)]
    mirrored_cotangent_all = [
        mirrored_cotangent,
        exchange(mirrored_cotangent, "ch", 1),
        mirrored_cotangent_x,
        exchange(mirrored_cotangent_x, "ch", 1),
    ]
    grad_norm = run(
        functools.partial(norm_grad_kernel, channels),
        place,
        (
            *cotangent_all,
            *mirrored_cotangent_all,
            w_out,
            exchange(w_out, "ch", 1),
            w_x_mine,
            w_x_other,
            exchange(w_x_mine, "ch", 1),
            exchange(w_x_other, "ch", 1),
        ),
        [((2 * rows, full), BF16)],
        [pltpu.VMEM((full, width), BF16)] * 2,
        gflop=2.1,
    )[0]
    mirrored_x, grad_norm = together(mirrored_x, grad_norm)
    mirrored_all = [mirrored, exchange(mirrored, "ch", 1), mirrored_x, exchange(mirrored_x, "ch", 1)]

    normalized, upstream, grad_gate_pre, first, second = run(
        functools.partial(combine_kernel, channels),
        place,
        (*gated_all, *mirrored_all, grad_norm, choose, gain.reshape(1, full), gate_pre, level_3),
        [((2 * rows, full), BF16), block, block, ((EDGE, width), BF16), ((EDGE, width), BF16)],
        [pltpu.VMEM((1, full), F32), pltpu.VMEM((rows, width), F32)],
        gflop=2.5,
    )
    first, second = swap_edges(first, second)
    out_sent, out_kept, gate_sent, gate_kept = run(
        functools.partial(products_kernel, channels),
        place,
        (normalized, cotangent, mirrored_cotangent, grad_gate_pre, *mains),
        [
            ((full // 4, width), BF16),
            ((full // 4, width), F32),
            ((full // 2, width), BF16),
            ((full // 2, width), F32),
        ],
        [pltpu.VMEM((full // 2, width), F32), pltpu.VMEM((full, width), F32)],
        gflop=0.8,
    )
    out_sent, gate_sent, first, second = together(out_sent, gate_sent, first, second)
    out_other = exchange(out_sent, "seq", steps[0])
    gate_other = exchange(gate_sent, "seq", steps[1])
    half = full // 2 + SPARE
    in_sent, in_kept = run(
        functools.partial(backward_kernel, channels),
        place,
        (upstream, first, second, conv_w, *mains, levels),
        [((half, width), BF16), ((half, width), F32)],
        [pltpu.VMEM((2 * half, width), F32)]
        + [pltpu.VMEM((BACK_FORE[k] + rows + BACK_AFT[k], width), F32) for k in (3, 2, 1)]
        + [pltpu.VMEM(levels.shape, F32)],
        gflop=0.5,
    )
    output = run(
        functools.partial(output_kernel, channels),
        place,
        (normalized, w_out, local_input),
        [block],
        gflop=0.3,
    )[0]

    down = [("halve", distance) for distance in steps]
    up = [("double", distance) for distance in steps[::-1]]
    out_down, out_up = down[:1] + down[2:], up[:-2] + up[-1:] + up[-2:-1]
    gate_down, gate_up = down[1:] + down[:1], up[-1:] + up[:-1]
    routes = [down + up + [("take",)], gate_down + gate_up + [None], out_down + out_up + [None]]
    results = []
    for route, sent, kept, other in zip(
        routes, (in_sent, None, None), (in_kept, gate_kept, out_kept), (None, gate_other, out_other)
    ):
        if other is None:
            other = exchange(sent, "seq", route[0][1])
        elif results:
            other = gate_other if len(results) == 1 else out_other
        for number, (done, upcoming) in enumerate(zip(route, route[1:])):
            prepared = advance(place, [(done, upcoming, kept, other)], conv_w.shape[:2])[0]
            if upcoming is not None and upcoming[0] != "take":
                sent, kept = prepared if len(prepared) == 2 else prepared * 2
                if not results and number == 0:
                    sent, gate_other = together(sent, gate_other)
                if not results and number == 1:
                    sent, out_other = together(sent, out_other)
                other = exchange(sent, "seq", upcoming[1])
        results.append(prepared)
    (grad_in, grad_conv), (sum_gate,), (sum_out,) = results
    return output, grad_in, sum_gate, sum_out, grad_conv


def solution(mesh):
    placed = (
        P("seq"),
        P("seq", "ch"),
        P(None, "ch"),
        P(None, "ch"),
        P(None, "ch"),
        P(None, None, "ch"),
        P(),
        P(),
        P(None, "ch"),
        P("seq", "ch"),
    )
    return jax.shard_map(
        local,
        mesh=mesh,
        in_specs=placed,
        out_specs=(
            P("seq", "ch"),
            P(None, "ch"),
            P(None, "ch"),
            P(None, "ch"),
            P(None, None, "ch"),
        ),
        check_vma=False,
    )
```
